128 devices in a mesh: gx: 16 (over y, x), gy: 8 (over z, core).
Axes of the slice: x: 4, y: 4, z: 4, core: 2. Of those that a mesh axis runs over, the one named last changes fastest.
Arguments:
- inputs: bfloat16 [8192, 6144], P('gy', 'gx'), may hold values from -24 to 24, as said below
- preact: bfloat16 [8192, 24576], P('gy', 'gx'), may hold values from -6 to 6
- upstream: bfloat16 [8192, 24576], P('gy', 'gx'), as said below
- weight: float32 [6144, 24576], P('gy', 'gx'), may hold values from -72 to 72, as said below
- row_factor: float32 [6144], P('gy'), may hold values from 0.2 to 20, as said below
- column_factor: float32 [24576], P('gx'), may hold values from 0.5 to 5
Outputs:
- update: float32 [6144, 24576], P('gy', 'gx')
- new_row_factor: float32 [6144], P('gy')
- new_column_factor: float32 [24576], P('gx')
The draws below stay inside these ranges and needn't reach their ends.
Inputs may be any that keep to these rules, and one draw needn't show every extreme that they name: `inputs`: entries lie within 24 in magnitude. `upstream`: entries lie within 36 / sqrt(8192) in magnitude. `weight`: entries lie within 72 in magnitude. `row_factor`: positive entries.
All inputs are finite; a program needn't handle non-finite values.
Results may differ from the reference program's by a relative error of at most 0.015.
Values may be sent and summed in bfloat16 or wider, within the bound.
No kernel may reach another device: no remote copies, remote signals or barrier semaphores. Data moves between devices by JAX's collectives and lax.ppermute only.
A program may use at most 192 MiB of HBM per device.

```python
import math
import jax
import jax.numpy as jnp
from jax import lax

D = 6144
FF = 24576
TOK_DEV = 1024
TOKENS = 8192
N_GY = 8


def log_uniform(key, count, lower, upper):
    return jnp.exp(jax.random.uniform(key, (count,), jnp.float32, math.log(lower), math.log(upper)))


def rising(count):
    return jnp.exp(math.log(3.0) * jnp.arange(count, dtype=jnp.float32) / count)


def growing(count, factor):
    return jnp.exp(math.log(factor) * jnp.arange(count, dtype=jnp.float32) / count)


def column_blocks(count):
    return jnp.arange(count, dtype=jnp.int32) * 16 // count


def token_signal(key):
    return jax.random.truncated_normal(jax.random.fold_in(key, 101), -2.0, 2.0, (TOKENS, 1), jnp.float32)


def draw_inputs(key, part):
    signal = token_signal(key)
    key = jax.random.fold_in(key, 11)
    first, second, third = jax.random.split(key, 3)
    scales = rising(D) * log_uniform(second, D, 0.5, 2.0)
    loading = jax.random.bernoulli(third, 0.5, (D,)).astype(jnp.float32)
    loading = loading * log_uniform(jax.random.fold_in(third, 1), D, 0.5, 1.0)
    spread_values = jax.random.truncated_normal(first, -3.5, 3.5, (TOKENS, D), jnp.float32)
    values = 0.8 * spread_values + 0.6 * signal * loading[None, :]
    return (values * scales[None, :]).astype(jnp.bfloat16)


def draw_upstream(key, part):
    signal = token_signal(key)
    key = jax.random.fold_in(key, 12)
    first, second, third = jax.random.split(key, 3)
    scales = rising(FF) * log_uniform(second, FF, 0.3, 3.0) / math.sqrt(TOKENS)
    chosen = jax.random.permutation(third, 16)[column_blocks(FF)] < 8
    loading = chosen.astype(jnp.float32) * log_uniform(jax.random.fold_in(third, 1), FF, 0.5, 1.0)
    spread_values = jax.random.truncated_normal(first, -4.0, 4.0, (TOKENS, FF), jnp.float32)
    values = 0.7 * spread_values + 0.5 * signal * loading[None, :]
    return (values * scales[None, :]).astype(jnp.bfloat16)


def draw_weight(key, part):
    key = jax.random.fold_in(key, 13)
    first, second, third, fourth = jax.random.split(key, 4)
    row_scales = rising(D) * log_uniform(second, D, 0.5, 2.0)
    levels = jnp.exp(jax.random.uniform(fourth, (16,), jnp.float32, -1.5, 0.0))
    column_scales = rising(FF) * log_uniform(third, FF, 0.5, 2.0) * levels[column_blocks(FF)]
    values = jax.random.truncated_normal(first, -4.0, 4.0, (D, FF), jnp.float32)
    return 0.5 * values * row_scales[:, None] * column_scales[None, :]


def draw_row_factor(key, part):
    key = jax.random.fold_in(key, 14)
    return 0.25 * growing(D, 4.0) * log_uniform(key, D, 0.8, 1.25)


def level_of(own_key, shape, cuts, low, top_value):
    factor_of = 1.0
    for axis_at, parts in cuts:
        heights = jax.random.uniform(jax.random.fold_in(jax.random.fold_in(own_key, 6), axis_at), (parts,), jnp.float32, low / len(cuts), top_value / len(cuts))
        factor_of = factor_of * jnp.repeat(jnp.exp(heights), shape[axis_at] // parts).reshape((-1,) + (1,) * (len(shape) - 1 - axis_at))
    return factor_of


def noise(rng, extent, width, reach, cuts=(), kind=jnp.bfloat16):
    array = width * jax.random.normal(rng, extent, jnp.float32)
    if cuts:
        array = array * level_of(rng, extent, cuts, -0.22, 0.18)
    return jnp.clip(array, -reach, reach).astype(kind)


def setup_inputs(seed: int = 0) -> dict:
    streams_of = jax.random.split(jax.random.key(seed), 7)
    inputs = draw_inputs(jax.random.fold_in(streams_of[6], 71), 0)
    preact = noise(streams_of[1], (TOKENS, FF), 1.0, 6.0, ((0, 8), (1, 16)))
    upstream = draw_upstream(jax.random.fold_in(streams_of[6], 71), 0)
    weight = draw_weight(jax.random.fold_in(streams_of[6], 71), 0)
    row_factor = draw_row_factor(jax.random.fold_in(streams_of[6], 71), 0)
    column_factor = jnp.clip(jnp.exp(math.log(5.0) - 2.3025851 * jax.random.uniform(streams_of[5], (FF,), jnp.float32) ** level_of(streams_of[5], (FF,), ((0, 16),), -0.2, 0.2)), 0.5, 5.0)
    return {"inputs": inputs, "preact": preact, "upstream": upstream, "weight": weight, "row_factor": row_factor, "column_factor": column_factor}


second_decay = 0.8
clip_ratio = 1.0
unit_eps = 1e-06
factor_eps = 1e-30

def gelu_slope(preact, upstream):
    value = preact.astype(jnp.float32)
    normal_cdf = 0.5 * (1.0 + jax.scipy.special.erf(value * 0.7071067811865476))
    density = jnp.exp(-0.5 * value * value) * 0.3989422804014327
    return (upstream.astype(jnp.float32) * (normal_cdf + value * density)).astype(jnp.bfloat16)

def reference(inputs, preact, upstream, weight, row_factor, column_factor):
    slope = gelu_slope(preact, upstream)

    def add_group(total, index):
        start = index * TOK_DEV
        rows_in = lax.dynamic_slice_in_dim(inputs, start, TOK_DEV, 0)
        rows_slope = lax.dynamic_slice_in_dim(slope, start, TOK_DEV, 0)
        partial_sum = jnp.dot(rows_in.T, rows_slope, preferred_element_type=jnp.float32).astype(jnp.bfloat16)
        partial_sum = lax.optimization_barrier(partial_sum)
        return (total + partial_sum.astype(jnp.float32), None)
    grad, _ = lax.scan(add_group, jnp.zeros((D, FF), jnp.float32), jnp.arange(N_GY, dtype=jnp.int32))
    grad_norm = jnp.sqrt(lax.optimization_barrier(jnp.sum(grad * grad, axis=0)))
    weight_norm = jnp.sqrt(lax.optimization_barrier(jnp.sum(weight * weight, axis=0)))
    clip_factor = jnp.minimum(1.0, clip_ratio * weight_norm / (grad_norm + unit_eps))
    clipped = grad * clip_factor[None, :]
    squared = clipped * clipped
    new_row = second_decay * row_factor + (1.0 - second_decay) * (lax.optimization_barrier(jnp.sum(squared, axis=1)) / FF + factor_eps)
    new_column = second_decay * column_factor + (1.0 - second_decay) * (lax.optimization_barrier(jnp.sum(squared, axis=0)) / D + factor_eps)
    row_mean = jnp.sum(new_row) / D
    weight_rms = jnp.sqrt(jnp.sum(weight * weight) / (D * FF))
    update = -weight_rms * clipped / jnp.sqrt(new_row[:, None] * new_column[None, :] / row_mean)
    return (update, new_row, new_column)
```

```python
import jax
import jax.numpy as jnp
from jax import lax
from jax.experimental import pallas as pl
from jax.experimental.pallas import tpu as pltpu
from jax.sharding import PartitionSpec as P

D = 6144
FF = 24576
TOK = 1024
FEAT = 384
HALF = 768
NCH = 2

second_decay = 0.8
clip_ratio = 1.0
unit_eps = 1e-06
factor_eps = 1e-30

BOTH = ("gx", "gy")
FLIP = (0, 2, 1, 3)


def moves(dx, dy, dz, other_core):
    pairs = []
    for y in range(4):
        for x in range(4):
            for z in range(4):
                for core in range(2):
                    s = 1 - 2 * core
                    tx, ty, tz = (x + s * dx) % 4, (y + s * dy) % 4, (z + s * dz) % 4
                    tc = 1 - core if other_core else core
                    pairs.append(((y * 4 + x) * 8 + z * 2 + core, (ty * 4 + tx) * 8 + tz * 2 + tc))
    return pairs


ALONG_X = moves(1, 0, 0, False)
ALONG_Y = moves(0, 1, 0, False)
ALONG_Z = moves(0, 0, 1, False)
SWAP = moves(0, 0, 0, True)


def send(value, pairs):
    return lax.ppermute(value, BOTH, pairs)


def gelu_slope(preact, upstream):
    value = preact.astype(jnp.float32)
    normal_cdf = 0.5 * (1.0 + jax.scipy.special.erf(value * 0.7071067811865476))
    density = jnp.exp(-0.5 * value * value) * 0.3989422804014327
    return (upstream.astype(jnp.float32) * (normal_cdf + value * density)).astype(jnp.bfloat16)


def gather_ring(own, other, pairs):
    behind_own = send(own, pairs)
    behind_other = send(other, pairs)
    opposite_own = send(behind_own, pairs)
    ahead_other = send(behind_own, SWAP)
    ahead_own = send(behind_other, SWAP)
    opposite_other = send(opposite_own, SWAP)
    return (behind_own, behind_other), (ahead_own, ahead_other), (opposite_own, opposite_other)


def unit_partials(order, slope_own, slope_other, entries):
    arrays = []
    position = {}
    plan = []
    rows = 0
    for places in entries:
        count = places[0][0][0].shape[-2]
        for i, halves in enumerate(places):
            for h, (array, index) in enumerate(halves):
                if id(array) not in position:
                    position[id(array)] = len(arrays)
                    arrays.append(array)
                plan.append((i, h, rows, count, position[id(array)], index))
        rows += count

    def kernel(order_ref, own_ref, other_ref, *refs):
        feature_refs = refs[: len(arrays)]
        out_last, out_1, out_2, out_3, held, sems = refs[len(arrays) :]
        for i, h, start, count, which, index in plan:
            source = feature_refs[which]
            source = source.at[index] if index is not None else source
            pltpu.make_async_copy(
                source, held.at[i, h, pl.ds(start, count)], sems.at[i]
            ).start()

        @pl.loop(0, 4)
        def _(i):
            pltpu.make_async_copy(held.at[i], held.at[i], sems.at[i]).wait()
            total = jnp.dot(held[i, 0], own_ref[...], preferred_element_type=jnp.float32)
            total += jnp.dot(held[i, 1], other_ref[...], preferred_element_type=jnp.float32)
            place = order_ref[i]

            @pl.when(place == 0)
            def _():
                out_last[...] = total

            for k, out in ((1, out_1), (2, out_2), (3, out_3)):

                @pl.when(place == k)
                def _():
                    out[...] = total.astype(jnp.bfloat16)

    narrow = jax.ShapeDtypeStruct((rows, HALF), jnp.bfloat16)
    vmem = pl.BlockSpec(memory_space=pltpu.VMEM)
    return pl.pallas_call(
        kernel,
        out_shape=(jax.ShapeDtypeStruct((rows, HALF), jnp.float32), narrow, narrow, narrow),
        in_specs=[pl.BlockSpec(memory_space=pltpu.SMEM), vmem, vmem]
        + [pl.BlockSpec(memory_space=pl.ANY)] * len(arrays),
        out_specs=(vmem,) * 4,
        scratch_shapes=[
            pltpu.VMEM((4, 2, rows, TOK), jnp.bfloat16),
            pltpu.SemaphoreType.DMA((4,)),
        ],
        compiler_params=pltpu.CompilerParams(vmem_limit_bytes=40 << 20),
        cost_estimate=pl.CostEstimate(
            flops=2 * 4 * rows * HALF * 2 * TOK,
            bytes_accessed=4 * rows * 2 * TOK * 2 + 2 * TOK * HALF * 2 + 10 * rows * HALF,
            transcendentals=0,
        ),
    )(order, slope_own, slope_other, *arrays)


def reduce_ring(order, slope_own, slope_other, entries):
    last, first, second, third = unit_partials(order, slope_own, slope_other, entries)
    got = send(first, ALONG_Z)
    got = send((second.astype(jnp.float32) + got.astype(jnp.float32)).astype(jnp.bfloat16), ALONG_Z)
    got = send((third.astype(jnp.float32) + got.astype(jnp.float32)).astype(jnp.bfloat16), ALONG_Z)
    return last + got.astype(jnp.float32)


def everyone(vector, axis, count):
    return lax.all_to_all(
        jnp.broadcast_to(vector[None, :], (count,) + vector.shape), axis, 0, 0, tiled=True
    )


def per_device(inputs, preact, upstream, weight, row_factor, column_factor):
    gx, gy = lax.axis_index("gx"), lax.axis_index("gy")
    y, x, z, core = gx // 4, gx % 4, gy // 2, gy % 2
    s = 1 - 2 * core
    steps = jnp.array([0, -1, 1, 2], jnp.int32)
    order = (s * (z - y) - steps) % 4

    features = inputs.T
    both = (features, send(features, SWAP))
    size = FEAT // 2 // NCH
    p_here = tuple(v[: FEAT // 2] for v in both)
    q_here = tuple(v[FEAT // 2 :] for v in both)

    def part(value, start):
        return lax.dynamic_slice_in_dim(value, start * HALF, HALF, 1)

    slope_mine = gelu_slope(part(preact, core), part(upstream, core))
    slope_yours = gelu_slope(part(preact, 1 - core), part(upstream, 1 - core))
    slope_other = send(slope_yours, SWAP)
    ring = lambda entries: reduce_ring(order, slope_mine, slope_other, entries)

    p_behind, p_ahead, p_opposite = gather_ring(*p_here, ALONG_Y)
    q_behind, q_ahead, q_opposite = gather_ring(*q_here, ALONG_X)
    p_all = [p_here, p_behind, p_ahead, p_opposite]
    q_all = [q_here, q_behind, q_ahead, q_opposite]

    pieces = []
    own_p = ring([[tuple((v[h], None) for h in range(2)) for v in p_all]])
    pieces.append([(0, 0, FEAT // 2, own_p)])
    for chunk in range(NCH):
        lo = chunk * size
        p_own, p_other = (jnp.stack([v[h][lo : lo + size] for v in p_all]) for h in range(2))
        q_own, q_other = (jnp.stack([v[h][lo : lo + size] for v in q_all]) for h in range(2))
        behind, ahead, opposite = gather_ring(p_own, p_other, ALONG_X)
        near = ring(
            [
                [((behind[0], i), (behind[1], i)) for i in range(4)],
                [((ahead[0], FLIP[i]), (ahead[1], FLIP[i])) for i in range(4)],
            ]
        )
        pieces.append([(1, lo, size, near[:size]), (2, lo, size, near[size:])])
        q_b, q_a, q_o = gather_ring(q_own, q_other, ALONG_Y)
        entries = [[((opposite[0], i), (opposite[1], FLIP[i])) for i in range(4)]]
        for g in range(4):
            entries.append(
                [
                    ((q_own, g), (q_other, g)),
                    ((q_b[0], g), (q_b[1], g)),
                    ((q_a[0], FLIP[g]), (q_a[1], FLIP[g])),
                    ((q_o[0], g), (q_o[1], FLIP[g])),
                ]
            )
        far = ring(entries)
        group = [(3, lo, size, far[:size])]
        for g in range(4):
            group.append((g, FEAT // 2 + lo, size, far[(g + 1) * size : (g + 2) * size]))
        pieces.append(group)

    places = {}
    for group in pieces:
        for g, start, _, value in group:
            places[(g, start)] = value
    grad_rel = jnp.stack(
        [jnp.concatenate([places[k] for k in sorted(places) if k[0] == g]) for g in range(4)]
    )

    weight_sq = weight * weight
    weight_local = jnp.sum(weight_sq, axis=0)
    grad_local = jnp.sum(grad_rel * grad_rel, axis=(0, 1))
    where = jnp.array([0, 2, 3, 1], jnp.int32)

    def rows_of(owner):
        out = []
        for i in range(2):
            at = where[(s * (2 * owner + i - x)) % 4]
            out.append(lax.dynamic_index_in_dim(grad_rel, at, 0, keepdims=False))
        return jnp.concatenate(out)

    kept = rows_of(core)
    got = send(rows_of(1 - core), SWAP)
    row_local = jnp.broadcast_to(jnp.sum(row_factor)[None], (128,))
    gathered = everyone(jnp.concatenate([grad_local, weight_local, row_local]), "gy", 8)
    grad_sq = jnp.sum(gathered[:, :HALF].reshape(4, 2 * HALF), axis=0)
    weight_col_sq = jnp.sum(gathered[:, HALF : 3 * HALF], axis=0)
    row_total = jnp.sum(gathered[:, 3 * HALF])

    clip_factor = jnp.minimum(
        1.0, clip_ratio * jnp.sqrt(weight_col_sq) / (jnp.sqrt(grad_sq) + unit_eps)
    )
    column_sums = clip_factor * clip_factor * grad_sq
    new_column = second_decay * column_factor + (1.0 - second_decay) * (
        column_sums / D + factor_eps
    )
    grad = jnp.concatenate(
        [jnp.where(core == 0, kept, got), jnp.where(core == 0, got, kept)], axis=1
    )
    clipped = grad * clip_factor[None, :]
    row_part = jnp.sum(clipped * clipped, axis=1)
    totals = jnp.concatenate(
        [
            jnp.broadcast_to(jnp.sum(column_sums)[None], (128,)),
            jnp.broadcast_to(jnp.sum(weight_col_sq)[None], (128,)),
        ]
    )
    summed = jnp.sum(everyone(jnp.concatenate([row_part, totals]), "gx", 16), axis=0)
    row_sums, clipped_total, weight_total = summed[:768], summed[768], summed[896]
    new_row = second_decay * row_factor + (1.0 - second_decay) * (row_sums / FF + factor_eps)
    row_mean = (
        second_decay * row_total + (1.0 - second_decay) * (clipped_total / FF + D * factor_eps)
    ) / D
    weight_rms = jnp.sqrt(weight_total / (D * FF))
    update = (
        -weight_rms
        * clipped
        * lax.rsqrt(new_row)[:, None]
        * (jnp.sqrt(row_mean) * lax.rsqrt(new_column))[None, :]
    )
    return (update, new_row, new_column)


def solution(mesh):
    in_specs = (P("gy", "gx"), P("gy", "gx"), P("gy", "gx"), P("gy", "gx"), P("gy"), P("gx"))
    out_specs = (P("gy", "gx"), P("gy"), P("gx"))
    return jax.shard_map(
        per_device, mesh=mesh, in_specs=in_specs, out_specs=out_specs, check_vma=False
    )
```

```python
import jax
import jax.numpy as jnp
from jax import lax
from jax.experimental import pallas as pl
from jax.experimental.pallas import tpu as pltpu
from jax.sharding import PartitionSpec as P

D = 6144
FF = 24576
TOK = 1024
FEAT = 384
HALF = 768
NCH = 2

second_decay = 0.8
clip_ratio = 1.0
unit_eps = 1e-06
factor_eps = 1e-30

BOTH = ("gx", "gy")
FLIP = (0, 2, 1, 3)


def moves(dx, dy, dz, other_core):
    pairs = []
    for y in range(4):
        for x in range(4):
            for z in range(4):
                for core in range(2):
                    s = 1 - 2 * core
                    tx, ty, tz = (x + s * dx) % 4, (y + s * dy) % 4, (z + s * dz) % 4
                    tc = 1 - core if other_core else core
                    pairs.append(((y * 4 + x) * 8 + z * 2 + core, (ty * 4 + tx) * 8 + tz * 2 + tc))
    return pairs


ALONG_X = moves(1, 0, 0, False)
ALONG_Y = moves(0, 1, 0, False)
ALONG_Z = moves(0, 0, 1, False)
ALONG_Z2 = moves(0, 0, 2, False)
ALONG_Z3 = moves(0, 0, 3, False)
SWAP = moves(0, 0, 0, True)


def send(value, pairs):
    return lax.ppermute(value, BOTH, pairs)


def gelu_slope(preact, upstream):
    value = preact.astype(jnp.float32)
    normal_cdf = 0.5 * (1.0 + jax.scipy.special.erf(value * 0.7071067811865476))
    density = jnp.exp(-0.5 * value * value) * 0.3989422804014327
    return (upstream.astype(jnp.float32) * (normal_cdf + value * density)).astype(jnp.bfloat16)


def gather_ring(own, other, pairs):
    behind_own = send(own, pairs)
    behind_other = send(other, pairs)
    opposite_own = send(behind_own, pairs)
    ahead_other = send(behind_own, SWAP)
    ahead_own = send(behind_other, SWAP)
    opposite_other = send(opposite_own, SWAP)
    return (behind_own, behind_other), (ahead_own, ahead_other), (opposite_own, opposite_other)


def unit_partials(order, slope_own, slope_other, entries, low, high, waits=()):
    arrays = []
    position = {}
    plan = []
    rows = 0
    for places in entries:
        count = places[0][0][0].shape[-2]
        for i, halves in enumerate(places):
            for h, (array, index) in enumerate(halves):
                if id(array) not in position:
                    position[id(array)] = len(arrays)
                    arrays.append(array)
                plan.append((i, h, rows, count, position[id(array)], index))
        rows += count
    many = high - low

    def kernel(order_ref, own_ref, other_ref, *refs):
        feature_refs = refs[: len(arrays)]
        outs = refs[len(arrays) + len(waits) : len(arrays) + len(waits) + many]
        held, slopes, feature_sem, slope_sem = refs[len(arrays) + len(waits) + many :]
        pltpu.make_async_copy(own_ref, slopes.at[pl.ds(0, TOK)], slope_sem).start()
        pltpu.make_async_copy(other_ref, slopes.at[pl.ds(TOK, TOK)], slope_sem).start()
        for i in range(4):
            place = order_ref[i]

            @pl.when((place >= low) & (place < high))
            def _():
                base = pl.multiple_of((place - low) * rows, rows)
                for at, h, start, count, which, index in plan:
                    if at == i:
                        source = feature_refs[which]
                        source = source.at[index] if index is not None else source
                        pltpu.make_async_copy(
                            source,
                            held.at[pl.ds(base + start, count), pl.ds(h * TOK, TOK)],
                            feature_sem,
                        ).start()

        pltpu.make_async_copy(slopes, slopes, slope_sem).wait()
        pltpu.make_async_copy(held, held, feature_sem).wait()

        @pl.loop(0, HALF // 256)
        def _(j):
            columns = pl.ds(pl.multiple_of(j * 256, 256), 256)
            total = jnp.dot(held[...], slopes[:, columns], preferred_element_type=jnp.float32)
            for k, out in enumerate(outs):
                out[:, columns] = total[k * rows : (k + 1) * rows].astype(out.dtype)

    vmem = pl.BlockSpec(memory_space=pltpu.VMEM)
    anywhere = pl.BlockSpec(memory_space=pl.ANY)
    return pl.pallas_call(
        kernel,
        out_shape=tuple(
            jax.ShapeDtypeStruct((rows, HALF), jnp.float32 if k == 3 else jnp.bfloat16)
            for k in range(low, high)
        ),
        in_specs=[pl.BlockSpec(memory_space=pltpu.SMEM)]
        + [anywhere] * (2 + len(arrays) + len(waits)),
        out_specs=(vmem,) * many,
        scratch_shapes=[
            pltpu.VMEM((many * rows, 2 * TOK), jnp.bfloat16),
            pltpu.VMEM((2 * TOK, HALF), jnp.bfloat16),
            pltpu.SemaphoreType.DMA,
            pltpu.SemaphoreType.DMA,
        ],
        compiler_params=pltpu.CompilerParams(vmem_limit_bytes=44 << 20),
        cost_estimate=pl.CostEstimate(
            flops=4 * many * rows * HALF * 2 * TOK,
            bytes_accessed=many * rows * 2 * TOK * 2 + 2 * TOK * HALF * 2 + 10 * rows * HALF,
            transcendentals=0,
        ),
    )(order, slope_own, slope_other, *arrays, *waits)


def add_narrow(a, b):
    return (a.astype(jnp.float32) + b.astype(jnp.float32)).astype(jnp.bfloat16)


def reduce_ring(order, slope_own, slope_other, entries, waits=(), split=False):
    part = lambda low, high: unit_partials(order, slope_own, slope_other, entries, low, high, waits)
    if split:
        first, second = part(0, 2)
        third, last = part(2, 4)
    else:
        first, second, third, last = part(0, 4)
    got = send(first, ALONG_Z)
    got = send(add_narrow(second, got), ALONG_Z)
    got = send(add_narrow(third, got), ALONG_Z)
    return last + got.astype(jnp.float32)


def after(value, *before):
    return lax.optimization_barrier((value,) + before)[0]


def everyone(vector, axis, count):
    return lax.all_to_all(
        jnp.broadcast_to(vector[None, :], (count,) + vector.shape), axis, 0, 0, tiled=True
    )


def per_device(inputs, preact, upstream, weight, row_factor, column_factor):
    gx, gy = lax.axis_index("gx"), lax.axis_index("gy")
    y, x, z, core = gx // 4, gx % 4, gy // 2, gy % 2
    s = 1 - 2 * core
    steps = jnp.array([0, -1, 1, 2], jnp.int32)
    order = (s * (z - y) - steps + 3) % 4

    mine = inputs.T
    p_mine, q_mine = lax.optimization_barrier((mine[: FEAT // 2], mine[FEAT // 2 :]))
    p_here = (p_mine, send(p_mine, SWAP))
    q_here = (q_mine, send(q_mine, SWAP))
    size = FEAT // 2 // NCH
    preact, upstream, weight = lax.optimization_barrier((preact, upstream, weight, *p_here, *q_here))[:3]

    def part(value, start):
        return lax.dynamic_slice_in_dim(value, start * HALF, HALF, 1)

    slope_yours = gelu_slope(part(preact, 1 - core), part(upstream, 1 - core))
    slope_other = send(slope_yours, SWAP)
    slope_mine = gelu_slope(part(preact, core), part(upstream, core))
    ring = lambda entries, **kw: reduce_ring(order, slope_mine, slope_other, entries, **kw)

    weight_local = jnp.sum(weight * weight, axis=0)
    row_local = jnp.broadcast_to(jnp.sum(row_factor)[None], (128,))
    weight_mine = lax.dynamic_slice_in_dim(weight_local, core * HALF, HALF)
    weight_yours = lax.dynamic_slice_in_dim(weight_local, (1 - core) * HALF, HALF)
    early = jnp.concatenate([weight_mine, row_local]) + send(
        jnp.concatenate([weight_yours, row_local]), SWAP
    )

    p_behind, p_ahead, p_opposite = gather_ring(*p_here, ALONG_Y)
    q_behind, q_ahead, q_opposite = gather_ring(*q_here, ALONG_X)
    p_all = [p_here, p_behind, p_ahead, p_opposite]
    q_all = [q_here, q_behind, q_ahead, q_opposite]

    pieces = []
    own_p = ring([[tuple((v[h], None) for h in range(2)) for v in p_all]], waits=(early,))
    pieces.append([(0, 0, FEAT // 2, own_p)])
    behind = opposite = q_b = q_o = None
    for chunk in range(NCH):
        lo = chunk * size
        p_own, p_other = (jnp.stack([v[h][lo : lo + size] for v in p_all]) for h in range(2))
        q_own, q_other = (jnp.stack([v[h][lo : lo + size] for v in q_all]) for h in range(2))
        if chunk:
            p_own, p_other = after(p_own, behind[1]), after(p_other, opposite[0])
            q_own, q_other = after(q_own, q_b[1]), after(q_other, q_o[0])
        behind, ahead, opposite = gather_ring(p_own, p_other, ALONG_X)
        near = ring(
            [
                [((behind[0], i), (behind[1], i)) for i in range(4)],
                [((ahead[0], FLIP[i]), (ahead[1], FLIP[i])) for i in range(4)],
            ]
        )
        pieces.append([(1, lo, size, near[:size]), (2, lo, size, near[size:])])
        q_b, q_a, q_o = gather_ring(q_own, q_other, ALONG_Y)
        entries = [[((opposite[0], i), (opposite[1], FLIP[i])) for i in range(4)]]
        for g in range(4):
            entries.append(
                [
                    ((q_own, g), (q_other, g)),
                    ((q_b[0], g), (q_b[1], g)),
                    ((q_a[0], FLIP[g]), (q_a[1], FLIP[g])),
                    ((q_o[0], g), (q_o[1], FLIP[g])),
                ]
            )
        far = ring(entries, split=True)
        group = [(3, lo, size, far[:size])]
        for g in range(4):
            group.append((g, FEAT // 2 + lo, size, far[(g + 1) * size : (g + 2) * size]))
        pieces.append(group)

    places = {}
    for group in pieces:
        for g, start, _, value in group:
            places[(g, start)] = value
    grad_rel = jnp.stack(
        [jnp.concatenate([places[k] for k in sorted(places) if k[0] == g]) for g in range(4)]
    )

    grad_local = jnp.sum(grad_rel * grad_rel, axis=(0, 1))
    where = jnp.array([0, 2, 3, 1], jnp.int32)

    def rows_of(owner):
        out = []
        for i in range(2):
            at = where[(s * (2 * owner + i - x)) % 4]
            out.append(lax.dynamic_index_in_dim(grad_rel, at, 0, keepdims=False))
        return jnp.concatenate(out)

    kept = rows_of(core)
    got = send(rows_of(1 - core), SWAP)
    column_stats = jnp.concatenate([grad_local, early])
    for pairs in (ALONG_Z, ALONG_Z2, ALONG_Z3):
        column_stats = column_stats + send(jnp.concatenate([grad_local, early]), pairs)
    mine_stats = column_stats[: 2 * HALF]
    yours_stats = send(mine_stats, SWAP)

    def all_columns(start):
        a, b = mine_stats[start : start + HALF], yours_stats[start : start + HALF]
        return jnp.concatenate([jnp.where(core == 0, a, b), jnp.where(core == 0, b, a)])

    grad_sq = all_columns(0)
    weight_col_sq = all_columns(HALF)
    row_total = column_stats[2 * HALF]

    clip_factor = jnp.minimum(
        1.0, clip_ratio * jnp.sqrt(weight_col_sq) / (jnp.sqrt(grad_sq) + unit_eps)
    )
    column_sums = clip_factor * clip_factor * grad_sq
    new_column = second_decay * column_factor + (1.0 - second_decay) * (
        column_sums / D + factor_eps
    )
    grad = jnp.concatenate(
        [jnp.where(core == 0, kept, got), jnp.where(core == 0, got, kept)], axis=1
    )
    clipped = grad * clip_factor[None, :]
    row_part = jnp.sum(clipped * clipped, axis=1)
    totals = jnp.concatenate(
        [
            jnp.broadcast_to(jnp.sum(column_sums)[None], (128,)),
            jnp.broadcast_to(jnp.sum(weight_col_sq)[None], (128,)),
        ]
    )
    summed = jnp.sum(everyone(jnp.concatenate([row_part, totals]), "gx", 16), axis=0)
    row_sums, clipped_total, weight_total = summed[:768], summed[768], summed[896]
    new_row = second_decay * row_factor + (1.0 - second_decay) * (row_sums / FF + factor_eps)
    row_mean = (
        second_decay * row_total + (1.0 - second_decay) * (clipped_total / FF + D * factor_eps)
    ) / D
    weight_rms = jnp.sqrt(weight_total / (D * FF))
    update = (
        -weight_rms
        * clipped
        * lax.rsqrt(new_row)[:, None]
        * (jnp.sqrt(row_mean) * lax.rsqrt(new_column))[None, :]
    )
    return (update, new_row, new_column)


def solution(mesh):
    in_specs = (P("gy", "gx"), P("gy", "gx"), P("gy", "gx"), P("gy", "gx"), P("gy"), P("gx"))
    out_specs = (P("gy", "gx"), P("gy"), P("gx"))
    return jax.shard_map(
        per_device, mesh=mesh, in_specs=in_specs, out_specs=out_specs, check_vma=False
    )
```

```python
import jax
import jax.numpy as jnp
from jax import lax
from jax.experimental import pallas as pl
from jax.experimental.pallas import tpu as pltpu
from jax.sharding import PartitionSpec as P

D = 6144
FF = 24576
TOK = 1024
FEAT = 384
HALF = 768
NCH = 2

second_decay = 0.8
clip_ratio = 1.0
unit_eps = 1e-06
factor_eps = 1e-30

BOTH = ("gx", "gy")
FLIP = (0, 2, 1, 3)


def moves(dx, dy, dz, other_core):
    pairs = []
    for y in range(4):
        for x in range(4):
            for z in range(4):
                for core in range(2):
                    s = 1 - 2 * core
                    tx, ty, tz = (x + s * dx) % 4, (y + s * dy) % 4, (z + s * dz) % 4
                    tc = 1 - core if other_core else core
                    pairs.append(((y * 4 + x) * 8 + z * 2 + core, (ty * 4 + tx) * 8 + tz * 2 + tc))
    return pairs


ALONG_X = moves(1, 0, 0, False)
ALONG_Y = moves(0, 1, 0, False)
ALONG_Z = moves(0, 0, 1, False)
ALONG_Z2 = moves(0, 0, 2, False)
ALONG_Z3 = moves(0, 0, 3, False)
SWAP = moves(0, 0, 0, True)


STEPS = (0, -1, 1, 2)
CHEAP = pl.CostEstimate(flops=1024, bytes_accessed=1024, transcendentals=0)


def coordinates():
    gx, gy = lax.axis_index("gx"), lax.axis_index("gy")
    return gx >> 2, gx & 3, gy >> 1, gy & 1


def send(value, pairs):
    return lax.ppermute(value, BOTH, pairs)


def slope_half(preact, upstream, other, waits=()):
    count = 4
    rows = TOK // count

    def kernel(pre_ref, up_ref, *refs):
        out, pre, up, sems = refs[len(waits) :]
        core = coordinates()[3]
        half = 1 - core if other else core
        columns = pl.ds(pl.multiple_of(half * HALF, HALF), HALF)
        for k in range(count):
            at = pl.ds(k * rows, rows)
            pltpu.make_async_copy(pre_ref.at[at, columns], pre.at[at], sems.at[0, k]).start()
            pltpu.make_async_copy(up_ref.at[at, columns], up.at[at], sems.at[1, k]).start()
        for k in range(count):
            at = pl.ds(k * rows, rows)
            pltpu.make_async_copy(pre.at[at], pre.at[at], sems.at[0, k]).wait()
            pltpu.make_async_copy(up.at[at], up.at[at], sems.at[1, k]).wait()

            @pl.loop(0, rows // 16)
            def _(j):
                tile = pl.ds(pl.multiple_of(k * rows + j * 16, 16), 16)
                value = pre[tile].astype(jnp.float32)
                normal_cdf = 0.5 * (1.0 + lax.erf(value * 0.7071067811865476))
                density = jnp.exp(-0.5 * value * value) * 0.3989422804014327
                slope = up[tile].astype(jnp.float32) * (normal_cdf + value * density)
                out[tile] = slope.astype(jnp.bfloat16)

    anywhere = pl.BlockSpec(memory_space=pl.ANY)
    half_block = pltpu.VMEM((TOK, HALF), jnp.bfloat16)
    return pl.pallas_call(
        kernel,
        out_shape=jax.ShapeDtypeStruct((TOK, HALF), jnp.bfloat16),
        in_specs=[anywhere] * (2 + len(waits)),
        out_specs=pl.BlockSpec(memory_space=pltpu.VMEM),
        scratch_shapes=[half_block, half_block, pltpu.SemaphoreType.DMA((2, count))],
        compiler_params=pltpu.CompilerParams(vmem_limit_bytes=24 << 20),
        cost_estimate=CHEAP,
    )(preact, upstream, *waits)


def unit_partials(slope_own, slope_other, entries, low, high, waits=()):
    arrays = []
    position = {}
    plan = []
    rows = 0
    for places in entries:
        count = places[0][0][0].shape[-2]
        for i, halves in enumerate(places):
            for h, (array, index) in enumerate(halves):
                if id(array) not in position:
                    position[id(array)] = len(arrays)
                    arrays.append(array)
                plan.append((i, h, rows, count, position[id(array)], index))
        rows += count
    many = high - low

    def kernel(own_ref, other_ref, *refs):
        feature_refs = refs[: len(arrays)]
        outs = refs[len(arrays) + len(waits) : len(arrays) + len(waits) + many]
        held, slopes, feature_sem, slope_sem = refs[len(arrays) + len(waits) + many :]
        pltpu.make_async_copy(own_ref, slopes.at[pl.ds(0, TOK)], slope_sem).start()
        pltpu.make_async_copy(other_ref, slopes.at[pl.ds(TOK, TOK)], slope_sem).start()
        y, _, z, core = coordinates()
        for i in range(4):
            place = ((1 - 2 * core) * (z - y) - STEPS[i] + 3) & 3

            @pl.when((place >= low) & (place < high))
            def _():
                base = pl.multiple_of((place - low) * rows, rows)
                for at, h, start, count, which, index in plan:
                    if at == i:
                        source = feature_refs[which]
                        source = source.at[index] if index is not None else source
                        pltpu.make_async_copy(
                            source,
                            held.at[pl.ds(base + start, count), pl.ds(h * TOK, TOK)],
                            feature_sem,
                        ).start()

        pltpu.make_async_copy(slopes, slopes, slope_sem).wait()
        pltpu.make_async_copy(held, held, feature_sem).wait()

        @pl.loop(0, HALF // 256)
        def _(j):
            columns = pl.ds(pl.multiple_of(j * 256, 256), 256)
            total = jnp.dot(held[...], slopes[:, columns], preferred_element_type=jnp.float32)
            for k, out in enumerate(outs):
                out[:, columns] = total[k * rows : (k + 1) * rows].astype(out.dtype)

    vmem = pl.BlockSpec(memory_space=pltpu.VMEM)
    anywhere = pl.BlockSpec(memory_space=pl.ANY)
    return pl.pallas_call(
        kernel,
        out_shape=tuple(
            jax.ShapeDtypeStruct((rows, HALF), jnp.float32 if k == 3 else jnp.bfloat16)
            for k in range(low, high)
        ),
        in_specs=[anywhere] * (2 + len(arrays) + len(waits)),
        out_specs=(vmem,) * many,
        scratch_shapes=[
            pltpu.VMEM((many * rows, 2 * TOK), jnp.bfloat16),
            pltpu.VMEM((2 * TOK, HALF), jnp.bfloat16),
            pltpu.SemaphoreType.DMA,
            pltpu.SemaphoreType.DMA,
        ],
        compiler_params=pltpu.CompilerParams(vmem_limit_bytes=44 << 20),
        cost_estimate=CHEAP,
    )(slope_own, slope_other, *arrays, *waits)


def add_narrow(a, b):
    return (a.astype(jnp.float32) + b.astype(jnp.float32)).astype(jnp.bfloat16)


def after(value, *before):
    return lax.optimization_barrier((value,) + before)[0]


def stack_places(values):
    size = values[0].shape[0] // NCH

    def kernel(*refs):
        sources, outs, sems = refs[:4], refs[4 : 4 + NCH], refs[4 + NCH]
        for k in range(NCH):
            for i, source in enumerate(sources):
                pltpu.make_async_copy(
                    source.at[pl.ds(k * size, size)], outs[k].at[i], sems.at[k]
                ).start()
        for k in range(NCH):
            pltpu.make_async_copy(outs[k], outs[k], sems.at[k]).wait()

    anywhere = pl.BlockSpec(memory_space=pl.ANY)
    return pl.pallas_call(
        kernel,
        out_shape=(jax.ShapeDtypeStruct((4, size, TOK), jnp.bfloat16),) * NCH,
        in_specs=[anywhere] * 4,
        out_specs=(anywhere,) * NCH,
        scratch_shapes=[pltpu.SemaphoreType.DMA((NCH,))],
        cost_estimate=CHEAP,
    )(*values)


def place_rows(last, got, pieces, before):
    rows = last.shape[0]

    def kernel(last_ref, got_ref, *refs):
        kept, sent, sums, value, sem = refs[len(before) :]
        total = last_ref[...] + got_ref[...].astype(jnp.float32)
        value[...] = total
        _, x, _, core = coordinates()
        for g, low, start, count in pieces:
            column = (x + (1 - 2 * core) * STEPS[g]) & 3
            row = pl.multiple_of((column & 1) * FEAT + low, 32)
            source = value.at[pl.ds(start, count)]

            @pl.when((column >> 1) == core)
            def _():
                pltpu.make_async_copy(source, kept.at[pl.ds(row, count)], sem).start()

            @pl.when((column >> 1) != core)
            def _():
                pltpu.make_async_copy(source, sent.at[pl.ds(row, count)], sem).start()

        squares = jnp.sum(total * total, axis=0, keepdims=True)
        sums[...] = squares + refs[2][...] if before else squares
        pltpu.make_async_copy(value, value, sem).wait()

    anywhere = pl.BlockSpec(memory_space=pl.ANY)
    vmem = pl.BlockSpec(memory_space=pltpu.VMEM)
    block = jax.ShapeDtypeStruct((HALF, HALF), jnp.float32)
    return pl.pallas_call(
        kernel,
        out_shape=(block, block, jax.ShapeDtypeStruct((1, HALF), jnp.float32)),
        in_specs=[vmem, vmem]
        + ([anywhere, anywhere, vmem] if before else []),
        out_specs=(anywhere, anywhere, vmem),
        scratch_shapes=[pltpu.VMEM((rows, HALF), jnp.float32), pltpu.SemaphoreType.DMA],
        input_output_aliases={2: 0, 3: 1} if before else {},
        compiler_params=pltpu.CompilerParams(vmem_limit_bytes=24 << 20),
        cost_estimate=CHEAP,
    )(last, got, *before)


def everyone(vector, axis, count):
    return lax.all_to_all(
        jnp.broadcast_to(vector[None, :], (count,) + vector.shape), axis, 0, 0, tiled=True
    )


def per_device(inputs, preact, upstream, weight, row_factor, column_factor):
    core = coordinates()[3]

    mine = inputs.T
    p, q = lax.optimization_barrier((mine[: FEAT // 2], mine[FEAT // 2 :]))
    size = FEAT // 2 // NCH

    p_swap, q_swap = send(p, SWAP), send(q, SWAP)
    ya, xa = send(p, ALONG_Y), send(q, ALONG_X)
    yb, xb = send(p_swap, ALONG_Y), send(q_swap, ALONG_X)

    slope_yours = slope_half(preact, upstream, True, (p_swap, q_swap))
    slope_other = send(slope_yours, SWAP)
    slope_mine = slope_half(preact, upstream, False, (p_swap, q_swap))
    ya, xa, yb, xb = lax.optimization_barrier((ya, xa, yb, xb, slope_other, slope_mine))[:4]
    y2, x2 = send(ya, ALONG_Y), send(xa, ALONG_X)
    weight = after(weight, slope_mine)
    weight_local = jnp.sum(weight * weight, axis=0)
    row_local = jnp.broadcast_to(jnp.sum(row_factor)[None], (128,))
    weight_mine = lax.dynamic_slice_in_dim(weight_local, core * HALF, HALF)
    weight_yours = lax.dynamic_slice_in_dim(weight_local, (1 - core) * HALF, HALF)

    ya_swap, yb_swap = send(ya, SWAP), send(yb, SWAP)
    xa_swap = send(after(xa, ya_swap, yb_swap), SWAP)
    xb_swap = send(after(xb, ya_swap, yb_swap), SWAP)
    early_swap = send(after(jnp.concatenate([weight_yours, row_local]), ya_swap, yb_swap), SWAP)
    early = jnp.concatenate([weight_mine, row_local]) + early_swap
    y2_swap = send(after(y2, xa_swap, xb_swap, early_swap), SWAP)
    x2_swap = send(after(x2, xa_swap, xb_swap, early_swap), SWAP)
    p_own = stack_places((p, ya, yb_swap, y2))
    q_own = stack_places((q, xa, xb_swap, x2))
    p_other = stack_places((p_swap, yb, ya_swap, y2_swap))
    q_other = stack_places((q_swap, xb, xa_swap, x2_swap))

    def units(entries, low=0, high=4, waits=()):
        return unit_partials(slope_mine, slope_other, entries, low, high, waits)

    def hop(value):
        return send(value, ALONG_Z)

    own_entries = [((p, None), (p_swap, None)), ((ya, None), (yb, None))]
    own_entries += [((yb_swap, None), (ya_swap, None)), ((y2, None), (y2_swap, None))]
    own = units([own_entries], waits=(early, p_other[0], q_other[0]))

    def gather(chunk, gate_a, gate_b, gate_2):
        xa, ya = send(after(p_own[chunk], *gate_a), ALONG_X), send(after(q_own[chunk], *gate_a), ALONG_Y)
        xb, yb = send(after(p_other[chunk], *gate_b), ALONG_X), send(after(q_other[chunk], *gate_b), ALONG_Y)
        x2, y2 = send(after(xa, *gate_2), ALONG_X), send(after(ya, *gate_2), ALONG_Y)
        return xa, ya, xb, yb, x2, y2

    def swap_near(xa, ya, xb, yb, *gate):
        xa, ya, xb, yb = lax.optimization_barrier((xa, ya, xb, yb, *gate))[:4]
        xa_swap, xb_swap = send(xa, SWAP), send(xb, SWAP)
        ya_swap = send(after(ya, xa_swap, xb_swap), SWAP)
        yb_swap = send(after(yb, xa_swap, xb_swap), SWAP)
        return xa_swap, ya_swap, xb_swap, yb_swap

    def swap_far(x2, y2, *gate):
        x2, y2 = lax.optimization_barrier((x2, y2, *gate))[:2]
        return send(x2, SWAP), send(y2, SWAP)

    def near_entries(xa, xb, xa_swap, xb_swap):
        return [
            [((xa, i), (xb, i)) for i in range(4)],
            [((xb_swap, FLIP[i]), (xa_swap, FLIP[i])) for i in range(4)],
        ]

    def far_entries(chunk, ya, yb, ya_swap, yb_swap, x2, x2_swap, y2, y2_swap):
        entries = [[((x2, i), (x2_swap, FLIP[i])) for i in range(4)]]
        for g in range(4):
            entries.append(
                [
                    ((q_own[chunk], g), (q_other[chunk], g)),
                    ((ya, g), (yb, g)),
                    ((yb_swap, FLIP[g]), (ya_swap, FLIP[g])),
                    ((y2, g), (y2_swap, FLIP[g])),
                ]
            )
        return entries

    xa, ya, xb, yb, x2, y2 = gather(0, (), (), (own[0],))
    own_got = hop(own[0])
    own_2 = add_narrow(own[1], own_got)
    xa_swap, ya_swap, xb_swap, yb_swap = swap_near(xa, ya, xb, yb, own_2)
    own_got = hop(own_2)
    near0 = units(near_entries(xa, xb, xa_swap, xb_swap))
    near0_got = hop(near0[0])
    own_3 = add_narrow(own[2], own_got)
    x2_swap, y2_swap = swap_far(x2, y2, near0[0], ya_swap, yb_swap)
    own_got = hop(own_3)
    far0_entries = far_entries(0, ya, yb, ya_swap, yb_swap, x2, x2_swap, y2, y2_swap)
    xa, ya, xb, yb, x2, y2 = gather(1, (ya_swap, yb_swap, near0[0]), (x2_swap, y2_swap), ())
    far0 = units(far0_entries, 0, 2, waits=(xa, ya, own_3))
    far0_got = hop(far0[0])

    near0_2 = add_narrow(near0[1], near0_got)
    near0_got = hop(near0_2)
    far0 += units(far0_entries, 2, 4, waits=(near0_2,))
    xa_swap, ya_swap, xb_swap, yb_swap = swap_near(xa, ya, xb, yb, far0[2])
    far0_2 = add_narrow(far0[1], far0_got)
    near1 = units(near_entries(xa, xb, xa_swap, xb_swap), waits=(far0_2,))
    far0_got = hop(far0_2)
    near1_got = hop(near1[0])
    near0_3 = add_narrow(near0[2], near0_got)
    x2_swap, y2_swap = swap_far(x2, y2, near1[0], ya_swap, yb_swap)
    near0_got = hop(near0_3)
    far1_entries = far_entries(1, ya, yb, ya_swap, yb_swap, x2, x2_swap, y2, y2_swap)
    far1 = units(far1_entries, 0, 2, waits=(near0_3,))
    far1_got = hop(far1[0])
    near1_2 = add_narrow(near1[1], near1_got)
    near1_got = hop(near1_2)
    far0_3 = add_narrow(far0[2], far0_got)
    far1 += units(far1_entries, 2, 4, waits=(near1_2, far0_3))
    far0_got = hop(far0_3)

    placed = place_rows(own[3], own_got, [(0, 0, 0, FEAT // 2)], ())
    near_pieces = lambda chunk: [(1, chunk * size, 0, size), (2, chunk * size, size, size)]
    far_pieces = lambda chunk: [(3, chunk * size, 0, size)] + [
        (g, FEAT // 2 + chunk * size, (g + 1) * size, size) for g in range(4)
    ]
    placed = place_rows(near0[3], near0_got, near_pieces(0), placed)
    far1_got = hop(after(add_narrow(far1[1], far1_got), placed[2]))
    near1_got = hop(add_narrow(near1[2], near1_got))
    placed = place_rows(far0[3], far0_got, far_pieces(0), placed)
    far1_got = hop(after(add_narrow(far1[2], far1_got), placed[2]))
    placed = place_rows(near1[3], near1_got, near_pieces(1), placed)
    placed = place_rows(far1[3], far1_got, far_pieces(1), placed)
    kept, sent, grad_local = placed
    got = send(sent, SWAP)
    grad_local = grad_local[0]
    column_stats = jnp.concatenate([grad_local, early])
    for pairs in (ALONG_Z, ALONG_Z2, ALONG_Z3):
        column_stats = column_stats + send(jnp.concatenate([grad_local, early]), pairs)
    mine_stats = column_stats[: 2 * HALF]
    yours_stats = send(mine_stats, SWAP)

    def all_columns(start):
        a, b = mine_stats[start : start + HALF], yours_stats[start : start + HALF]
        return jnp.concatenate([jnp.where(core == 0, a, b), jnp.where(core == 0, b, a)])

    grad_sq = all_columns(0)
    weight_col_sq = all_columns(HALF)
    row_total = column_stats[2 * HALF]

    clip_factor = jnp.minimum(
        1.0, clip_ratio * jnp.sqrt(weight_col_sq) / (jnp.sqrt(grad_sq) + unit_eps)
    )
    column_sums = clip_factor * clip_factor * grad_sq
    new_column = second_decay * column_factor + (1.0 - second_decay) * (
        column_sums / D + factor_eps
    )
    grad = jnp.concatenate(
        [jnp.where(core == 0, kept, got), jnp.where(core == 0, got, kept)], axis=1
    )
    clipped = grad * clip_factor[None, :]
    row_part = jnp.sum(clipped * clipped, axis=1)
    totals = jnp.concatenate(
        [
            jnp.broadcast_to(jnp.sum(column_sums)[None], (128,)),
            jnp.broadcast_to(jnp.sum(weight_col_sq)[None], (128,)),
        ]
    )
    summed = jnp.sum(everyone(jnp.concatenate([row_part, totals]), "gx", 16), axis=0)
    row_sums, clipped_total, weight_total = summed[:768], summed[768], summed[896]
    new_row = second_decay * row_factor + (1.0 - second_decay) * (row_sums / FF + factor_eps)
    row_mean = (
        second_decay * row_total + (1.0 - second_decay) * (clipped_total / FF + D * factor_eps)
    ) / D
    weight_rms = jnp.sqrt(weight_total / (D * FF))
    update = (
        -weight_rms
        * clipped
        * lax.rsqrt(new_row)[:, None]
        * (jnp.sqrt(row_mean) * lax.rsqrt(new_column))[None, :]
    )
    return (update, new_row, new_column)


def solution(mesh):
    in_specs = (P("gy", "gx"), P("gy", "gx"), P("gy", "gx"), P("gy", "gx"), P("gy"), P("gx"))
    out_specs = (P("gy", "gx"), P("gy"), P("gx"))
    return jax.shard_map(
        per_device, mesh=mesh, in_specs=in_specs, out_specs=out_specs, check_vma=False
    )
```

```python
import jax
import jax.numpy as jnp
from jax import lax
from jax.experimental import pallas as pl
from jax.experimental.pallas import tpu as pltpu
from jax.sharding import PartitionSpec as P

D = 6144
FF = 24576
TOK = 1024
FEAT = 384
HALF = 768
NCH = 2

second_decay = 0.8
clip_ratio = 1.0
unit_eps = 1e-06
factor_eps = 1e-30

BOTH = ("gx", "gy")
FLIP = (0, 2, 1, 3)


def moves(dx, dy, dz, other_core):
    pairs = []
    for y in range(4):
        for x in range(4):
            for z in range(4):
                for core in range(2):
                    s = 1 - 2 * core
                    tx, ty, tz = (x + s * dx) % 4, (y + s * dy) % 4, (z + s * dz) % 4
                    tc = 1 - core if other_core else core
                    pairs.append(((y * 4 + x) * 8 + z * 2 + core, (ty * 4 + tx) * 8 + tz * 2 + tc))
    return pairs


ALONG_X = moves(1, 0, 0, False)
ALONG_Y = moves(0, 1, 0, False)
ALONG_Z = moves(0, 0, 1, False)
ALONG_Z2 = moves(0, 0, 2, False)
ALONG_Z3 = moves(0, 0, 3, False)
SWAP = moves(0, 0, 0, True)


STEPS = (0, -1, 1, 2)
CHEAP = pl.CostEstimate(flops=1024, bytes_accessed=1024, transcendentals=0)


def coordinates():
    gx, gy = lax.axis_index("gx"), lax.axis_index("gy")
    return gx >> 2, gx & 3, gy >> 1, gy & 1


def send(value, pairs):
    return lax.ppermute(value, BOTH, pairs)


def slope_half(preact, upstream, other, waits=()):
    count = 4
    rows = TOK // count

    def kernel(pre_ref, up_ref, *refs):
        out, pre, up, sems = refs[len(waits) :]
        core = coordinates()[3]
        half = 1 - core if other else core
        columns = pl.ds(pl.multiple_of(half * HALF, HALF), HALF)
        for k in range(count):
            at = pl.ds(k * rows, rows)
            pltpu.make_async_copy(pre_ref.at[at, columns], pre.at[at], sems.at[0, k]).start()
            pltpu.make_async_copy(up_ref.at[at, columns], up.at[at], sems.at[1, k]).start()
        for k in range(count):
            at = pl.ds(k * rows, rows)
            pltpu.make_async_copy(pre.at[at], pre.at[at], sems.at[0, k]).wait()
            pltpu.make_async_copy(up.at[at], up.at[at], sems.at[1, k]).wait()

            @pl.loop(0, rows // 16)
            def _(j):
                tile = pl.ds(pl.multiple_of(k * rows + j * 16, 16), 16)
                value = pre[tile].astype(jnp.float32)
                normal_cdf = 0.5 * (1.0 + lax.erf(value * 0.7071067811865476))
                density = jnp.exp(-0.5 * value * value) * 0.3989422804014327
                slope = up[tile].astype(jnp.float32) * (normal_cdf + value * density)
                out[tile] = slope.astype(jnp.bfloat16)

    anywhere = pl.BlockSpec(memory_space=pl.ANY)
    half_block = pltpu.VMEM((TOK, HALF), jnp.bfloat16)
    return pl.pallas_call(
        kernel,
        out_shape=jax.ShapeDtypeStruct((TOK, HALF), jnp.bfloat16),
        in_specs=[anywhere] * (2 + len(waits)),
        out_specs=pl.BlockSpec(memory_space=pltpu.VMEM),
        scratch_shapes=[half_block, half_block, pltpu.SemaphoreType.DMA((2, count))],
        compiler_params=pltpu.CompilerParams(vmem_limit_bytes=24 << 20),
        cost_estimate=CHEAP,
    )(preact, upstream, *waits)


def unit_partials(slope_own, slope_other, entries, low, high, waits=()):
    arrays = []
    position = {}
    plan = []
    rows = 0
    for places in entries:
        count = places[0][0][0].shape[-2]
        for i, halves in enumerate(places):
            for h, (array, index) in enumerate(halves):
                if id(array) not in position:
                    position[id(array)] = len(arrays)
                    arrays.append(array)
                plan.append((i, h, rows, count, position[id(array)], index))
        rows += count
    many = high - low

    def kernel(own_ref, other_ref, *refs):
        feature_refs = refs[: len(arrays)]
        outs = refs[len(arrays) + len(waits) : len(arrays) + len(waits) + many]
        held, slopes, feature_sem, slope_sem = refs[len(arrays) + len(waits) + many :]
        pltpu.make_async_copy(own_ref, slopes.at[pl.ds(0, TOK)], slope_sem).start()
        pltpu.make_async_copy(other_ref, slopes.at[pl.ds(TOK, TOK)], slope_sem).start()
        y, _, z, core = coordinates()
        for i in range(4):
            place = ((1 - 2 * core) * (z - y) - STEPS[i] + 3) & 3

            @pl.when((place >= low) & (place < high))
            def _():
                base = pl.multiple_of((place - low) * rows, rows)
                for at, h, start, count, which, index in plan:
                    if at == i:
                        source = feature_refs[which]
                        source = source.at[index] if index is not None else source
                        pltpu.make_async_copy(
                            source,
                            held.at[pl.ds(base + start, count), pl.ds(h * TOK, TOK)],
                            feature_sem,
                        ).start()

        pltpu.make_async_copy(slopes, slopes, slope_sem).wait()
        pltpu.make_async_copy(held, held, feature_sem).wait()

        @pl.loop(0, HALF // 256)
        def _(j):
            columns = pl.ds(pl.multiple_of(j * 256, 256), 256)
            total = jnp.dot(held[...], slopes[:, columns], preferred_element_type=jnp.float32)
            for k, out in enumerate(outs):
                out[:, columns] = total[k * rows : (k + 1) * rows].astype(out.dtype)

    vmem = pl.BlockSpec(memory_space=pltpu.VMEM)
    anywhere = pl.BlockSpec(memory_space=pl.ANY)
    return pl.pallas_call(
        kernel,
        out_shape=tuple(
            jax.ShapeDtypeStruct((rows, HALF), jnp.float32 if k == 3 else jnp.bfloat16)
            for k in range(low, high)
        ),
        in_specs=[anywhere] * (2 + len(arrays) + len(waits)),
        out_specs=(vmem,) * many,
        scratch_shapes=[
            pltpu.VMEM((many * rows, 2 * TOK), jnp.bfloat16),
            pltpu.VMEM((2 * TOK, HALF), jnp.bfloat16),
            pltpu.SemaphoreType.DMA,
            pltpu.SemaphoreType.DMA,
        ],
        compiler_params=pltpu.CompilerParams(vmem_limit_bytes=44 << 20),
        cost_estimate=CHEAP,
    )(slope_own, slope_other, *arrays, *waits)


def add_narrow(a, b):
    return (a.astype(jnp.float32) + b.astype(jnp.float32)).astype(jnp.bfloat16)


def after(value, *before):
    return lax.optimization_barrier((value,) + before)[0]


def turn(inputs):
    def kernel(ref, first, second):
        turned = ref[...].T
        first[...] = turned[: FEAT // 2]
        second[...] = turned[FEAT // 2 :]

    vmem = pl.BlockSpec(memory_space=pltpu.VMEM)
    half = jax.ShapeDtypeStruct((FEAT // 2, TOK), jnp.bfloat16)
    return pl.pallas_call(
        kernel, out_shape=(half, half), in_specs=[vmem], out_specs=(vmem, vmem), cost_estimate=CHEAP
    )(inputs)


def join(*pairs):
    def kernel(*refs):
        for k, out in enumerate(refs[2 * len(pairs) :]):
            out[0], out[1] = refs[2 * k][...], refs[2 * k + 1][...]

    vmem = pl.BlockSpec(memory_space=pltpu.VMEM)
    return pl.pallas_call(
        kernel,
        out_shape=tuple(jax.ShapeDtypeStruct((2,) + a.shape, a.dtype) for a, _ in pairs),
        in_specs=[vmem] * (2 * len(pairs)),
        out_specs=(vmem,) * len(pairs),
        cost_estimate=CHEAP,
    )(*[value for pair in pairs for value in pair])


def stack_rows(sources, start, count):
    arrays = []
    which = []
    for array, index in sources:
        if not any(array is other for other in arrays):
            arrays.append(array)
        which.append(([array is other for other in arrays].index(True), index))

    def kernel(*refs):
        out = refs[-1]
        for k, (at, index) in enumerate(which):
            source = refs[at] if index is None else refs[at].at[index]
            out[k // 4, k % 4] = source[pl.ds(start, count)]

    vmem = pl.BlockSpec(memory_space=pltpu.VMEM)
    return pl.pallas_call(
        kernel,
        out_shape=jax.ShapeDtypeStruct((2, 4, count, TOK), jnp.bfloat16),
        in_specs=[vmem] * len(arrays),
        out_specs=vmem,
        compiler_params=pltpu.CompilerParams(vmem_limit_bytes=24 << 20),
        cost_estimate=CHEAP,
    )(*arrays)


def place_rows(last, got, pieces, before):
    rows = last.shape[0]

    def kernel(last_ref, got_ref, *refs):
        kept, sent, sums, value, sem = refs[len(before) :]
        total = last_ref[...] + got_ref[...].astype(jnp.float32)
        value[...] = total
        _, x, _, core = coordinates()
        for g, low, start, count in pieces:
            column = (x + (1 - 2 * core) * STEPS[g]) & 3
            row = pl.multiple_of((column & 1) * FEAT + low, 32)
            source = value.at[pl.ds(start, count)]

            @pl.when((column >> 1) == core)
            def _():
                pltpu.make_async_copy(source, kept.at[pl.ds(row, count)], sem).start()

            @pl.when((column >> 1) != core)
            def _():
                pltpu.make_async_copy(source, sent.at[pl.ds(row, count)], sem).start()

        squares = jnp.sum(total * total, axis=0, keepdims=True)
        sums[...] = squares + refs[2][...] if before else squares
        pltpu.make_async_copy(value, value, sem).wait()

    anywhere = pl.BlockSpec(memory_space=pl.ANY)
    vmem = pl.BlockSpec(memory_space=pltpu.VMEM)
    block = jax.ShapeDtypeStruct((HALF, HALF), jnp.float32)
    return pl.pallas_call(
        kernel,
        out_shape=(block, block, jax.ShapeDtypeStruct((1, HALF), jnp.float32)),
        in_specs=[vmem, vmem]
        + ([anywhere, anywhere, vmem] if before else []),
        out_specs=(anywhere, anywhere, vmem),
        scratch_shapes=[pltpu.VMEM((rows, HALF), jnp.float32), pltpu.SemaphoreType.DMA],
        input_output_aliases={2: 0, 3: 1} if before else {},
        compiler_params=pltpu.CompilerParams(vmem_limit_bytes=24 << 20),
        cost_estimate=CHEAP,
    )(last, got, *before)


def everyone(vector, axis, count):
    return lax.all_to_all(
        jnp.broadcast_to(vector[None, :], (count,) + vector.shape), axis, 0, 0, tiled=True
    )


def per_device(inputs, preact, upstream, weight, row_factor, column_factor):
    core = coordinates()[3]

    p, q = turn(inputs)
    size = FEAT // 2 // NCH

    p_both, q_both = join((p, send(p, SWAP)), (q, send(q, SWAP)))
    y1, x1 = send(p_both, ALONG_Y), send(q_both, ALONG_X)
    slope_yours = slope_half(preact, upstream, True, (p_both, q_both))
    slope_other = send(slope_yours, SWAP)
    slope_mine = slope_half(preact, upstream, False, (p_both, q_both))
    weight = after(weight, slope_mine)
    weight_local = jnp.sum(weight * weight, axis=0)
    row_local = jnp.broadcast_to(jnp.sum(row_factor)[None], (128,))
    weight_mine = lax.dynamic_slice_in_dim(weight_local, core * HALF, HALF)
    weight_yours = lax.dynamic_slice_in_dim(weight_local, (1 - core) * HALF, HALF)
    early = jnp.concatenate([weight_mine, row_local])
    early = early + send(jnp.concatenate([weight_yours, row_local]), SWAP)
    y1, x1 = lax.optimization_barrier((y1, x1, slope_yours, slope_mine, early))[:2]
    y2, x2 = send(y1[0], ALONG_Y), send(x1[0], ALONG_X)
    y1_swap, x1_swap = send(y1, SWAP), send(x1, SWAP)
    y2, x2 = lax.optimization_barrier((y2, x2, y1_swap, x1_swap))[:2]
    y2_swap, x2_swap = send(y2, SWAP), send(x2, SWAP)
    p_places = [(p_both, 0), (y1, 0), (y1_swap, 1), (y2, None)]
    p_places += [(p_both, 1), (y1, 1), (y1_swap, 0), (y2_swap, None)]
    q_places = [(q_both, 0), (x1, 0), (x1_swap, 1), (x2, None)]
    q_places += [(q_both, 1), (x1, 1), (x1_swap, 0), (x2_swap, None)]

    def units(entries, low=0, high=4, waits=()):
        return unit_partials(slope_mine, slope_other, entries, low, high, waits)

    def hop(value):
        return send(value, ALONG_Z)

    def near_entries(x1, x1_swap):
        return [
            [((x1, (0, i)), (x1, (1, i))) for i in range(4)],
            [((x1_swap, (1, FLIP[i])), (x1_swap, (0, FLIP[i]))) for i in range(4)],
        ]

    def far_entries(q_here, y1, y1_swap, x2, x2_swap, y2, y2_swap):
        entries = [[((x2, i), (x2_swap, FLIP[i])) for i in range(4)]]
        for g in range(4):
            entries.append(
                [
                    ((q_here, (0, g)), (q_here, (1, g))),
                    ((y1, (0, g)), (y1, (1, g))),
                    ((y1_swap, (1, FLIP[g])), (y1_swap, (0, FLIP[g]))),
                    ((y2, g), (y2_swap, FLIP[g])),
                ]
            )
        return entries

    p_here = stack_rows(p_places, 0, size)
    q_here = stack_rows(q_places, 0, size)
    x1, y1 = send(p_here, ALONG_X), send(q_here, ALONG_Y)
    own = units([[(p_places[i], p_places[4 + i]) for i in range(4)]], waits=(p_here, q_here))
    own_got = hop(own[0])
    p_next = stack_rows(p_places, size, size)
    q_next = stack_rows(q_places, size, size)
    own_2 = add_narrow(own[1], own_got)
    own_got = hop(own_2)
    own_3 = add_narrow(own[2], own_got)
    own_got = hop(own_3)
    x1, y1 = lax.optimization_barrier((x1, y1, own_3, p_next, q_next))[:2]
    x2, y2 = send(x1[0], ALONG_X), send(y1[0], ALONG_Y)
    x1_swap, y1_swap = send(x1, SWAP), send(y1, SWAP)

    p_next, q_next = lax.optimization_barrier((p_next, q_next, x1_swap, y1_swap))[:2]
    x1_next, y1_next = send(p_next, ALONG_X), send(q_next, ALONG_Y)
    near0 = units(near_entries(x1, x1_swap), waits=(y1_swap,))
    near0_got = hop(near0[0])
    x2, y2 = lax.optimization_barrier((x2, y2, near0[0]))[:2]
    x2_swap, y2_swap = send(x2, SWAP), send(y2, SWAP)
    placed = place_rows(own[3], own_got, [(0, 0, 0, FEAT // 2)], ())
    far0_entries = far_entries(q_here, y1, y1_swap, x2, x2_swap, y2, y2_swap)
    far0 = units(far0_entries, 0, 2, waits=(placed[2],))
    far0_got = hop(far0[0])
    near0_2 = add_narrow(near0[1], near0_got)
    near0_got = hop(near0_2)
    far0 += units(far0_entries, 2, 4, waits=(near0_2, far0[0]))
    x1, y1 = lax.optimization_barrier((x1_next, y1_next, far0[0]))[:2]
    x2, y2 = send(x1[0], ALONG_X), send(y1[0], ALONG_Y)
    x1, y1 = lax.optimization_barrier((x1, y1, far0[2]))[:2]
    x1_swap, y1_swap = send(x1, SWAP), send(y1, SWAP)
    far0_2 = add_narrow(far0[1], far0_got)
    far0_got = hop(far0_2)
    near1 = units(near_entries(x1, x1_swap), waits=(far0_2, y1_swap))
    near1_got = hop(near1[0])
    near0_3 = add_narrow(near0[2], near0_got)
    near0_got = hop(near0_3)
    x2, y2 = lax.optimization_barrier((x2, y2, near1[0]))[:2]
    x2_swap, y2_swap = send(x2, SWAP), send(y2, SWAP)
    far0_3 = add_narrow(far0[2], far0_got)
    far0_got = hop(far0_3)
    far1_entries = far_entries(q_next, y1, y1_swap, x2, x2_swap, y2, y2_swap)
    far1 = units(far1_entries, 0, 2, waits=(far0_3, near0_3))
    far1_got = hop(far1[0])
    near1_2 = add_narrow(near1[1], near1_got)
    near1_got = hop(near1_2)
    near_pieces = lambda chunk: [(1, chunk * size, 0, size), (2, chunk * size, size, size)]
    far_pieces = lambda chunk: [(3, chunk * size, 0, size)] + [
        (g, FEAT // 2 + chunk * size, (g + 1) * size, size) for g in range(4)
    ]
    placed = place_rows(near0[3], near0_got, near_pieces(0), placed)
    far1 += units(far1_entries, 2, 4, waits=(near1_2, placed[2], far1[0]))
    far1_got = hop(add_narrow(far1[1], far1_got))
    near1_got = hop(add_narrow(near1[2], near1_got))
    placed = place_rows(far0[3], far0_got, far_pieces(0), placed)
    far1_got = hop(after(add_narrow(far1[2], far1_got), placed[2]))
    placed = place_rows(near1[3], near1_got, near_pieces(1), placed)
    placed = place_rows(far1[3], far1_got, far_pieces(1), placed)
    kept, sent, grad_local = placed
    got = send(sent, SWAP)
    grad_local = grad_local[0]
    column_stats = jnp.concatenate([grad_local, early])
    for pairs in (ALONG_Z, ALONG_Z2, ALONG_Z3):
        column_stats = column_stats + send(jnp.concatenate([grad_local, early]), pairs)
    mine_stats = column_stats[: 2 * HALF]
    yours_stats = send(mine_stats, SWAP)

    def all_columns(start):
        a, b = mine_stats[start : start + HALF], yours_stats[start : start + HALF]
        return jnp.concatenate([jnp.where(core == 0, a, b), jnp.where(core == 0, b, a)])

    grad_sq = all_columns(0)
    weight_col_sq = all_columns(HALF)
    row_total = column_stats[2 * HALF]

    clip_factor = jnp.minimum(
        1.0, clip_ratio * jnp.sqrt(weight_col_sq) / (jnp.sqrt(grad_sq) + unit_eps)
    )
    column_sums = clip_factor * clip_factor * grad_sq
    new_column = second_decay * column_factor + (1.0 - second_decay) * (
        column_sums / D + factor_eps
    )
    grad = jnp.concatenate(
        [jnp.where(core == 0, kept, got), jnp.where(core == 0, got, kept)], axis=1
    )
    clipped = grad * clip_factor[None, :]
    row_part = jnp.sum(clipped * clipped, axis=1)
    totals = jnp.concatenate(
        [
            jnp.broadcast_to(jnp.sum(column_sums)[None], (128,)),
            jnp.broadcast_to(jnp.sum(weight_col_sq)[None], (128,)),
        ]
    )
    summed = jnp.sum(everyone(jnp.concatenate([row_part, totals]), "gx", 16), axis=0)
    row_sums, clipped_total, weight_total = summed[:768], summed[768], summed[896]
    new_row = second_decay * row_factor + (1.0 - second_decay) * (row_sums / FF + factor_eps)
    row_mean = (
        second_decay * row_total + (1.0 - second_decay) * (clipped_total / FF + D * factor_eps)
    ) / D
    weight_rms = jnp.sqrt(weight_total / (D * FF))
    update = (
        -weight_rms
        * clipped
        * lax.rsqrt(new_row)[:, None]
        * (jnp.sqrt(row_mean) * lax.rsqrt(new_column))[None, :]
    )
    return (update, new_row, new_column)


def solution(mesh):
    in_specs = (P("gy", "gx"), P("gy", "gx"), P("gy", "gx"), P("gy", "gx"), P("gy"), P("gx"))
    out_specs = (P("gy", "gx"), P("gy"), P("gx"))
    return jax.shard_map(
        per_device, mesh=mesh, in_specs=in_specs, out_specs=out_specs, check_vma=False
    )
```

```python
import jax
import jax.numpy as jnp
from jax import lax
from jax.experimental import pallas as pl
from jax.experimental.pallas import tpu as pltpu
from jax.sharding import PartitionSpec as P

D = 6144
FF = 24576
TOK = 1024
FEAT = 384
HALF = 768
NCH = 2

second_decay = 0.8
clip_ratio = 1.0
unit_eps = 1e-06
factor_eps = 1e-30

BOTH = ("gx", "gy")
FLIP = (0, 2, 1, 3)


def moves(dx, dy, dz, other_core):
    pairs = []
    for y in range(4):
        for x in range(4):
            for z in range(4):
                for core in range(2):
                    s = 1 - 2 * core
                    tx, ty, tz = (x + s * dx) % 4, (y + s * dy) % 4, (z + s * dz) % 4
                    tc = 1 - core if other_core else core
                    pairs.append(((y * 4 + x) * 8 + z * 2 + core, (ty * 4 + tx) * 8 + tz * 2 + tc))
    return pairs


ALONG_X = moves(1, 0, 0, False)
ALONG_Y = moves(0, 1, 0, False)
ALONG_Z = moves(0, 0, 1, False)
ALONG_Z2 = moves(0, 0, 2, False)
ALONG_Z3 = moves(0, 0, 3, False)
SWAP = moves(0, 0, 0, True)


STEPS = (0, -1, 1, 2)
CHEAP = pl.CostEstimate(flops=1024, bytes_accessed=1024, transcendentals=0)


def coordinates():
    gx, gy = lax.axis_index("gx"), lax.axis_index("gy")
    return gx >> 2, gx & 3, gy >> 1, gy & 1


def send(value, pairs):
    return lax.ppermute(value, BOTH, pairs)


def slope_half(preact, upstream, other, waits=()):
    count = 4
    rows = TOK // count

    def kernel(pre_ref, up_ref, *refs):
        out, pre, up, sems = refs[len(waits) :]
        core = coordinates()[3]
        half = 1 - core if other else core
        columns = pl.ds(pl.multiple_of(half * HALF, HALF), HALF)
        for k in range(count):
            at = pl.ds(k * rows, rows)
            pltpu.make_async_copy(pre_ref.at[at, columns], pre.at[at], sems.at[0, k]).start()
            pltpu.make_async_copy(up_ref.at[at, columns], up.at[at], sems.at[1, k]).start()
        for k in range(count):
            at = pl.ds(k * rows, rows)
            pltpu.make_async_copy(pre.at[at], pre.at[at], sems.at[0, k]).wait()
            pltpu.make_async_copy(up.at[at], up.at[at], sems.at[1, k]).wait()

            @pl.loop(0, rows // 16)
            def _(j):
                tile = pl.ds(pl.multiple_of(k * rows + j * 16, 16), 16)
                value = pre[tile].astype(jnp.float32)
                normal_cdf = 0.5 * (1.0 + lax.erf(value * 0.7071067811865476))
                density = jnp.exp(-0.5 * value * value) * 0.3989422804014327
                slope = up[tile].astype(jnp.float32) * (normal_cdf + value * density)
                out[tile] = slope.astype(jnp.bfloat16)

    anywhere = pl.BlockSpec(memory_space=pl.ANY)
    half_block = pltpu.VMEM((TOK, HALF), jnp.bfloat16)
    return pl.pallas_call(
        kernel,
        out_shape=jax.ShapeDtypeStruct((TOK, HALF), jnp.bfloat16),
        in_specs=[pl.BlockSpec(memory_space=pltpu.HBM)] * 2 + [anywhere] * len(waits),
        out_specs=pl.BlockSpec(memory_space=pltpu.VMEM),
        scratch_shapes=[half_block, half_block, pltpu.SemaphoreType.DMA((2, count))],
        compiler_params=pltpu.CompilerParams(vmem_limit_bytes=24 << 20),
        cost_estimate=CHEAP,
    )(preact, upstream, *waits)


def unit_partials(slope_own, slope_other, entries, low, high, waits=()):
    arrays = []
    position = {}
    plan = []
    rows = 0
    for places in entries:
        count = places[0][0][0].shape[-2]
        for i, halves in enumerate(places):
            for h, (array, index) in enumerate(halves):
                if id(array) not in position:
                    position[id(array)] = len(arrays)
                    arrays.append(array)
                plan.append((i, h, rows, count, position[id(array)], index))
        rows += count
    many = high - low

    def kernel(own_ref, other_ref, *refs):
        feature_refs = refs[: len(arrays)]
        outs = refs[len(arrays) + len(waits) : len(arrays) + len(waits) + many]
        held, slopes, feature_sem, slope_sem = refs[len(arrays) + len(waits) + many :]
        pltpu.make_async_copy(own_ref, slopes.at[pl.ds(0, TOK)], slope_sem).start()
        pltpu.make_async_copy(other_ref, slopes.at[pl.ds(TOK, TOK)], slope_sem).start()
        y, _, z, core = coordinates()
        for i in range(4):
            place = ((1 - 2 * core) * (z - y) - STEPS[i] + 3) & 3

            @pl.when((place >= low) & (place < high))
            def _():
                base = pl.multiple_of((place - low) * rows, rows)
                for at, h, start, count, which, index in plan:
                    if at == i:
                        source = feature_refs[which]
                        source = source.at[index] if index is not None else source
                        pltpu.make_async_copy(
                            source,
                            held.at[pl.ds(base + start, count), pl.ds(h * TOK, TOK)],
                            feature_sem,
                        ).start()

        pltpu.make_async_copy(slopes, slopes, slope_sem).wait()
        pltpu.make_async_copy(held, held, feature_sem).wait()

        @pl.loop(0, HALF // 256)
        def _(j):
            columns = pl.ds(pl.multiple_of(j * 256, 256), 256)
            total = jnp.dot(held[...], slopes[:, columns], preferred_element_type=jnp.float32)
            for k, out in enumerate(outs):
                out[:, columns] = total[k * rows : (k + 1) * rows].astype(out.dtype)

    vmem = pl.BlockSpec(memory_space=pltpu.VMEM)
    anywhere = pl.BlockSpec(memory_space=pl.ANY)
    return pl.pallas_call(
        kernel,
        out_shape=tuple(
            jax.ShapeDtypeStruct((rows, HALF), jnp.float32 if k == 3 else jnp.bfloat16)
            for k in range(low, high)
        ),
        in_specs=[anywhere] * (2 + len(arrays) + len(waits)),
        out_specs=(vmem,) * many,
        scratch_shapes=[
            pltpu.VMEM((many * rows, 2 * TOK), jnp.bfloat16),
            pltpu.VMEM((2 * TOK, HALF), jnp.bfloat16),
            pltpu.SemaphoreType.DMA,
            pltpu.SemaphoreType.DMA,
        ],
        compiler_params=pltpu.CompilerParams(vmem_limit_bytes=44 << 20),
        cost_estimate=CHEAP,
    )(slope_own, slope_other, *arrays, *waits)


def add_narrow(a, b):
    return (a.astype(jnp.float32) + b.astype(jnp.float32)).astype(jnp.bfloat16)


def after(value, *before):
    return lax.optimization_barrier((value,) + before)[0]


def turn(inputs):
    def kernel(ref, first, second):
        turned = ref[...].T
        first[...] = turned[: FEAT // 2]
        second[...] = turned[FEAT // 2 :]

    vmem = pl.BlockSpec(memory_space=pltpu.VMEM)
    half = jax.ShapeDtypeStruct((FEAT // 2, TOK), jnp.bfloat16)
    return pl.pallas_call(
        kernel, out_shape=(half, half), in_specs=[vmem], out_specs=(vmem, vmem), cost_estimate=CHEAP
    )(inputs)


def stack_rows(sources, start, count):
    arrays = []
    which = []
    for array, index in sources:
        if not any(array is other for other in arrays):
            arrays.append(array)
        which.append(([array is other for other in arrays].index(True), index))

    def kernel(*refs):
        out = refs[-1]
        for k, (at, index) in enumerate(which):
            source = refs[at] if index is None else refs[at].at[index]
            out[k // 4, k % 4] = source[pl.ds(start, count)]

    vmem = pl.BlockSpec(memory_space=pltpu.VMEM)
    return pl.pallas_call(
        kernel,
        out_shape=jax.ShapeDtypeStruct((2, 4, count, TOK), jnp.bfloat16),
        in_specs=[vmem] * len(arrays),
        out_specs=vmem,
        compiler_params=pltpu.CompilerParams(vmem_limit_bytes=24 << 20),
        cost_estimate=CHEAP,
    )(*arrays)


def place_rows(last, got, pieces, before):
    rows = last.shape[0]

    def kernel(last_ref, got_ref, *refs):
        kept, sent, sums, value, sem = refs[len(before) :]
        total = last_ref[...] + got_ref[...].astype(jnp.float32)
        value[...] = total
        _, x, _, core = coordinates()
        for g, low, start, count in pieces:
            column = (x + (1 - 2 * core) * STEPS[g]) & 3
            row = pl.multiple_of((column & 1) * FEAT + low, 32)
            source = value.at[pl.ds(start, count)]

            @pl.when((column >> 1) == core)
            def _():
                pltpu.make_async_copy(source, kept.at[pl.ds(row, count)], sem).start()

            @pl.when((column >> 1) != core)
            def _():
                pltpu.make_async_copy(source, sent.at[pl.ds(row, count)], sem).start()

        squares = jnp.sum(total * total, axis=0, keepdims=True)
        sums[...] = squares + refs[2][...] if before else squares
        pltpu.make_async_copy(value, value, sem).wait()

    anywhere = pl.BlockSpec(memory_space=pl.ANY)
    vmem = pl.BlockSpec(memory_space=pltpu.VMEM)
    block = jax.ShapeDtypeStruct((HALF, HALF), jnp.float32)
    return pl.pallas_call(
        kernel,
        out_shape=(block, block, jax.ShapeDtypeStruct((1, HALF), jnp.float32)),
        in_specs=[vmem, vmem]
        + ([anywhere, anywhere, vmem] if before else []),
        out_specs=(anywhere, anywhere, vmem),
        scratch_shapes=[pltpu.VMEM((rows, HALF), jnp.float32), pltpu.SemaphoreType.DMA],
        input_output_aliases={2: 0, 3: 1} if before else {},
        compiler_params=pltpu.CompilerParams(vmem_limit_bytes=24 << 20),
        cost_estimate=CHEAP,
    )(last, got, *before)


def clip_rows(mine, yours, kept, got):
    def kernel(mine_ref, yours_ref, kept_ref, got_ref, payload, clips, sums):
        core = coordinates()[3]
        total = weights = None
        squares = None
        both = []
        for stats, grad in ((mine_ref, kept_ref), (yours_ref, got_ref)):
            grad_sq, weight_sq = stats[:, :HALF], stats[:, HALF : 2 * HALF]
            clip = jnp.minimum(
                1.0, clip_ratio * jnp.sqrt(weight_sq) / (jnp.sqrt(grad_sq) + unit_eps)
            )
            column = clip * clip * grad_sq
            both.append((clip, column))
            clipped = grad[...] * clip
            squares = clipped * clipped if squares is None else squares + clipped * clipped
            column_total = jnp.sum(column, axis=1, keepdims=True)
            weight_total = jnp.sum(weight_sq, axis=1, keepdims=True)
            total = column_total if total is None else total + column_total
            weights = weight_total if weights is None else weights + weight_total
        for at in range(2):
            columns = pl.ds(at * HALF, HALF)
            here = core == at
            clips[:, columns] = jnp.where(here, both[0][0], both[1][0])
            sums[:, columns] = jnp.where(here, both[0][1], both[1][1])
        payload[:, :HALF] = lax.dot_general(
            jnp.ones((16, HALF), jnp.float32),
            squares,
            (((1,), (1,)), ((), ())),
            precision=lax.Precision.HIGHEST,
            preferred_element_type=jnp.float32,
        )
        payload[:, HALF : HALF + 128] = jnp.broadcast_to(total, (16, 128))
        payload[:, HALF + 128 :] = jnp.broadcast_to(weights, (16, 128))

    vmem = pl.BlockSpec(memory_space=pltpu.VMEM)
    columns = jax.ShapeDtypeStruct((1, 2 * HALF), jnp.float32)
    return pl.pallas_call(
        kernel,
        out_shape=(jax.ShapeDtypeStruct((16, HALF + 256), jnp.float32), columns, columns),
        in_specs=[vmem] * 4,
        out_specs=(vmem,) * 3,
        compiler_params=pltpu.CompilerParams(vmem_limit_bytes=32 << 20),
        cost_estimate=CHEAP,
    )(mine, yours, kept, got)


def finish(gathered, row_total, clips, sums, row_factor, column_factor, kept, got):
    step = 128

    def kernel(
        gathered_ref, row_total_ref, clip_ref, sum_ref, row_ref, column_ref, kept_ref, got_ref,
        update, new_row_ref, new_column_ref,
    ):
        core = coordinates()[3]
        at = pl.ds(pl.multiple_of(pl.program_id(0) * step, step), step)
        clipped_total = jnp.sum(gathered_ref[:, HALF : HALF + 1], axis=0, keepdims=True)
        weight_total = jnp.sum(gathered_ref[:, HALF + 128 : HALF + 129], axis=0, keepdims=True)
        row_mean = (
            second_decay * row_total_ref[:, :1]
            + (1.0 - second_decay) * (clipped_total / FF + D * factor_eps)
        ) / D
        weight_rms = jnp.sqrt(weight_total / (D * FF))
        new_column = second_decay * column_ref[...] + (1.0 - second_decay) * (
            sum_ref[...] / D + factor_eps
        )
        new_column_ref[...] = new_column
        row_sums = jnp.sum(gathered_ref[:, at], axis=0, keepdims=True)
        new_row = second_decay * row_ref[:, at] + (1.0 - second_decay) * (
            row_sums / FF + factor_eps
        )
        new_row_ref[:, at] = new_row
        down = jnp.broadcast_to(lax.rsqrt(new_row), (step, step)).T[:, :1]
        across = -weight_rms * clip_ref[...] * (jnp.sqrt(row_mean) * lax.rsqrt(new_column))
        first = jnp.where(core == 0, kept_ref[...], got_ref[...])
        second = jnp.where(core == 0, got_ref[...], kept_ref[...])
        update[:, :HALF] = first * across[:, :HALF] * down
        update[:, HALF:] = second * across[:, HALF:] * down

    whole = lambda *shape: pl.BlockSpec(shape, lambda i: (0, 0))
    rows = lambda width: pl.BlockSpec((step, width), lambda i: (i, 0))
    return pl.pallas_call(
        kernel,
        grid=(HALF // step,),
        out_shape=(
            jax.ShapeDtypeStruct((HALF, 2 * HALF), jnp.float32),
            jax.ShapeDtypeStruct((1, HALF), jnp.float32),
            jax.ShapeDtypeStruct((1, 2 * HALF), jnp.float32),
        ),
        in_specs=[
            whole(16, HALF + 256), whole(1, 128), whole(1, 2 * HALF), whole(1, 2 * HALF),
            whole(1, HALF), whole(1, 2 * HALF), rows(HALF), rows(HALF),
        ],
        out_specs=(rows(2 * HALF), whole(1, HALF), whole(1, 2 * HALF)),
        compiler_params=pltpu.CompilerParams(vmem_limit_bytes=32 << 20),
        cost_estimate=CHEAP,
    )(gathered, row_total, clips, sums, row_factor, column_factor, kept, got)


def per_device(inputs, preact, upstream, weight, row_factor, column_factor):
    core = coordinates()[3]

    p, q = turn(inputs)
    size = FEAT // 2 // NCH

    p_swap, q_swap = send(p, SWAP), send(q, SWAP)
    ya, xa = send(p, ALONG_Y), send(q, ALONG_X)
    yb, xb = send(p_swap, ALONG_Y), send(q_swap, ALONG_X)
    slope_yours = slope_half(preact, upstream, True, (p_swap, q_swap))
    slope_other = send(slope_yours, SWAP)
    slope_mine = slope_half(preact, upstream, False, (p_swap, q_swap))
    ya, xa = lax.optimization_barrier((ya, xa, slope_yours, slope_mine))[:2]
    y2, x2 = send(ya, ALONG_Y), send(xa, ALONG_X)
    ya_swap, xa_swap = send(ya, SWAP), send(xa, SWAP)
    yb, xb = lax.optimization_barrier((yb, xb, ya_swap, xa_swap))[:2]
    yb_swap, xb_swap = send(yb, SWAP), send(xb, SWAP)
    y2, x2 = lax.optimization_barrier((y2, x2, yb_swap, xb_swap))[:2]
    y2_swap, x2_swap = send(y2, SWAP), send(x2, SWAP)
    p_places = [(p, None), (ya, None), (yb_swap, None), (y2, None)]
    p_places += [(p_swap, None), (yb, None), (ya_swap, None), (y2_swap, None)]
    q_places = [(q, None), (xa, None), (xb_swap, None), (x2, None)]
    q_places += [(q_swap, None), (xb, None), (xa_swap, None), (x2_swap, None)]

    def units(entries, low=0, high=4, waits=()):
        return unit_partials(slope_mine, slope_other, entries, low, high, waits)

    def hop(value):
        return send(value, ALONG_Z)

    def near_entries(x1, x1_swap):
        return [
            [((x1, (0, i)), (x1, (1, i))) for i in range(4)],
            [((x1_swap, (1, FLIP[i])), (x1_swap, (0, FLIP[i]))) for i in range(4)],
        ]

    def far_entries(q_here, y1, y1_swap, x2, x2_swap, y2, y2_swap):
        entries = [[((x2, i), (x2_swap, FLIP[i])) for i in range(4)]]
        for g in range(4):
            entries.append(
                [
                    ((q_here, (0, g)), (q_here, (1, g))),
                    ((y1, (0, g)), (y1, (1, g))),
                    ((y1_swap, (1, FLIP[g])), (y1_swap, (0, FLIP[g]))),
                    ((y2, g), (y2_swap, FLIP[g])),
                ]
            )
        return entries

    p_here = stack_rows(p_places, 0, size)
    q_here = stack_rows(q_places, 0, size)
    x1, y1 = send(p_here, ALONG_X), send(q_here, ALONG_Y)
    own = units([[(p_places[i], p_places[4 + i]) for i in range(4)]], waits=(p_here, q_here))
    own_got = hop(own[0])
    weight = after(weight, own[0])
    weight_local = jnp.sum(weight * weight, axis=0)
    row_local = jnp.broadcast_to(jnp.sum(row_factor)[None], (128,))
    weight_mine = lax.dynamic_slice_in_dim(weight_local, core * HALF, HALF)
    weight_yours = lax.dynamic_slice_in_dim(weight_local, (1 - core) * HALF, HALF)
    early = jnp.concatenate([weight_mine, row_local])
    early = early + send(jnp.concatenate([weight_yours, row_local]), SWAP)
    p_next = stack_rows(p_places, size, size)
    q_next = stack_rows(q_places, size, size)
    own_2 = add_narrow(own[1], own_got)
    own_got = hop(own_2)
    own_3 = add_narrow(own[2], own_got)
    x1, y1 = lax.optimization_barrier((x1, y1, own_3, p_next, q_next, early))[:2]
    x2, y2 = send(x1[0], ALONG_X), send(y1[0], ALONG_Y)
    x1_swap, y1_swap = send(x1, SWAP), send(y1, SWAP)

    p_next, q_next = lax.optimization_barrier((p_next, q_next, x1_swap, y1_swap))[:2]
    x1_next, y1_next = send(p_next, ALONG_X), send(q_next, ALONG_Y)
    near0 = units(near_entries(x1, x1_swap), waits=(y1_swap,))
    near0_got = hop(near0[0])
    x2, y2 = lax.optimization_barrier((x2, y2, near0[0]))[:2]
    x2_swap, y2_swap = send(x2, SWAP), send(y2, SWAP)
    far0_entries = far_entries(q_here, y1, y1_swap, x2, x2_swap, y2, y2_swap)
    near0_2 = add_narrow(near0[1], near0_got)
    near0_got = hop(near0_2)
    far0 = units(far0_entries, 0, 2, waits=(near0_2,))
    far0_got = hop(far0[0])
    near0_3 = add_narrow(near0[2], after(near0_got, far0[0]))
    x1, y1 = lax.optimization_barrier((x1_next, y1_next, far0[0], near0_3))[:2]
    x2, y2 = send(x1[0], ALONG_X), send(y1[0], ALONG_Y)
    x1_swap, y1_swap = send(x1, SWAP), send(y1, SWAP)
    near0_got = hop(after(near0_3, x1_swap, y1_swap))
    own_got = hop(after(own_3, x1_swap, y1_swap))
    far0_2 = add_narrow(far0[1], after(far0_got, x1_swap))
    far0_got = hop(far0_2)
    far0 += units(far0_entries, 2, 4, waits=(far0_2,))
    near_pieces = lambda chunk: [(1, chunk * size, 0, size), (2, chunk * size, size, size)]
    far_pieces = lambda chunk: [(3, chunk * size, 0, size)] + [
        (g, FEAT // 2 + chunk * size, (g + 1) * size, size) for g in range(4)
    ]
    placed = place_rows(own[3], after(own_got, far0[2]), [(0, 0, 0, FEAT // 2)], ())
    placed = place_rows(near0[3], after(near0_got, far0[2]), near_pieces(0), placed)
    near1 = units(near_entries(x1, x1_swap), waits=(far0[2], placed[2], y1_swap))
    near1_got = hop(near1[0])
    x2, y2 = lax.optimization_barrier((x2, y2, near1[0]))[:2]
    x2_swap, y2_swap = send(x2, SWAP), send(y2, SWAP)
    far1_entries = far_entries(q_next, y1, y1_swap, x2, x2_swap, y2, y2_swap)
    far1 = units(far1_entries[:2])
    far1_got = hop(far1[0])
    near1_2 = add_narrow(near1[1], after(near1_got, far1[0]))
    near1_got = hop(near1_2)
    far0_3 = add_narrow(far0[2], after(far0_got, far1[0]))
    far0_got = hop(far0_3)
    last1 = units(far1_entries[2:], waits=(far0_3, near1_2))
    last1_got = hop(last1[0])
    near1_3 = add_narrow(near1[2], after(near1_got, last1[0]))
    far1_2 = add_narrow(far1[1], after(far1_got, last1[0]))
    far1_got = hop(far1_2)
    near1_got = hop(near1_3)
    placed = place_rows(far0[3], after(far0_got, far1_2), far_pieces(0), placed)
    last1_2 = add_narrow(last1[1], after(last1_got, placed[2]))
    last1_got = hop(last1_2)
    placed = place_rows(near1[3], after(near1_got, last1_2), near_pieces(1), placed)
    far1_got = hop(add_narrow(far1[2], after(far1_got, placed[2])))
    last1_got = hop(add_narrow(last1[2], last1_got))
    placed = place_rows(far1[3], far1_got, far_pieces(1)[:2], placed)
    last_pieces = [(g, low, start - 2 * size, count) for g, low, start, count in far_pieces(1)[2:]]
    placed = place_rows(last1[3], last1_got, last_pieces, placed)
    kept, sent, grad_local = placed
    got = send(sent, SWAP)
    local = jnp.concatenate([grad_local, early[None, :]], axis=1)
    column_stats = local
    for pairs in (ALONG_Z, ALONG_Z2, ALONG_Z3):
        column_stats = column_stats + send(local, pairs)
    yours_stats = send(column_stats, SWAP)
    payload, clips, sums = clip_rows(column_stats, yours_stats, kept, got)
    gathered = lax.all_to_all(payload[:, None, :], "gx", 0, 0, tiled=True)[:, 0]
    update, new_row, new_column = finish(
        gathered, column_stats[:, 2 * HALF :], clips, sums, row_factor[None, :],
        column_factor[None, :], kept, got,
    )
    return (update, new_row[0], new_column[0])


def solution(mesh):
    in_specs = (P("gy", "gx"), P("gy", "gx"), P("gy", "gx"), P("gy", "gx"), P("gy"), P("gx"))
    out_specs = (P("gy", "gx"), P("gy"), P("gx"))
    return jax.shard_map(
        per_device, mesh=mesh, in_specs=in_specs, out_specs=out_specs, check_vma=False
    )
```

```python
import jax
import jax.numpy as jnp
from jax import lax
from jax.experimental import pallas as pl
from jax.experimental.pallas import tpu as pltpu
from jax.sharding import PartitionSpec as P

D = 6144
FF = 24576
TOK = 1024
FEAT = 384
HALF = 768
NCH = 2

second_decay = 0.8
clip_ratio = 1.0
unit_eps = 1e-06
factor_eps = 1e-30

BOTH = ("gx", "gy")
FLIP = (0, 2, 1, 3)


def moves(dx, dy, dz, other_core):
    pairs = []
    for y in range(4):
        for x in range(4):
            for z in range(4):
                for core in range(2):
                    s = 1 - 2 * core
                    tx, ty, tz = (x + s * dx) % 4, (y + s * dy) % 4, (z + s * dz) % 4
                    tc = 1 - core if other_core else core
                    pairs.append(((y * 4 + x) * 8 + z * 2 + core, (ty * 4 + tx) * 8 + tz * 2 + tc))
    return pairs


ALONG_X = moves(1, 0, 0, False)
ALONG_Y = moves(0, 1, 0, False)
ALONG_Z = moves(0, 0, 1, False)
ALONG_Z2 = moves(0, 0, 2, False)
ALONG_Z3 = moves(0, 0, 3, False)
ROUND_X = [moves(k, 0, 0, False) for k in (1, 2, 3)]
ROUND_Y = [moves(0, k, 0, False) for k in (1, 2, 3)]
SWAP = moves(0, 0, 0, True)


STEPS = (0, -1, 1, 2)
CHEAP = pl.CostEstimate(flops=1024, bytes_accessed=1024, transcendentals=0)


def coordinates():
    gx, gy = lax.axis_index("gx"), lax.axis_index("gy")
    return gx >> 2, gx & 3, gy >> 1, gy & 1


def send(value, pairs):
    return lax.ppermute(value, BOTH, pairs)


def slope_half(preact, upstream, other, waits=()):
    count = 4
    rows = TOK // count

    def kernel(pre_ref, up_ref, *refs):
        out, pre, up, sems = refs[len(waits) :]
        core = coordinates()[3]
        half = 1 - core if other else core
        columns = pl.ds(pl.multiple_of(half * HALF, HALF), HALF)
        for k in range(count):
            at = pl.ds(k * rows, rows)
            pltpu.make_async_copy(pre_ref.at[at, columns], pre.at[at], sems.at[0, k]).start()
            pltpu.make_async_copy(up_ref.at[at, columns], up.at[at], sems.at[1, k]).start()
        for k in range(count):
            at = pl.ds(k * rows, rows)
            pltpu.make_async_copy(pre.at[at], pre.at[at], sems.at[0, k]).wait()
            pltpu.make_async_copy(up.at[at], up.at[at], sems.at[1, k]).wait()

            @pl.loop(0, rows // 16)
            def _(j):
                tile = pl.ds(pl.multiple_of(k * rows + j * 16, 16), 16)
                value = pre[tile].astype(jnp.float32)
                normal_cdf = 0.5 * (1.0 + lax.erf(value * 0.7071067811865476))
                density = jnp.exp(-0.5 * value * value) * 0.3989422804014327
                slope = up[tile].astype(jnp.float32) * (normal_cdf + value * density)
                out[tile] = slope.astype(jnp.bfloat16)

    anywhere = pl.BlockSpec(memory_space=pl.ANY)
    half_block = pltpu.VMEM((TOK, HALF), jnp.bfloat16)
    return pl.pallas_call(
        kernel,
        out_shape=jax.ShapeDtypeStruct((TOK, HALF), jnp.bfloat16),
        in_specs=[pl.BlockSpec(memory_space=pltpu.HBM)] * 2 + [anywhere] * len(waits),
        out_specs=pl.BlockSpec(memory_space=pltpu.VMEM),
        scratch_shapes=[half_block, half_block, pltpu.SemaphoreType.DMA((2, count))],
        compiler_params=pltpu.CompilerParams(vmem_limit_bytes=24 << 20),
        cost_estimate=CHEAP,
    )(preact, upstream, *waits)


def unit_partials(slope_own, slope_other, entries, low, high, waits=()):
    arrays = []
    position = {}
    plan = []
    rows = 0
    for places in entries:
        count = places[0][0][0].shape[-2]
        for i, halves in enumerate(places):
            for h, (array, index) in enumerate(halves):
                if id(array) not in position:
                    position[id(array)] = len(arrays)
                    arrays.append(array)
                plan.append((i, h, rows, count, position[id(array)], index))
        rows += count
    many = high - low

    def kernel(own_ref, other_ref, *refs):
        feature_refs = refs[: len(arrays)]
        outs = refs[len(arrays) + len(waits) : len(arrays) + len(waits) + many]
        held, slopes, feature_sem, slope_sem = refs[len(arrays) + len(waits) + many :]
        pltpu.make_async_copy(own_ref, slopes.at[pl.ds(0, TOK)], slope_sem).start()
        pltpu.make_async_copy(other_ref, slopes.at[pl.ds(TOK, TOK)], slope_sem).start()
        y, _, z, core = coordinates()
        for i in range(4):
            place = ((1 - 2 * core) * (z - y) - STEPS[i] + 3) & 3

            @pl.when((place >= low) & (place < high))
            def _():
                base = pl.multiple_of((place - low) * rows, rows)
                for at, h, start, count, which, index in plan:
                    if at == i:
                        source = feature_refs[which]
                        source = source.at[index] if index is not None else source
                        pltpu.make_async_copy(
                            source,
                            held.at[pl.ds(base + start, count), pl.ds(h * TOK, TOK)],
                            feature_sem,
                        ).start()

        pltpu.make_async_copy(slopes, slopes, slope_sem).wait()
        pltpu.make_async_copy(held, held, feature_sem).wait()

        @pl.loop(0, HALF // 256)
        def _(j):
            columns = pl.ds(pl.multiple_of(j * 256, 256), 256)
            total = jnp.dot(held[...], slopes[:, columns], preferred_element_type=jnp.float32)
            for k, out in enumerate(outs):
                out[:, columns] = total[k * rows : (k + 1) * rows].astype(out.dtype)

    vmem = pl.BlockSpec(memory_space=pltpu.VMEM)
    anywhere = pl.BlockSpec(memory_space=pl.ANY)
    return pl.pallas_call(
        kernel,
        out_shape=tuple(
            jax.ShapeDtypeStruct((rows, HALF), jnp.float32 if k == 3 else jnp.bfloat16)
            for k in range(low, high)
        ),
        in_specs=[anywhere] * (2 + len(arrays) + len(waits)),
        out_specs=(vmem,) * many,
        scratch_shapes=[
            pltpu.VMEM((many * rows, 2 * TOK), jnp.bfloat16),
            pltpu.VMEM((2 * TOK, HALF), jnp.bfloat16),
            pltpu.SemaphoreType.DMA,
            pltpu.SemaphoreType.DMA,
        ],
        compiler_params=pltpu.CompilerParams(vmem_limit_bytes=44 << 20),
        cost_estimate=CHEAP,
    )(slope_own, slope_other, *arrays, *waits)


def add_narrow(a, b):
    return (a.astype(jnp.float32) + b.astype(jnp.float32)).astype(jnp.bfloat16)


def after(value, *before):
    return lax.optimization_barrier((value,) + before)[0]


def turn(inputs):
    def kernel(ref, first, second):
        turned = ref[...].T
        first[...] = turned[: FEAT // 2]
        second[...] = turned[FEAT // 2 :]

    vmem = pl.BlockSpec(memory_space=pltpu.VMEM)
    half = jax.ShapeDtypeStruct((FEAT // 2, TOK), jnp.bfloat16)
    return pl.pallas_call(
        kernel, out_shape=(half, half), in_specs=[vmem], out_specs=(vmem, vmem), cost_estimate=CHEAP
    )(inputs)


def stack_rows(sources, start, count):
    arrays = []
    which = []
    for array, index in sources:
        if not any(array is other for other in arrays):
            arrays.append(array)
        which.append(([array is other for other in arrays].index(True), index))

    def kernel(*refs):
        out = refs[-1]
        for k, (at, index) in enumerate(which):
            source = refs[at] if index is None else refs[at].at[index]
            out[k // 4, k % 4] = source[pl.ds(start, count)]

    vmem = pl.BlockSpec(memory_space=pltpu.VMEM)
    return pl.pallas_call(
        kernel,
        out_shape=jax.ShapeDtypeStruct((2, 4, count, TOK), jnp.bfloat16),
        in_specs=[vmem] * len(arrays),
        out_specs=vmem,
        compiler_params=pltpu.CompilerParams(vmem_limit_bytes=24 << 20),
        cost_estimate=CHEAP,
    )(*arrays)


def place_rows(last, got, pieces, before):
    rows = last.shape[0]

    def kernel(last_ref, got_ref, *refs):
        kept, sent, sums, value, sem = refs[len(before) :]
        total = last_ref[...] + got_ref[...].astype(jnp.float32)
        value[...] = total
        _, x, _, core = coordinates()
        for g, low, start, count in pieces:
            column = (x + (1 - 2 * core) * STEPS[g]) & 3
            row = pl.multiple_of((column & 1) * FEAT + low, 32)
            source = value.at[pl.ds(start, count)]

            @pl.when((column >> 1) == core)
            def _():
                pltpu.make_async_copy(source, kept.at[pl.ds(row, count)], sem).start()

            @pl.when((column >> 1) != core)
            def _():
                pltpu.make_async_copy(source, sent.at[pl.ds(row, count)], sem).start()

        squares = jnp.sum(total * total, axis=0, keepdims=True)
        sums[...] = squares + refs[2][...] if before else squares
        pltpu.make_async_copy(value, value, sem).wait()

    anywhere = pl.BlockSpec(memory_space=pl.ANY)
    vmem = pl.BlockSpec(memory_space=pltpu.VMEM)
    block = jax.ShapeDtypeStruct((HALF, HALF), jnp.float32)
    return pl.pallas_call(
        kernel,
        out_shape=(block, block, jax.ShapeDtypeStruct((1, HALF), jnp.float32)),
        in_specs=[vmem, vmem]
        + ([anywhere, anywhere, vmem] if before else []),
        out_specs=(anywhere, anywhere, vmem),
        scratch_shapes=[pltpu.VMEM((rows, HALF), jnp.float32), pltpu.SemaphoreType.DMA],
        input_output_aliases={2: 0, 3: 1} if before else {},
        compiler_params=pltpu.CompilerParams(vmem_limit_bytes=24 << 20),
        cost_estimate=CHEAP,
    )(last, got, *before)


def clip_rows(mine, yours, column_factor, kept, got):
    def kernel(mine_ref, yours_ref, column_ref, kept_ref, got_ref, payload, clips, news):
        core = coordinates()[3]
        total = weights = None
        squares = None
        both = []
        for stats, grad in ((mine_ref, kept_ref), (yours_ref, got_ref)):
            grad_sq, weight_sq = stats[:, :HALF], stats[:, HALF : 2 * HALF]
            clip = jnp.minimum(
                1.0, clip_ratio * jnp.sqrt(weight_sq) / (jnp.sqrt(grad_sq) + unit_eps)
            )
            column = clip * clip * grad_sq
            both.append((clip, column))
            clipped = grad[...] * clip
            squares = clipped * clipped if squares is None else squares + clipped * clipped
            column_total = jnp.sum(column, axis=1, keepdims=True)
            weight_total = jnp.sum(weight_sq, axis=1, keepdims=True)
            total = column_total if total is None else total + column_total
            weights = weight_total if weights is None else weights + weight_total
        for at in range(2):
            columns = pl.ds(at * HALF, HALF)
            here = core == at
            clips[:, columns] = jnp.where(here, both[0][0], both[1][0])
            sums = jnp.where(here, both[0][1], both[1][1])
            news[:, columns] = second_decay * column_ref[:, columns] + (1.0 - second_decay) * (
                sums / D + factor_eps
            )
        row_sums = lax.dot_general(
            jnp.ones((8, HALF), jnp.float32),
            squares,
            (((1,), (1,)), ((), ())),
            precision=lax.Precision.HIGHEST,
            preferred_element_type=jnp.float32,
        )
        payload[:, :HALF] = row_sums[:1]
        payload[:, HALF : HALF + 128] = jnp.broadcast_to(total, (1, 128))
        payload[:, HALF + 128 :] = jnp.broadcast_to(weights, (1, 128))

    vmem = pl.BlockSpec(memory_space=pltpu.VMEM)
    columns = jax.ShapeDtypeStruct((1, 2 * HALF), jnp.float32)
    return pl.pallas_call(
        kernel,
        out_shape=(jax.ShapeDtypeStruct((1, HALF + 256), jnp.float32), columns, columns),
        in_specs=[vmem] * 5,
        out_specs=(vmem,) * 3,
        compiler_params=pltpu.CompilerParams(vmem_limit_bytes=32 << 20),
        cost_estimate=CHEAP,
    )(mine, yours, column_factor, kept, got)


def finish(summed, row_total, clips, new_column, row_factor, kept, got):
    step = 128

    def kernel(
        summed_ref, row_total_ref, clip_ref, column_ref, row_ref, kept_ref, got_ref,
        update, new_row_ref,
    ):
        core = coordinates()[3]
        at = pl.ds(pl.multiple_of(pl.program_id(0) * step, step), step)
        clipped_total = summed_ref[:, HALF : HALF + 1]
        weight_total = summed_ref[:, HALF + 128 : HALF + 129]
        row_mean = (
            second_decay * row_total_ref[:, :1]
            + (1.0 - second_decay) * (clipped_total / FF + D * factor_eps)
        ) / D
        weight_rms = jnp.sqrt(weight_total / (D * FF))
        row_sums = summed_ref[:, at]
        new_row = second_decay * row_ref[:, at] + (1.0 - second_decay) * (
            row_sums / FF + factor_eps
        )
        new_row_ref[:, at] = new_row
        down = jnp.broadcast_to(lax.rsqrt(new_row), (step, step)).T[:, :1]
        across = -weight_rms * clip_ref[...] * (jnp.sqrt(row_mean) * lax.rsqrt(column_ref[...]))
        first = jnp.where(core == 0, kept_ref[...], got_ref[...])
        second = jnp.where(core == 0, got_ref[...], kept_ref[...])
        update[:, :HALF] = first * across[:, :HALF] * down
        update[:, HALF:] = second * across[:, HALF:] * down

    whole = lambda *shape: pl.BlockSpec(shape, lambda i: (0, 0))
    rows = lambda width: pl.BlockSpec((step, width), lambda i: (i, 0))
    return pl.pallas_call(
        kernel,
        grid=(HALF // step,),
        out_shape=(
            jax.ShapeDtypeStruct((HALF, 2 * HALF), jnp.float32),
            jax.ShapeDtypeStruct((1, HALF), jnp.float32),
        ),
        in_specs=[
            whole(1, HALF + 256), whole(1, 128), whole(1, 2 * HALF), whole(1, 2 * HALF),
            whole(1, HALF), rows(HALF), rows(HALF),
        ],
        out_specs=(rows(2 * HALF), whole(1, HALF)),
        compiler_params=pltpu.CompilerParams(vmem_limit_bytes=32 << 20),
        cost_estimate=CHEAP,
    )(summed, row_total, clips, new_column, row_factor, kept, got)


def per_device(inputs, preact, upstream, weight, row_factor, column_factor):
    core = coordinates()[3]

    p, q = turn(inputs)
    size = FEAT // 2 // NCH

    p_swap, q_swap = send(p, SWAP), send(q, SWAP)
    ya, xa = send(p, ALONG_Y), send(q, ALONG_X)
    yb, xb = send(p_swap, ALONG_Y), send(q_swap, ALONG_X)
    slope_yours = slope_half(preact, upstream, True, (p_swap, q_swap))
    slope_other = send(slope_yours, SWAP)
    slope_mine = slope_half(preact, upstream, False, (p_swap, q_swap))
    ya, xa = lax.optimization_barrier((ya, xa, slope_yours, slope_mine))[:2]
    y2, x2 = send(ya, ALONG_Y), send(xa, ALONG_X)
    ya_swap, xa_swap = send(ya, SWAP), send(xa, SWAP)
    yb, xb = lax.optimization_barrier((yb, xb, ya_swap, xa_swap))[:2]
    yb_swap, xb_swap = send(yb, SWAP), send(xb, SWAP)
    y2, x2 = lax.optimization_barrier((y2, x2, yb_swap, xb_swap))[:2]
    y2_swap, x2_swap = send(y2, SWAP), send(x2, SWAP)
    p_places = [(p, None), (ya, None), (yb_swap, None), (y2, None)]
    p_places += [(p_swap, None), (yb, None), (ya_swap, None), (y2_swap, None)]
    q_places = [(q, None), (xa, None), (xb_swap, None), (x2, None)]
    q_places += [(q_swap, None), (xb, None), (xa_swap, None), (x2_swap, None)]

    def units(entries, low=0, high=4, waits=()):
        return unit_partials(slope_mine, slope_other, entries, low, high, waits)

    def hop(value):
        return send(value, ALONG_Z)

    def near_entries(x1, x1_swap):
        return [
            [((x1, (0, i)), (x1, (1, i))) for i in range(4)],
            [((x1_swap, (1, FLIP[i])), (x1_swap, (0, FLIP[i]))) for i in range(4)],
        ]

    def far_entries(q_here, y1, y1_swap, x2, x2_swap, y2, y2_swap):
        entries = [[((x2, i), (x2_swap, FLIP[i])) for i in range(4)]]
        for g in range(4):
            entries.append(
                [
                    ((q_here, (0, g)), (q_here, (1, g))),
                    ((y1, (0, g)), (y1, (1, g))),
                    ((y1_swap, (1, FLIP[g])), (y1_swap, (0, FLIP[g]))),
                    ((y2, g), (y2_swap, FLIP[g])),
                ]
            )
        return entries

    p_here = stack_rows(p_places, 0, size)
    q_here = stack_rows(q_places, 0, size)
    x1, y1 = send(p_here, ALONG_X), send(q_here, ALONG_Y)
    own = units([[(p_places[i], p_places[4 + i]) for i in range(4)]], waits=(p_here, q_here))
    own_got = hop(own[0])
    weight = after(weight, own[0])
    weight_local = jnp.sum(weight * weight, axis=0)
    row_local = jnp.broadcast_to(jnp.sum(row_factor)[None], (128,))
    weight_mine = lax.dynamic_slice_in_dim(weight_local, core * HALF, HALF)
    weight_yours = lax.dynamic_slice_in_dim(weight_local, (1 - core) * HALF, HALF)
    early = jnp.concatenate([weight_mine, row_local])
    early = early + send(jnp.concatenate([weight_yours, row_local]), SWAP)
    p_next = stack_rows(p_places, size, size)
    q_next = stack_rows(q_places, size, size)
    own_2 = add_narrow(own[1], own_got)
    own_got = hop(own_2)
    own_3 = add_narrow(own[2], own_got)
    x1, y1 = lax.optimization_barrier((x1, y1, own_3, p_next, q_next, early))[:2]
    x2, y2 = send(x1[0], ALONG_X), send(y1[0], ALONG_Y)
    x1_swap, y1_swap = send(x1, SWAP), send(y1, SWAP)

    p_next, q_next = lax.optimization_barrier((p_next, q_next, x1_swap, y1_swap))[:2]
    x1_next, y1_next = send(p_next, ALONG_X), send(q_next, ALONG_Y)
    near0 = units(near_entries(x1, x1_swap), waits=(y1_swap,))
    near0_got = hop(near0[0])
    x2, y2 = lax.optimization_barrier((x2, y2, near0[0]))[:2]
    x2_swap, y2_swap = send(x2, SWAP), send(y2, SWAP)
    far0_entries = far_entries(q_here, y1, y1_swap, x2, x2_swap, y2, y2_swap)
    near0_2 = add_narrow(near0[1], near0_got)
    near0_got = hop(near0_2)
    far0 = units(far0_entries, 0, 2, waits=(near0_2,))
    far0_got = hop(far0[0])
    near0_3 = add_narrow(near0[2], after(near0_got, far0[0]))
    x1, y1 = lax.optimization_barrier((x1_next, y1_next, far0[0], near0_3))[:2]
    x2, y2 = send(x1[0], ALONG_X), send(y1[0], ALONG_Y)
    x1_swap, y1_swap = send(x1, SWAP), send(y1, SWAP)
    near0_got = hop(after(near0_3, x1_swap, y1_swap))
    own_got = hop(after(own_3, x1_swap, y1_swap))
    far0_2 = add_narrow(far0[1], after(far0_got, x1_swap))
    far0_got = hop(far0_2)
    far0 += units(far0_entries, 2, 4, waits=(far0_2,))
    near_pieces = lambda chunk: [(1, chunk * size, 0, size), (2, chunk * size, size, size)]
    far_pieces = lambda chunk: [(3, chunk * size, 0, size)] + [
        (g, FEAT // 2 + chunk * size, (g + 1) * size, size) for g in range(4)
    ]
    placed = place_rows(own[3], after(own_got, far0[2]), [(0, 0, 0, FEAT // 2)], ())
    near1 = units(near_entries(x1, x1_swap), waits=(far0[2], placed[2], y1_swap))
    near1_got = hop(near1[0])
    x2, y2 = lax.optimization_barrier((x2, y2, near1[0]))[:2]
    x2_swap, y2_swap = send(x2, SWAP), send(y2, SWAP)
    far1_entries = far_entries(q_next, y1, y1_swap, x2, x2_swap, y2, y2_swap)
    far0_3 = add_narrow(far0[2], far0_got)
    far0_got = hop(far0_3)
    far1 = units(far1_entries[:2], waits=(far0_3,))
    far1_got = hop(far1[0])
    near1_2 = add_narrow(near1[1], after(near1_got, far1[0]))
    near1_got = hop(near1_2)
    placed = place_rows(near0[3], after(near0_got, far1[0]), near_pieces(0), placed)
    last1 = units(far1_entries[2:], waits=(near1_2, placed[2]))
    last1_got = hop(last1[0])
    near1_3 = add_narrow(near1[2], after(near1_got, last1[0]))
    far1_2 = add_narrow(far1[1], after(far1_got, last1[0]))
    far1_got = hop(far1_2)
    near1_got = hop(near1_3)
    placed = place_rows(far0[3], after(far0_got, far1_2), far_pieces(0), placed)
    last1_2 = add_narrow(last1[1], after(last1_got, placed[2]))
    last1_got = hop(last1_2)
    placed = place_rows(near1[3], after(near1_got, last1_2), near_pieces(1), placed)
    far1_got = hop(add_narrow(far1[2], after(far1_got, placed[2])))
    last1_got = hop(add_narrow(last1[2], last1_got))
    placed = place_rows(far1[3], far1_got, far_pieces(1)[:2], placed)
    last_pieces = [(g, low, start - 2 * size, count) for g, low, start, count in far_pieces(1)[2:]]
    placed = place_rows(last1[3], last1_got, last_pieces, placed)
    kept, sent, grad_local = placed
    got = send(sent, SWAP)
    local = jnp.concatenate([grad_local, early[None, :]], axis=1)
    column_stats = local
    for pairs in (ALONG_Z, ALONG_Z2, ALONG_Z3):
        column_stats = column_stats + send(local, pairs)
    yours_stats = send(column_stats, SWAP)
    summed, clips, new_column = clip_rows(
        column_stats, yours_stats, column_factor[None, :], kept, got
    )
    for along in (ROUND_X, ROUND_Y):
        summed = sum((send(summed, pairs) for pairs in along), summed)
    update, new_row = finish(
        summed, column_stats[:, 2 * HALF :], clips, new_column, row_factor[None, :], kept, got
    )
    return (update, new_row[0], new_column[0])


def solution(mesh):
    in_specs = (P("gy", "gx"), P("gy", "gx"), P("gy", "gx"), P("gy", "gx"), P("gy"), P("gx"))
    out_specs = (P("gy", "gx"), P("gy"), P("gx"))
    return jax.shard_map(
        per_device, mesh=mesh, in_specs=in_specs, out_specs=out_specs, check_vma=False
    )
```

```python
import jax
import jax.numpy as jnp
from jax import lax
from jax.experimental import pallas as pl
from jax.experimental.pallas import tpu as pltpu
from jax.sharding import PartitionSpec as P

D = 6144
FF = 24576
TOK = 1024
FEAT = 384
HALF = 768
NCH = 2

second_decay = 0.8
clip_ratio = 1.0
unit_eps = 1e-06
factor_eps = 1e-30

BOTH = ("gx", "gy")
FLIP = (0, 2, 1, 3)


def moves(dx, dy, dz, other_core):
    pairs = []
    for y in range(4):
        for x in range(4):
            for z in range(4):
                for core in range(2):
                    s = 1 - 2 * core
                    tx, ty, tz = (x + s * dx) % 4, (y + s * dy) % 4, (z + s * dz) % 4
                    tc = 1 - core if other_core else core
                    pairs.append(((y * 4 + x) * 8 + z * 2 + core, (ty * 4 + tx) * 8 + tz * 2 + tc))
    return pairs


ALONG_X = moves(1, 0, 0, False)
ALONG_Y = moves(0, 1, 0, False)
ALONG_Z = moves(0, 0, 1, False)
ALONG_Z2 = moves(0, 0, 2, False)
ALONG_Z3 = moves(0, 0, 3, False)
ROUND_X = [moves(k, 0, 0, False) for k in (1, 2, 3)]
ROUND_Y = [moves(0, k, 0, False) for k in (1, 2, 3)]
SWAP = moves(0, 0, 0, True)


STEPS = (0, -1, 1, 2)
CHEAP = pl.CostEstimate(flops=1024, bytes_accessed=1024, transcendentals=0)


def coordinates():
    gx, gy = lax.axis_index("gx"), lax.axis_index("gy")
    return gx >> 2, gx & 3, gy >> 1, gy & 1


def send(value, pairs):
    return lax.ppermute(value, BOTH, pairs)


def slope_half(preact, upstream, other, waits=()):
    count = 4
    rows = TOK // count

    def kernel(pre_ref, up_ref, *refs):
        out, pre, up, sems = refs[len(waits) :]
        core = coordinates()[3]
        half = 1 - core if other else core
        columns = pl.ds(pl.multiple_of(half * HALF, HALF), HALF)
        for k in range(count):
            at = pl.ds(k * rows, rows)
            pltpu.make_async_copy(pre_ref.at[at, columns], pre.at[at], sems.at[0, k]).start()
            pltpu.make_async_copy(up_ref.at[at, columns], up.at[at], sems.at[1, k]).start()
        for k in range(count):
            at = pl.ds(k * rows, rows)
            pltpu.make_async_copy(pre.at[at], pre.at[at], sems.at[0, k]).wait()
            pltpu.make_async_copy(up.at[at], up.at[at], sems.at[1, k]).wait()

            @pl.loop(0, rows // 16)
            def _(j):
                tile = pl.ds(pl.multiple_of(k * rows + j * 16, 16), 16)
                value = pre[tile].astype(jnp.float32)
                normal_cdf = 0.5 * (1.0 + lax.erf(value * 0.7071067811865476))
                density = jnp.exp(-0.5 * value * value) * 0.3989422804014327
                slope = up[tile].astype(jnp.float32) * (normal_cdf + value * density)
                out[tile] = slope.astype(jnp.bfloat16)

    anywhere = pl.BlockSpec(memory_space=pl.ANY)
    half_block = pltpu.VMEM((TOK, HALF), jnp.bfloat16)
    return pl.pallas_call(
        kernel,
        out_shape=jax.ShapeDtypeStruct((TOK, HALF), jnp.bfloat16),
        in_specs=[pl.BlockSpec(memory_space=pltpu.HBM)] * 2 + [anywhere] * len(waits),
        out_specs=pl.BlockSpec(memory_space=pltpu.VMEM),
        scratch_shapes=[half_block, half_block, pltpu.SemaphoreType.DMA((2, count))],
        compiler_params=pltpu.CompilerParams(vmem_limit_bytes=24 << 20),
        cost_estimate=CHEAP,
    )(preact, upstream, *waits)


def unit_partials(slope_own, slope_other, entries, low, high, waits=()):
    arrays = []
    position = {}
    plan = []
    rows = 0
    for places in entries:
        count = places[0][0][0].shape[-2]
        for i, halves in enumerate(places):
            for h, (array, index) in enumerate(halves):
                if id(array) not in position:
                    position[id(array)] = len(arrays)
                    arrays.append(array)
                plan.append((i, h, rows, count, position[id(array)], index))
        rows += count
    many = high - low

    def kernel(own_ref, other_ref, *refs):
        feature_refs = refs[: len(arrays)]
        outs = refs[len(arrays) + len(waits) : len(arrays) + len(waits) + many]
        held, slopes, feature_sem, slope_sem = refs[len(arrays) + len(waits) + many :]
        pltpu.make_async_copy(own_ref, slopes.at[pl.ds(0, TOK)], slope_sem).start()
        pltpu.make_async_copy(other_ref, slopes.at[pl.ds(TOK, TOK)], slope_sem).start()
        y, _, z, core = coordinates()
        for i in range(4):
            place = ((1 - 2 * core) * (z - y) - STEPS[i] + 3) & 3

            @pl.when((place >= low) & (place < high))
            def _():
                base = pl.multiple_of((place - low) * rows, rows)
                for at, h, start, count, which, index in plan:
                    if at == i:
                        source = feature_refs[which]
                        source = source.at[index] if index is not None else source
                        pltpu.make_async_copy(
                            source,
                            held.at[pl.ds(base + start, count), pl.ds(h * TOK, TOK)],
                            feature_sem,
                        ).start()

        pltpu.make_async_copy(slopes, slopes, slope_sem).wait()
        pltpu.make_async_copy(held, held, feature_sem).wait()

        @pl.loop(0, HALF // 256)
        def _(j):
            columns = pl.ds(pl.multiple_of(j * 256, 256), 256)
            total = jnp.dot(held[...], slopes[:, columns], preferred_element_type=jnp.float32)
            for k, out in enumerate(outs):
                out[:, columns] = total[k * rows : (k + 1) * rows].astype(out.dtype)

    vmem = pl.BlockSpec(memory_space=pltpu.VMEM)
    anywhere = pl.BlockSpec(memory_space=pl.ANY)
    return pl.pallas_call(
        kernel,
        out_shape=tuple(
            jax.ShapeDtypeStruct((rows, HALF), jnp.float32 if k == 3 else jnp.bfloat16)
            for k in range(low, high)
        ),
        in_specs=[anywhere] * (2 + len(arrays) + len(waits)),
        out_specs=(vmem,) * many,
        scratch_shapes=[
            pltpu.VMEM((many * rows, 2 * TOK), jnp.bfloat16),
            pltpu.VMEM((2 * TOK, HALF), jnp.bfloat16),
            pltpu.SemaphoreType.DMA,
            pltpu.SemaphoreType.DMA,
        ],
        compiler_params=pltpu.CompilerParams(vmem_limit_bytes=44 << 20),
        cost_estimate=CHEAP,
    )(slope_own, slope_other, *arrays, *waits)


def add_narrow(a, b):
    return (a.astype(jnp.float32) + b.astype(jnp.float32)).astype(jnp.bfloat16)


def after(value, *before):
    return lax.optimization_barrier((value,) + before)[0]


def turn(inputs):
    def kernel(ref, first, second):
        turned = ref[...].T
        first[...] = turned[: FEAT // 2]
        second[...] = turned[FEAT // 2 :]

    vmem = pl.BlockSpec(memory_space=pltpu.VMEM)
    half = jax.ShapeDtypeStruct((FEAT // 2, TOK), jnp.bfloat16)
    return pl.pallas_call(
        kernel, out_shape=(half, half), in_specs=[vmem], out_specs=(vmem, vmem), cost_estimate=CHEAP
    )(inputs)


def stack_rows(sources, start, count):
    arrays = []
    which = []
    for array, index in sources:
        if not any(array is other for other in arrays):
            arrays.append(array)
        which.append(([array is other for other in arrays].index(True), index))

    def kernel(*refs):
        out = refs[-1]
        for k, (at, index) in enumerate(which):
            source = refs[at] if index is None else refs[at].at[index]
            out[k // 4, k % 4] = source[pl.ds(start, count)]

    vmem = pl.BlockSpec(memory_space=pltpu.VMEM)
    return pl.pallas_call(
        kernel,
        out_shape=jax.ShapeDtypeStruct((2, 4, count, TOK), jnp.bfloat16),
        in_specs=[vmem] * len(arrays),
        out_specs=vmem,
        compiler_params=pltpu.CompilerParams(vmem_limit_bytes=24 << 20),
        cost_estimate=CHEAP,
    )(*arrays)


def place_rows(last, got, pieces, before):
    rows = last.shape[0]

    def kernel(last_ref, got_ref, *refs):
        kept, sent, sums, value, sem = refs[len(before) :]
        total = last_ref[...] + got_ref[...].astype(jnp.float32)
        value[...] = total
        _, x, _, core = coordinates()
        for g, low, start, count in pieces:
            column = (x + (1 - 2 * core) * STEPS[g]) & 3
            row = pl.multiple_of((column & 1) * FEAT + low, 32)
            source = value.at[pl.ds(start, count)]

            @pl.when((column >> 1) == core)
            def _():
                pltpu.make_async_copy(source, kept.at[pl.ds(row, count)], sem).start()

            @pl.when((column >> 1) != core)
            def _():
                pltpu.make_async_copy(source, sent.at[pl.ds(row, count)], sem).start()

        squares = jnp.sum(total * total, axis=0, keepdims=True)
        sums[...] = squares + refs[2][...] if before else squares
        pltpu.make_async_copy(value, value, sem).wait()

    anywhere = pl.BlockSpec(memory_space=pl.ANY)
    vmem = pl.BlockSpec(memory_space=pltpu.VMEM)
    block = jax.ShapeDtypeStruct((HALF, HALF), jnp.float32)
    return pl.pallas_call(
        kernel,
        out_shape=(block, block, jax.ShapeDtypeStruct((1, HALF), jnp.float32)),
        in_specs=[vmem, vmem]
        + ([anywhere, anywhere, vmem] if before else []),
        out_specs=(anywhere, anywhere, vmem),
        scratch_shapes=[pltpu.VMEM((rows, HALF), jnp.float32), pltpu.SemaphoreType.DMA],
        input_output_aliases={2: 0, 3: 1} if before else {},
        compiler_params=pltpu.CompilerParams(vmem_limit_bytes=24 << 20),
        cost_estimate=CHEAP,
    )(last, got, *before)


def clip_rows(mine, yours, column_factor, kept, got):
    def kernel(mine_ref, yours_ref, column_ref, kept_ref, got_ref, payload, clips, news):
        core = coordinates()[3]
        total = weights = None
        squares = None
        both = []
        for stats, grad in ((mine_ref, kept_ref), (yours_ref, got_ref)):
            grad_sq, weight_sq = stats[:, :HALF], stats[:, HALF : 2 * HALF]
            clip = jnp.minimum(
                1.0, clip_ratio * jnp.sqrt(weight_sq) / (jnp.sqrt(grad_sq) + unit_eps)
            )
            column = clip * clip * grad_sq
            both.append((clip, column))
            clipped = grad[...] * clip
            squares = clipped * clipped if squares is None else squares + clipped * clipped
            column_total = jnp.sum(column, axis=1, keepdims=True)
            weight_total = jnp.sum(weight_sq, axis=1, keepdims=True)
            total = column_total if total is None else total + column_total
            weights = weight_total if weights is None else weights + weight_total
        for at in range(2):
            columns = pl.ds(at * HALF, HALF)
            here = core == at
            clips[:, columns] = jnp.where(here, both[0][0], both[1][0])
            sums = jnp.where(here, both[0][1], both[1][1])
            news[:, columns] = second_decay * column_ref[:, columns] + (1.0 - second_decay) * (
                sums / D + factor_eps
            )
        row_sums = lax.dot_general(
            jnp.ones((8, HALF), jnp.float32),
            squares,
            (((1,), (1,)), ((), ())),
            precision=lax.Precision.HIGHEST,
            preferred_element_type=jnp.float32,
        )
        payload[:, :HALF] = row_sums[:1]
        payload[:, HALF : HALF + 128] = jnp.broadcast_to(total, (1, 128))
        payload[:, HALF + 128 :] = jnp.broadcast_to(weights, (1, 128))

    vmem = pl.BlockSpec(memory_space=pltpu.VMEM)
    columns = jax.ShapeDtypeStruct((1, 2 * HALF), jnp.float32)
    return pl.pallas_call(
        kernel,
        out_shape=(jax.ShapeDtypeStruct((1, HALF + 256), jnp.float32), columns, columns),
        in_specs=[vmem] * 5,
        out_specs=(vmem,) * 3,
        compiler_params=pltpu.CompilerParams(vmem_limit_bytes=32 << 20),
        cost_estimate=CHEAP,
    )(mine, yours, column_factor, kept, got)


def finish(summed, row_total, clips, new_column, row_factor, kept, got):
    step = 128

    def kernel(
        summed_ref, row_total_ref, clip_ref, column_ref, row_ref, kept_ref, got_ref,
        update, new_row_ref,
    ):
        core = coordinates()[3]
        at = pl.ds(pl.multiple_of(pl.program_id(0) * step, step), step)
        clipped_total = summed_ref[:, HALF : HALF + 1]
        weight_total = summed_ref[:, HALF + 128 : HALF + 129]
        row_mean = (
            second_decay * row_total_ref[:, :1]
            + (1.0 - second_decay) * (clipped_total / FF + D * factor_eps)
        ) / D
        weight_rms = jnp.sqrt(weight_total / (D * FF))
        row_sums = summed_ref[:, at]
        new_row = second_decay * row_ref[:, at] + (1.0 - second_decay) * (
            row_sums / FF + factor_eps
        )
        new_row_ref[:, at] = new_row
        down = jnp.broadcast_to(lax.rsqrt(new_row), (step, step)).T[:, :1]
        across = -weight_rms * clip_ref[...] * (jnp.sqrt(row_mean) * lax.rsqrt(column_ref[...]))
        first = jnp.where(core == 0, kept_ref[...], got_ref[...])
        second = jnp.where(core == 0, got_ref[...], kept_ref[...])
        update[:, :HALF] = first * across[:, :HALF] * down
        update[:, HALF:] = second * across[:, HALF:] * down

    whole = lambda *shape: pl.BlockSpec(shape, lambda i: (0, 0))
    rows = lambda width: pl.BlockSpec((step, width), lambda i: (i, 0))
    return pl.pallas_call(
        kernel,
        grid=(HALF // step,),
        out_shape=(
            jax.ShapeDtypeStruct((HALF, 2 * HALF), jnp.float32),
            jax.ShapeDtypeStruct((1, HALF), jnp.float32),
        ),
        in_specs=[
            whole(1, HALF + 256), whole(1, 128), whole(1, 2 * HALF), whole(1, 2 * HALF),
            whole(1, HALF), rows(HALF), rows(HALF),
        ],
        out_specs=(rows(2 * HALF), whole(1, HALF)),
        compiler_params=pltpu.CompilerParams(vmem_limit_bytes=32 << 20),
        cost_estimate=CHEAP,
    )(summed, row_total, clips, new_column, row_factor, kept, got)


def per_device(inputs, preact, upstream, weight, row_factor, column_factor):
    core = coordinates()[3]

    p, q = turn(inputs)
    size = FEAT // 2 // NCH

    p_swap, q_swap = send(p, SWAP), send(q, SWAP)
    ya, xa = send(p, ALONG_Y), send(q, ALONG_X)
    yb, xb = send(p_swap, ALONG_Y), send(q_swap, ALONG_X)
    slope_yours = slope_half(preact, upstream, True, (p_swap, q_swap))
    slope_other = send(slope_yours, SWAP)
    slope_mine = slope_half(preact, upstream, False, (p_swap, q_swap))
    ya, xa, yb, xb = lax.optimization_barrier((ya, xa, yb, xb, slope_yours, slope_mine))[:4]
    y2, x2 = send(ya, ALONG_Y), send(xa, ALONG_X)
    ya_swap, xa_swap = send(ya, SWAP), send(xa, SWAP)
    yb, xb = lax.optimization_barrier((yb, xb, ya_swap, xa_swap))[:2]
    yb_swap, xb_swap = send(yb, SWAP), send(xb, SWAP)
    y2, x2 = lax.optimization_barrier((y2, x2, yb_swap, xb_swap))[:2]
    y2_swap, x2_swap = send(y2, SWAP), send(x2, SWAP)
    p_places = [(p, None), (ya, None), (yb_swap, None), (y2, None)]
    p_places += [(p_swap, None), (yb, None), (ya_swap, None), (y2_swap, None)]
    q_places = [(q, None), (xa, None), (xb_swap, None), (x2, None)]
    q_places += [(q_swap, None), (xb, None), (xa_swap, None), (x2_swap, None)]

    def units(entries, low=0, high=4, waits=()):
        return unit_partials(slope_mine, slope_other, entries, low, high, waits)

    def hop(value):
        return send(value, ALONG_Z)

    def near_entries(x1, x1_swap):
        return [
            [((x1, (0, i)), (x1, (1, i))) for i in range(4)],
            [((x1_swap, (1, FLIP[i])), (x1_swap, (0, FLIP[i]))) for i in range(4)],
        ]

    def far_entries(q_here, y1, y1_swap, x2, x2_swap, y2, y2_swap):
        entries = [[((x2, i), (x2_swap, FLIP[i])) for i in range(4)]]
        for g in range(4):
            entries.append(
                [
                    ((q_here, (0, g)), (q_here, (1, g))),
                    ((y1, (0, g)), (y1, (1, g))),
                    ((y1_swap, (1, FLIP[g])), (y1_swap, (0, FLIP[g]))),
                    ((y2, g), (y2_swap, FLIP[g])),
                ]
            )
        return entries

    p_here = stack_rows(p_places, 0, size)
    q_here = stack_rows(q_places, 0, size)
    x1, y1 = send(p_here, ALONG_X), send(q_here, ALONG_Y)
    own = units([[(p_places[i], p_places[4 + i]) for i in range(4)]], waits=(p_here, q_here))
    own_got = hop(own[0])
    weight = after(weight, own[0])
    weight_local = jnp.sum(weight * weight, axis=0)
    row_local = jnp.broadcast_to(jnp.sum(row_factor)[None], (128,))
    weight_mine = lax.dynamic_slice_in_dim(weight_local, core * HALF, HALF)
    weight_yours = lax.dynamic_slice_in_dim(weight_local, (1 - core) * HALF, HALF)
    early = jnp.concatenate([weight_mine, row_local])
    early = early + send(jnp.concatenate([weight_yours, row_local]), SWAP)
    p_next = stack_rows(p_places, size, size)
    q_next = stack_rows(q_places, size, size)
    own_2 = add_narrow(own[1], own_got)
    own_got = hop(own_2)
    own_3 = add_narrow(own[2], own_got)
    x1, y1 = lax.optimization_barrier((x1, y1, own_3, p_next, q_next, early))[:2]
    x2, y2 = send(x1[0], ALONG_X), send(y1[0], ALONG_Y)
    x1_swap, y1_swap = send(x1, SWAP), send(y1, SWAP)

    p_next, q_next = lax.optimization_barrier((p_next, q_next, x1_swap, y1_swap))[:2]
    x1_next, y1_next = send(p_next, ALONG_X), send(q_next, ALONG_Y)
    near0 = units(near_entries(x1, x1_swap), waits=(y1_swap,))
    near0_got = hop(near0[0])
    x2, y2 = lax.optimization_barrier((x2, y2, near0[0]))[:2]
    x2_swap, y2_swap = send(x2, SWAP), send(y2, SWAP)
    far0_entries = far_entries(q_here, y1, y1_swap, x2, x2_swap, y2, y2_swap)
    near0_2 = add_narrow(near0[1], near0_got)
    near0_got = hop(near0_2)
    far0 = units(far0_entries, 0, 2, waits=(near0_2,))
    far0_got = hop(far0[0])
    near0_3 = add_narrow(near0[2], after(near0_got, far0[0]))
    x1, y1 = lax.optimization_barrier((x1_next, y1_next, far0[0], near0_3))[:2]
    x2, y2 = send(x1[0], ALONG_X), send(y1[0], ALONG_Y)
    x1_swap, y1_swap = send(x1, SWAP), send(y1, SWAP)
    near0_got = hop(after(near0_3, x1_swap, y1_swap))
    own_got = hop(after(own_3, x1_swap, y1_swap))
    far0 += units(far0_entries, 2, 4)
    near_pieces = lambda chunk: [(1, chunk * size, 0, size), (2, chunk * size, size, size)]
    far_pieces = lambda chunk: [(3, chunk * size, 0, size)] + [
        (g, FEAT // 2 + chunk * size, (g + 1) * size, size) for g in range(4)
    ]
    near1 = units(near_entries(x1, x1_swap), waits=(far0[2], y1_swap))
    near1_got = hop(near1[0])
    far0_2 = add_narrow(far0[1], after(far0_got, near1[0]))
    far0_got = hop(far0_2)
    placed = place_rows(own[3], after(own_got, near1[0]), [(0, 0, 0, FEAT // 2)], ())
    placed = place_rows(near0[3], after(near0_got, near1[0]), near_pieces(0), placed)
    x2, y2 = lax.optimization_barrier((x2, y2, near1[0], far0_2, placed[2]))[:2]
    x2_swap, y2_swap = send(x2, SWAP), send(y2, SWAP)
    far1_entries = far_entries(q_next, y1, y1_swap, x2, x2_swap, y2, y2_swap)
    far1 = units(far1_entries[:2])
    far1_got = hop(far1[0])
    near1_2 = add_narrow(near1[1], after(near1_got, far1[0]))
    near1_got = hop(near1_2)
    far0_3 = add_narrow(far0[2], after(far0_got, far1[0]))
    far0_got = hop(far0_3)
    last1 = units(far1_entries[2:], waits=(near1_2, far0_3))
    last1_got = hop(last1[0])
    near1_3 = add_narrow(near1[2], after(near1_got, last1[0]))
    far1_2 = add_narrow(far1[1], after(far1_got, last1[0]))
    far1_got = hop(far1_2)
    near1_got = hop(near1_3)
    placed = place_rows(far0[3], after(far0_got, far1_2), far_pieces(0), placed)
    last1_2 = add_narrow(last1[1], after(last1_got, placed[2]))
    last1_got = hop(last1_2)
    placed = place_rows(near1[3], after(near1_got, last1_2), near_pieces(1), placed)
    far1_got = hop(add_narrow(far1[2], after(far1_got, placed[2])))
    last1_got = hop(add_narrow(last1[2], last1_got))
    placed = place_rows(far1[3], far1_got, far_pieces(1)[:2], placed)
    last_pieces = [(g, low, start - 2 * size, count) for g, low, start, count in far_pieces(1)[2:]]
    placed = place_rows(last1[3], last1_got, last_pieces, placed)
    kept, sent, grad_local = placed
    got = send(sent, SWAP)
    local = jnp.concatenate([grad_local, early[None, :]], axis=1)
    column_stats = local
    for pairs in (ALONG_Z, ALONG_Z2, ALONG_Z3):
        column_stats = column_stats + send(local, pairs)
    yours_stats = send(column_stats, SWAP)
    summed, clips, new_column = clip_rows(
        column_stats, yours_stats, column_factor[None, :], kept, got
    )
    for along in (ROUND_X, ROUND_Y):
        summed = sum((send(summed, pairs) for pairs in along), summed)
    update, new_row = finish(
        summed, column_stats[:, 2 * HALF :], clips, new_column, row_factor[None, :], kept, got
    )
    return (update, new_row[0], new_column[0])


def solution(mesh):
    in_specs = (P("gy", "gx"), P("gy", "gx"), P("gy", "gx"), P("gy", "gx"), P("gy"), P("gx"))
    out_specs = (P("gy", "gx"), P("gy"), P("gx"))
    return jax.shard_map(
        per_device, mesh=mesh, in_specs=in_specs, out_specs=out_specs, check_vma=False
    )
```

```python
import jax
import jax.numpy as jnp
from jax import lax
from jax.experimental import pallas as pl
from jax.experimental.pallas import tpu as pltpu
from jax.sharding import PartitionSpec as P

D = 6144
FF = 24576
TOK = 1024
FEAT = 384
HALF = 768
NCH = 2

second_decay = 0.8
clip_ratio = 1.0
unit_eps = 1e-06
factor_eps = 1e-30

BOTH = ("gx", "gy")
FLIP = (0, 2, 1, 3)


def moves(dx, dy, dz, other_core):
    pairs = []
    for y in range(4):
        for x in range(4):
            for z in range(4):
                for core in range(2):
                    s = 1 - 2 * core
                    tx, ty, tz = (x + s * dx) % 4, (y + s * dy) % 4, (z + s * dz) % 4
                    tc = 1 - core if other_core else core
                    pairs.append(((y * 4 + x) * 8 + z * 2 + core, (ty * 4 + tx) * 8 + tz * 2 + tc))
    return pairs


ALONG_X = moves(1, 0, 0, False)
ALONG_Y = moves(0, 1, 0, False)
ALONG_Z = moves(0, 0, 1, False)
ALONG_Z2 = moves(0, 0, 2, False)
ALONG_Z3 = moves(0, 0, 3, False)
ROUND_X = [moves(k, 0, 0, False) for k in (1, 2, 3)]
ROUND_Y = [moves(0, k, 0, False) for k in (1, 2, 3)]
SWAP = moves(0, 0, 0, True)


STEPS = (0, -1, 1, 2)
CHEAP = pl.CostEstimate(flops=1024, bytes_accessed=1024, transcendentals=0)


def coordinates():
    gx, gy = lax.axis_index("gx"), lax.axis_index("gy")
    return gx >> 2, gx & 3, gy >> 1, gy & 1


def send(value, pairs):
    return lax.ppermute(value, BOTH, pairs)


def slope_half(preact, upstream, other, waits=()):
    count = 4
    rows = TOK // count

    def kernel(pre_ref, up_ref, *refs):
        out, pre, up, sems = refs[len(waits) :]
        core = coordinates()[3]
        half = 1 - core if other else core
        columns = pl.ds(pl.multiple_of(half * HALF, HALF), HALF)
        for k in range(count):
            at = pl.ds(k * rows, rows)
            pltpu.make_async_copy(pre_ref.at[at, columns], pre.at[at], sems.at[0, k]).start()
            pltpu.make_async_copy(up_ref.at[at, columns], up.at[at], sems.at[1, k]).start()
        for k in range(count):
            at = pl.ds(k * rows, rows)
            pltpu.make_async_copy(pre.at[at], pre.at[at], sems.at[0, k]).wait()
            pltpu.make_async_copy(up.at[at], up.at[at], sems.at[1, k]).wait()

            @pl.loop(0, rows // 16)
            def _(j):
                tile = pl.ds(pl.multiple_of(k * rows + j * 16, 16), 16)
                value = pre[tile].astype(jnp.float32)
                normal_cdf = 0.5 * (1.0 + lax.erf(value * 0.7071067811865476))
                density = jnp.exp(-0.5 * value * value) * 0.3989422804014327
                slope = up[tile].astype(jnp.float32) * (normal_cdf + value * density)
                out[tile] = slope.astype(jnp.bfloat16)

    anywhere = pl.BlockSpec(memory_space=pl.ANY)
    half_block = pltpu.VMEM((TOK, HALF), jnp.bfloat16)
    return pl.pallas_call(
        kernel,
        out_shape=jax.ShapeDtypeStruct((TOK, HALF), jnp.bfloat16),
        in_specs=[pl.BlockSpec(memory_space=pltpu.HBM)] * 2 + [anywhere] * len(waits),
        out_specs=pl.BlockSpec(memory_space=pltpu.VMEM),
        scratch_shapes=[half_block, half_block, pltpu.SemaphoreType.DMA((2, count))],
        compiler_params=pltpu.CompilerParams(vmem_limit_bytes=24 << 20),
        cost_estimate=CHEAP,
    )(preact, upstream, *waits)


def unit_partials(slope_own, slope_other, entries, low, high, waits=()):
    arrays = []
    position = {}
    plan = []
    rows = 0
    for places in entries:
        count = places[0][0][0].shape[-2]
        for i, halves in enumerate(places):
            for h, (array, index) in enumerate(halves):
                if id(array) not in position:
                    position[id(array)] = len(arrays)
                    arrays.append(array)
                plan.append((i, h, rows, count, position[id(array)], index))
        rows += count
    many = high - low

    def kernel(own_ref, other_ref, *refs):
        feature_refs = refs[: len(arrays)]
        outs = refs[len(arrays) + len(waits) : len(arrays) + len(waits) + many]
        held, slopes, feature_sem, slope_sem = refs[len(arrays) + len(waits) + many :]
        pltpu.make_async_copy(own_ref, slopes.at[pl.ds(0, TOK)], slope_sem).start()
        pltpu.make_async_copy(other_ref, slopes.at[pl.ds(TOK, TOK)], slope_sem).start()
        y, _, z, core = coordinates()
        for i in range(4):
            place = ((1 - 2 * core) * (z - y) - STEPS[i] + 3) & 3

            @pl.when((place >= low) & (place < high))
            def _():
                base = pl.multiple_of((place - low) * rows, rows)
                for at, h, start, count, which, index in plan:
                    if at == i:
                        source = feature_refs[which]
                        source = source.at[index] if index is not None else source
                        pltpu.make_async_copy(
                            source,
                            held.at[pl.ds(base + start, count), pl.ds(h * TOK, TOK)],
                            feature_sem,
                        ).start()

        pltpu.make_async_copy(slopes, slopes, slope_sem).wait()
        pltpu.make_async_copy(held, held, feature_sem).wait()

        @pl.loop(0, HALF // 256)
        def _(j):
            columns = pl.ds(pl.multiple_of(j * 256, 256), 256)
            total = jnp.dot(held[...], slopes[:, columns], preferred_element_type=jnp.float32)
            for k, out in enumerate(outs):
                out[:, columns] = total[k * rows : (k + 1) * rows].astype(out.dtype)

    vmem = pl.BlockSpec(memory_space=pltpu.VMEM)
    anywhere = pl.BlockSpec(memory_space=pl.ANY)
    return pl.pallas_call(
        kernel,
        out_shape=tuple(
            jax.ShapeDtypeStruct((rows, HALF), jnp.float32 if k == 3 else jnp.bfloat16)
            for k in range(low, high)
        ),
        in_specs=[anywhere] * (2 + len(arrays) + len(waits)),
        out_specs=(vmem,) * many,
        scratch_shapes=[
            pltpu.VMEM((many * rows, 2 * TOK), jnp.bfloat16),
            pltpu.VMEM((2 * TOK, HALF), jnp.bfloat16),
            pltpu.SemaphoreType.DMA,
            pltpu.SemaphoreType.DMA,
        ],
        compiler_params=pltpu.CompilerParams(vmem_limit_bytes=44 << 20),
        cost_estimate=CHEAP,
    )(slope_own, slope_other, *arrays, *waits)


def add_narrow(a, b):
    return (a.astype(jnp.float32) + b.astype(jnp.float32)).astype(jnp.bfloat16)


def after(value, *before):
    return lax.optimization_barrier((value,) + before)[0]


def turn(inputs):
    def kernel(ref, first, second):
        turned = ref[...].T
        first[...] = turned[: FEAT // 2]
        second[...] = turned[FEAT // 2 :]

    vmem = pl.BlockSpec(memory_space=pltpu.VMEM)
    half = jax.ShapeDtypeStruct((FEAT // 2, TOK), jnp.bfloat16)
    return pl.pallas_call(
        kernel, out_shape=(half, half), in_specs=[vmem], out_specs=(vmem, vmem), cost_estimate=CHEAP
    )(inputs)


def stack_rows(sources, start, count):
    arrays = []
    which = []
    for array, index in sources:
        if not any(array is other for other in arrays):
            arrays.append(array)
        which.append(([array is other for other in arrays].index(True), index))

    def kernel(*refs):
        out = refs[-1]
        for k, (at, index) in enumerate(which):
            source = refs[at] if index is None else refs[at].at[index]
            out[k // 4, k % 4] = source[pl.ds(start, count)]

    vmem = pl.BlockSpec(memory_space=pltpu.VMEM)
    return pl.pallas_call(
        kernel,
        out_shape=jax.ShapeDtypeStruct((2, 4, count, TOK), jnp.bfloat16),
        in_specs=[vmem] * len(arrays),
        out_specs=vmem,
        compiler_params=pltpu.CompilerParams(vmem_limit_bytes=24 << 20),
        cost_estimate=CHEAP,
    )(*arrays)


def place_rows(last, got, pieces, before):
    rows = last.shape[0]

    def kernel(last_ref, got_ref, *refs):
        kept, sent, sums, value, sem = refs[len(before) :]
        total = last_ref[...] + got_ref[...].astype(jnp.float32)
        value[...] = total
        _, x, _, core = coordinates()
        for g, low, start, count in pieces:
            column = (x + (1 - 2 * core) * STEPS[g]) & 3
            row = pl.multiple_of((column & 1) * FEAT + low, 32)
            source = value.at[pl.ds(start, count)]

            @pl.when((column >> 1) == core)
            def _():
                pltpu.make_async_copy(source, kept.at[pl.ds(row, count)], sem).start()

            @pl.when((column >> 1) != core)
            def _():
                pltpu.make_async_copy(source, sent.at[pl.ds(row, count)], sem).start()

        squares = jnp.sum(total * total, axis=0, keepdims=True)
        sums[...] = squares + refs[2][...] if before else squares
        pltpu.make_async_copy(value, value, sem).wait()

    anywhere = pl.BlockSpec(memory_space=pl.ANY)
    vmem = pl.BlockSpec(memory_space=pltpu.VMEM)
    block = jax.ShapeDtypeStruct((HALF, HALF), jnp.float32)
    return pl.pallas_call(
        kernel,
        out_shape=(block, block, jax.ShapeDtypeStruct((1, HALF), jnp.float32)),
        in_specs=[vmem, vmem]
        + ([anywhere, anywhere, vmem] if before else []),
        out_specs=(anywhere, anywhere, vmem),
        scratch_shapes=[pltpu.VMEM((rows, HALF), jnp.float32), pltpu.SemaphoreType.DMA],
        input_output_aliases={2: 0, 3: 1} if before else {},
        compiler_params=pltpu.CompilerParams(vmem_limit_bytes=24 << 20),
        cost_estimate=CHEAP,
    )(last, got, *before)


def clip_rows(mine, yours, column_factor, kept, got):
    def kernel(mine_ref, yours_ref, column_ref, kept_ref, got_ref, payload, clips, news):
        core = coordinates()[3]
        total = weights = None
        squares = None
        both = []
        for stats, grad in ((mine_ref, kept_ref), (yours_ref, got_ref)):
            grad_sq, weight_sq = stats[:, :HALF], stats[:, HALF : 2 * HALF]
            clip = jnp.minimum(
                1.0, clip_ratio * jnp.sqrt(weight_sq) / (jnp.sqrt(grad_sq) + unit_eps)
            )
            column = clip * clip * grad_sq
            both.append((clip, column))
            clipped = grad[...] * clip
            squares = clipped * clipped if squares is None else squares + clipped * clipped
            column_total = jnp.sum(column, axis=1, keepdims=True)
            weight_total = jnp.sum(weight_sq, axis=1, keepdims=True)
            total = column_total if total is None else total + column_total
            weights = weight_total if weights is None else weights + weight_total
        for at in range(2):
            columns = pl.ds(at * HALF, HALF)
            here = core == at
            clips[:, columns] = jnp.where(here, both[0][0], both[1][0])
            sums = jnp.where(here, both[0][1], both[1][1])
            news[:, columns] = second_decay * column_ref[:, columns] + (1.0 - second_decay) * (
                sums / D + factor_eps
            )
        row_sums = lax.dot_general(
            jnp.ones((8, HALF), jnp.float32),
            squares,
            (((1,), (1,)), ((), ())),
            precision=lax.Precision.HIGHEST,
            preferred_element_type=jnp.float32,
        )
        payload[:, :HALF] = row_sums[:1]
        payload[:, HALF : HALF + 128] = jnp.broadcast_to(total, (1, 128))
        payload[:, HALF + 128 :] = jnp.broadcast_to(weights, (1, 128))

    vmem = pl.BlockSpec(memory_space=pltpu.VMEM)
    columns = jax.ShapeDtypeStruct((1, 2 * HALF), jnp.float32)
    return pl.pallas_call(
        kernel,
        out_shape=(jax.ShapeDtypeStruct((1, HALF + 256), jnp.float32), columns, columns),
        in_specs=[vmem] * 5,
        out_specs=(vmem,) * 3,
        compiler_params=pltpu.CompilerParams(vmem_limit_bytes=32 << 20),
        cost_estimate=CHEAP,
    )(mine, yours, column_factor, kept, got)


def finish(summed, row_total, clips, new_column, row_factor, kept, got):
    step = 128

    def kernel(
        summed_ref, row_total_ref, clip_ref, column_ref, row_ref, kept_ref, got_ref,
        update, new_row_ref,
    ):
        core = coordinates()[3]
        at = pl.ds(pl.multiple_of(pl.program_id(0) * step, step), step)
        clipped_total = summed_ref[:, HALF : HALF + 1]
        weight_total = summed_ref[:, HALF + 128 : HALF + 129]
        row_mean = (
            second_decay * row_total_ref[:, :1]
            + (1.0 - second_decay) * (clipped_total / FF + D * factor_eps)
        ) / D
        weight_rms = jnp.sqrt(weight_total / (D * FF))
        row_sums = summed_ref[:, at]
        new_row = second_decay * row_ref[:, at] + (1.0 - second_decay) * (
            row_sums / FF + factor_eps
        )
        new_row_ref[:, at] = new_row
        down = jnp.broadcast_to(lax.rsqrt(new_row), (step, step)).T[:, :1]
        across = -weight_rms * clip_ref[...] * (jnp.sqrt(row_mean) * lax.rsqrt(column_ref[...]))
        first = jnp.where(core == 0, kept_ref[...], got_ref[...])
        second = jnp.where(core == 0, got_ref[...], kept_ref[...])
        update[:, :HALF] = first * across[:, :HALF] * down
        update[:, HALF:] = second * across[:, HALF:] * down

    whole = lambda *shape: pl.BlockSpec(shape, lambda i: (0, 0))
    rows = lambda width: pl.BlockSpec((step, width), lambda i: (i, 0))
    return pl.pallas_call(
        kernel,
        grid=(HALF // step,),
        out_shape=(
            jax.ShapeDtypeStruct((HALF, 2 * HALF), jnp.float32),
            jax.ShapeDtypeStruct((1, HALF), jnp.float32),
        ),
        in_specs=[
            whole(1, HALF + 256), whole(1, 128), whole(1, 2 * HALF), whole(1, 2 * HALF),
            whole(1, HALF), rows(HALF), rows(HALF),
        ],
        out_specs=(rows(2 * HALF), whole(1, HALF)),
        compiler_params=pltpu.CompilerParams(vmem_limit_bytes=32 << 20),
        cost_estimate=CHEAP,
    )(summed, row_total, clips, new_column, row_factor, kept, got)


def per_device(inputs, preact, upstream, weight, row_factor, column_factor):
    core = coordinates()[3]

    p, q = turn(inputs)
    size = FEAT // 2 // NCH

    p_swap, q_swap = send(p, SWAP), send(q, SWAP)
    ya, xa = send(p, ALONG_Y), send(q, ALONG_X)
    yb, xb = send(p_swap, ALONG_Y), send(q_swap, ALONG_X)
    slope_yours = slope_half(preact, upstream, True, (p_swap, q_swap))
    slope_other = send(slope_yours, SWAP)
    slope_mine = slope_half(preact, upstream, False, (p_swap, q_swap))
    ya, xa, yb, xb = lax.optimization_barrier((ya, xa, yb, xb, slope_yours, slope_mine))[:4]
    y2, x2 = send(ya, ALONG_Y), send(xa, ALONG_X)
    ya_swap, xa_swap = send(ya, SWAP), send(xa, SWAP)
    yb, xb = lax.optimization_barrier((yb, xb, ya_swap, xa_swap))[:2]
    yb_swap, xb_swap = send(yb, SWAP), send(xb, SWAP)
    y2, x2 = lax.optimization_barrier((y2, x2, yb_swap, xb_swap))[:2]
    y2_swap, x2_swap = send(y2, SWAP), send(x2, SWAP)
    p_places = [(p, None), (ya, None), (yb_swap, None), (y2, None)]
    p_places += [(p_swap, None), (yb, None), (ya_swap, None), (y2_swap, None)]
    q_places = [(q, None), (xa, None), (xb_swap, None), (x2, None)]
    q_places += [(q_swap, None), (xb, None), (xa_swap, None), (x2_swap, None)]

    def units(entries, low=0, high=4, waits=()):
        return unit_partials(slope_mine, slope_other, entries, low, high, waits)

    def hop(value):
        return send(value, ALONG_Z)

    def near_entries(x1, x1_swap):
        return [
            [((x1, (0, i)), (x1, (1, i))) for i in range(4)],
            [((x1_swap, (1, FLIP[i])), (x1_swap, (0, FLIP[i]))) for i in range(4)],
        ]

    def far_entries(q_here, y1, y1_swap, x2, x2_swap, y2, y2_swap):
        entries = [[((x2, i), (x2_swap, FLIP[i])) for i in range(4)]]
        for g in range(4):
            entries.append(
                [
                    ((q_here, (0, g)), (q_here, (1, g))),
                    ((y1, (0, g)), (y1, (1, g))),
                    ((y1_swap, (1, FLIP[g])), (y1_swap, (0, FLIP[g]))),
                    ((y2, g), (y2_swap, FLIP[g])),
                ]
            )
        return entries

    p_here = stack_rows(p_places, 0, size)
    q_here = stack_rows(q_places, 0, size)
    x1, y1 = send(p_here, ALONG_X), send(q_here, ALONG_Y)
    own = units([[(p_places[i], p_places[4 + i]) for i in range(4)]], waits=(p_here, q_here))
    own_got = hop(own[0])
    weight = after(weight, own[0])
    weight_local = jnp.sum(weight * weight, axis=0)
    row_local = jnp.broadcast_to(jnp.sum(row_factor)[None], (128,))
    weight_mine = lax.dynamic_slice_in_dim(weight_local, core * HALF, HALF)
    weight_yours = lax.dynamic_slice_in_dim(weight_local, (1 - core) * HALF, HALF)
    early = jnp.concatenate([weight_mine, row_local])
    early = early + send(jnp.concatenate([weight_yours, row_local]), SWAP)
    p_next = stack_rows(p_places, size, size)
    q_next = stack_rows(q_places, size, size)
    own_2 = add_narrow(own[1], own_got)
    own_got = hop(own_2)
    own_3 = add_narrow(own[2], own_got)
    x1, y1 = lax.optimization_barrier((x1, y1, own_3, p_next, q_next, early))[:2]
    x2, y2 = send(x1[0], ALONG_X), send(y1[0], ALONG_Y)
    x1_swap, y1_swap = send(x1, SWAP), send(y1, SWAP)

    p_next, q_next = lax.optimization_barrier((p_next, q_next, x1_swap, y1_swap))[:2]
    x1_next, y1_next = send(p_next, ALONG_X), send(q_next, ALONG_Y)
    near0 = units(near_entries(x1, x1_swap), waits=(y1_swap,))
    near0_got = hop(near0[0])
    x2, y2 = lax.optimization_barrier((x2, y2, near0[0]))[:2]
    x2_swap, y2_swap = send(x2, SWAP), send(y2, SWAP)
    far0_entries = far_entries(q_here, y1, y1_swap, x2, x2_swap, y2, y2_swap)
    near0_2 = add_narrow(near0[1], near0_got)
    near0_got = hop(near0_2)
    far0 = units(far0_entries, 0, 2, waits=(near0_2,))
    far0_got = hop(far0[0])
    near0_3 = add_narrow(near0[2], after(near0_got, far0[0]))
    x1, y1 = lax.optimization_barrier((x1_next, y1_next, far0[0], near0_3))[:2]
    far0_2 = add_narrow(far0[1], far0_got)
    x2, y2 = lax.optimization_barrier((x1[0], y1[0], far0_2))[:2]
    x2, y2 = send(x2, ALONG_X), send(y2, ALONG_Y)
    far0_got = hop(far0_2)
    x1_swap, y1_swap = send(x1, SWAP), send(y1, SWAP)
    near0_got = hop(after(near0_3, x1_swap, y1_swap))
    own_got = hop(after(own_3, x1_swap, y1_swap))
    far0 += units(far0_entries, 2, 4)
    near_pieces = lambda chunk: [(1, chunk * size, 0, size), (2, chunk * size, size, size)]
    far_pieces = lambda chunk: [(3, chunk * size, 0, size)] + [
        (g, FEAT // 2 + chunk * size, (g + 1) * size, size) for g in range(4)
    ]
    near1 = units(near_entries(x1, x1_swap), waits=(far0[2], y1_swap))
    near1_got = hop(near1[0])
    placed = place_rows(own[3], after(own_got, near1[0]), [(0, 0, 0, FEAT // 2)], ())
    placed = place_rows(near0[3], after(near0_got, near1[0]), near_pieces(0), placed)
    x2, y2 = lax.optimization_barrier((x2, y2, near1[0], placed[2]))[:2]
    x2_swap, y2_swap = send(x2, SWAP), send(y2, SWAP)
    far1_entries = far_entries(q_next, y1, y1_swap, x2, x2_swap, y2, y2_swap)
    far0_3 = add_narrow(far0[2], after(far0_got, near1[0]))
    far0_got = hop(far0_3)
    far1 = units(far1_entries[:2], waits=(far0_3,))
    far1_got = hop(far1[0])
    near1_2 = add_narrow(near1[1], after(near1_got, far1[0]))
    near1_got = hop(near1_2)
    last1 = units(far1_entries[2:], waits=(near1_2,))
    last1_got = hop(last1[0])
    near1_3 = add_narrow(near1[2], after(near1_got, last1[0]))
    far1_2 = add_narrow(far1[1], after(far1_got, last1[0]))
    far1_got = hop(far1_2)
    near1_got = hop(near1_3)
    placed = place_rows(far0[3], after(far0_got, far1_2), far_pieces(0), placed)
    last1_2 = add_narrow(last1[1], after(last1_got, placed[2]))
    last1_got = hop(last1_2)
    placed = place_rows(near1[3], after(near1_got, last1_2), near_pieces(1), placed)
    far1_got = hop(add_narrow(far1[2], after(far1_got, placed[2])))
    last1_got = hop(add_narrow(last1[2], last1_got))
    placed = place_rows(far1[3], far1_got, far_pieces(1)[:2], placed)
    last_pieces = [(g, low, start - 2 * size, count) for g, low, start, count in far_pieces(1)[2:]]
    placed = place_rows(last1[3], last1_got, last_pieces, placed)
    kept, sent, grad_local = placed
    got = send(sent, SWAP)
    local = jnp.concatenate([grad_local, early[None, :]], axis=1)
    column_stats = local
    for pairs in (ALONG_Z, ALONG_Z2, ALONG_Z3):
        column_stats = column_stats + send(local, pairs)
    yours_stats = send(column_stats, SWAP)
    summed, clips, new_column = clip_rows(
        column_stats, yours_stats, column_factor[None, :], kept, got
    )
    for along in (ROUND_X, ROUND_Y):
        summed = sum((send(summed, pairs) for pairs in along), summed)
    update, new_row = finish(
        summed, column_stats[:, 2 * HALF :], clips, new_column, row_factor[None, :], kept, got
    )
    return (update, new_row[0], new_column[0])


def solution(mesh):
    in_specs = (P("gy", "gx"), P("gy", "gx"), P("gy", "gx"), P("gy", "gx"), P("gy"), P("gx"))
    out_specs = (P("gy", "gx"), P("gy"), P("gx"))
    return jax.shard_map(
        per_device, mesh=mesh, in_specs=in_specs, out_specs=out_specs, check_vma=False
    )
```

```python
import jax
import jax.numpy as jnp
from jax import lax
from jax.experimental import pallas as pl
from jax.experimental.pallas import tpu as pltpu
from jax.sharding import PartitionSpec as P

D = 6144
FF = 24576
TOK = 1024
FEAT = 384
HALF = 768
NCH = 2

second_decay = 0.8
clip_ratio = 1.0
unit_eps = 1e-06
factor_eps = 1e-30

BOTH = ("gx", "gy")
FLIP = (0, 2, 1, 3)


def moves(dx, dy, dz, other_core):
    pairs = []
    for y in range(4):
        for x in range(4):
            for z in range(4):
                for core in range(2):
                    s = 1 - 2 * core
                    tx, ty, tz = (x + s * dx) % 4, (y + s * dy) % 4, (z + s * dz) % 4
                    tc = 1 - core if other_core else core
                    pairs.append(((y * 4 + x) * 8 + z * 2 + core, (ty * 4 + tx) * 8 + tz * 2 + tc))
    return pairs


ALONG_X = moves(1, 0, 0, False)
ALONG_Y = moves(0, 1, 0, False)
ALONG_Z = moves(0, 0, 1, False)
ALONG_Z2 = moves(0, 0, 2, False)
ALONG_Z3 = moves(0, 0, 3, False)
ROUND_X = [moves(k, 0, 0, False) for k in (1, 2, 3)]
ROUND_Y = [moves(0, k, 0, False) for k in (1, 2, 3)]
SWAP = moves(0, 0, 0, True)


STEPS = (0, -1, 1, 2)
CHEAP = pl.CostEstimate(flops=1024, bytes_accessed=1024, transcendentals=0)


def coordinates():
    gx, gy = lax.axis_index("gx"), lax.axis_index("gy")
    return gx >> 2, gx & 3, gy >> 1, gy & 1


def send(value, pairs):
    return lax.ppermute(value, BOTH, pairs)


def slope_half(preact, upstream, other, waits=()):
    count = 4
    rows = TOK // count

    def kernel(pre_ref, up_ref, *refs):
        out, pre, up, sems = refs[len(waits) :]
        core = coordinates()[3]
        half = 1 - core if other else core
        columns = pl.ds(pl.multiple_of(half * HALF, HALF), HALF)
        for k in range(count):
            at = pl.ds(k * rows, rows)
            pltpu.make_async_copy(pre_ref.at[at, columns], pre.at[at], sems.at[0, k]).start()
            pltpu.make_async_copy(up_ref.at[at, columns], up.at[at], sems.at[1, k]).start()
        for k in range(count):
            at = pl.ds(k * rows, rows)
            pltpu.make_async_copy(pre.at[at], pre.at[at], sems.at[0, k]).wait()
            pltpu.make_async_copy(up.at[at], up.at[at], sems.at[1, k]).wait()

            @pl.loop(0, rows // 16)
            def _(j):
                tile = pl.ds(pl.multiple_of(k * rows + j * 16, 16), 16)
                value = pre[tile].astype(jnp.float32)
                normal_cdf = 0.5 * (1.0 + lax.erf(value * 0.7071067811865476))
                density = jnp.exp(-0.5 * value * value) * 0.3989422804014327
                slope = up[tile].astype(jnp.float32) * (normal_cdf + value * density)
                out[tile] = slope.astype(jnp.bfloat16)

    anywhere = pl.BlockSpec(memory_space=pl.ANY)
    half_block = pltpu.VMEM((TOK, HALF), jnp.bfloat16)
    return pl.pallas_call(
        kernel,
        out_shape=jax.ShapeDtypeStruct((TOK, HALF), jnp.bfloat16),
        in_specs=[pl.BlockSpec(memory_space=pltpu.HBM)] * 2 + [anywhere] * len(waits),
        out_specs=pl.BlockSpec(memory_space=pltpu.VMEM),
        scratch_shapes=[half_block, half_block, pltpu.SemaphoreType.DMA((2, count))],
        compiler_params=pltpu.CompilerParams(vmem_limit_bytes=24 << 20),
        cost_estimate=CHEAP,
    )(preact, upstream, *waits)


def unit_partials(slope_own, slope_other, entries, low, high, waits=()):
    arrays = []
    position = {}
    plan = []
    rows = 0
    for places in entries:
        count = places[0][0][0].shape[-2]
        for i, halves in enumerate(places):
            for h, (array, index) in enumerate(halves):
                if id(array) not in position:
                    position[id(array)] = len(arrays)
                    arrays.append(array)
                plan.append((i, h, rows, count, position[id(array)], index))
        rows += count
    many = high - low

    def kernel(own_ref, other_ref, *refs):
        feature_refs = refs[: len(arrays)]
        outs = refs[len(arrays) + len(waits) : len(arrays) + len(waits) + many]
        held, slopes, feature_sem, slope_sem = refs[len(arrays) + len(waits) + many :]
        pltpu.make_async_copy(own_ref, slopes.at[pl.ds(0, TOK)], slope_sem).start()
        pltpu.make_async_copy(other_ref, slopes.at[pl.ds(TOK, TOK)], slope_sem).start()
        y, _, z, core = coordinates()
        for i in range(4):
            place = ((1 - 2 * core) * (z - y) - STEPS[i] + 3) & 3

            @pl.when((place >= low) & (place < high))
            def _():
                base = pl.multiple_of((place - low) * rows, rows)
                for at, h, start, count, which, index in plan:
                    if at == i:
                        source = feature_refs[which]
                        source = source.at[index] if index is not None else source
                        pltpu.make_async_copy(
                            source,
                            held.at[pl.ds(base + start, count), pl.ds(h * TOK, TOK)],
                            feature_sem,
                        ).start()

        pltpu.make_async_copy(slopes, slopes, slope_sem).wait()
        pltpu.make_async_copy(held, held, feature_sem).wait()

        @pl.loop(0, HALF // 256)
        def _(j):
            columns = pl.ds(pl.multiple_of(j * 256, 256), 256)
            total = jnp.dot(held[...], slopes[:, columns], preferred_element_type=jnp.float32)
            for k, out in enumerate(outs):
                out[:, columns] = total[k * rows : (k + 1) * rows].astype(out.dtype)

    vmem = pl.BlockSpec(memory_space=pltpu.VMEM)
    anywhere = pl.BlockSpec(memory_space=pl.ANY)
    return pl.pallas_call(
        kernel,
        out_shape=tuple(
            jax.ShapeDtypeStruct((rows, HALF), jnp.float32 if k == 3 else jnp.bfloat16)
            for k in range(low, high)
        ),
        in_specs=[anywhere] * (2 + len(arrays) + len(waits)),
        out_specs=(vmem,) * many,
        scratch_shapes=[
            pltpu.VMEM((many * rows, 2 * TOK), jnp.bfloat16),
            pltpu.VMEM((2 * TOK, HALF), jnp.bfloat16),
            pltpu.SemaphoreType.DMA,
            pltpu.SemaphoreType.DMA,
        ],
        compiler_params=pltpu.CompilerParams(vmem_limit_bytes=44 << 20),
        cost_estimate=CHEAP,
    )(slope_own, slope_other, *arrays, *waits)


def add_narrow(a, b):
    return (a.astype(jnp.float32) + b.astype(jnp.float32)).astype(jnp.bfloat16)


def after(value, *before):
    return lax.optimization_barrier((value,) + before)[0]


def turn(inputs):
    def kernel(ref, first, second):
        turned = ref[...].T
        first[...] = turned[: FEAT // 2]
        second[...] = turned[FEAT // 2 :]

    vmem = pl.BlockSpec(memory_space=pltpu.VMEM)
    half = jax.ShapeDtypeStruct((FEAT // 2, TOK), jnp.bfloat16)
    return pl.pallas_call(
        kernel, out_shape=(half, half), in_specs=[vmem], out_specs=(vmem, vmem), cost_estimate=CHEAP
    )(inputs)


def stack_rows(sources, start, count):
    arrays = []
    which = []
    for array, index in sources:
        if not any(array is other for other in arrays):
            arrays.append(array)
        which.append(([array is other for other in arrays].index(True), index))

    def kernel(*refs):
        out = refs[-1]
        for k, (at, index) in enumerate(which):
            source = refs[at] if index is None else refs[at].at[index]
            out[k // 4, k % 4] = source[pl.ds(start, count)]

    vmem = pl.BlockSpec(memory_space=pltpu.VMEM)
    return pl.pallas_call(
        kernel,
        out_shape=jax.ShapeDtypeStruct((2, 4, count, TOK), jnp.bfloat16),
        in_specs=[vmem] * len(arrays),
        out_specs=vmem,
        compiler_params=pltpu.CompilerParams(vmem_limit_bytes=24 << 20),
        cost_estimate=CHEAP,
    )(*arrays)


def place_rows(last, got, pieces, before):
    rows = last.shape[0]

    def kernel(last_ref, got_ref, *refs):
        kept, sent, sums, value, sem = refs[len(before) :]
        total = last_ref[...] + got_ref[...].astype(jnp.float32)
        value[...] = total
        _, x, _, core = coordinates()
        for g, low, start, count in pieces:
            column = (x + (1 - 2 * core) * STEPS[g]) & 3
            row = pl.multiple_of((column & 1) * FEAT + low, 32)
            source = value.at[pl.ds(start, count)]

            @pl.when((column >> 1) == core)
            def _():
                pltpu.make_async_copy(source, kept.at[pl.ds(row, count)], sem).start()

            @pl.when((column >> 1) != core)
            def _():
                pltpu.make_async_copy(source, sent.at[pl.ds(row, count)], sem).start()

        squares = jnp.sum(total * total, axis=0, keepdims=True)
        sums[...] = squares + refs[2][...] if before else squares
        pltpu.make_async_copy(value, value, sem).wait()

    anywhere = pl.BlockSpec(memory_space=pl.ANY)
    vmem = pl.BlockSpec(memory_space=pltpu.VMEM)
    block = jax.ShapeDtypeStruct((HALF, HALF), jnp.float32)
    return pl.pallas_call(
        kernel,
        out_shape=(block, block, jax.ShapeDtypeStruct((1, HALF), jnp.float32)),
        in_specs=[vmem, vmem]
        + ([anywhere, anywhere, vmem] if before else []),
        out_specs=(anywhere, anywhere, vmem),
        scratch_shapes=[pltpu.VMEM((rows, HALF), jnp.float32), pltpu.SemaphoreType.DMA],
        input_output_aliases={2: 0, 3: 1} if before else {},
        compiler_params=pltpu.CompilerParams(vmem_limit_bytes=24 << 20),
        cost_estimate=CHEAP,
    )(last, got, *before)


def clip_rows(mine, yours, column_factor, kept, got):
    def kernel(mine_ref, yours_ref, column_ref, kept_ref, got_ref, payload, clips, news):
        core = coordinates()[3]
        total = weights = None
        squares = None
        both = []
        for stats, grad in ((mine_ref, kept_ref), (yours_ref, got_ref)):
            grad_sq, weight_sq = stats[:, :HALF], stats[:, HALF : 2 * HALF]
            clip = jnp.minimum(
                1.0, clip_ratio * jnp.sqrt(weight_sq) / (jnp.sqrt(grad_sq) + unit_eps)
            )
            column = clip * clip * grad_sq
            both.append((clip, column))
            clipped = grad[...] * clip
            squares = clipped * clipped if squares is None else squares + clipped * clipped
            column_total = jnp.sum(column, axis=1, keepdims=True)
            weight_total = jnp.sum(weight_sq, axis=1, keepdims=True)
            total = column_total if total is None else total + column_total
            weights = weight_total if weights is None else weights + weight_total
        for at in range(2):
            columns = pl.ds(at * HALF, HALF)
            here = core == at
            clips[:, columns] = jnp.where(here, both[0][0], both[1][0])
            sums = jnp.where(here, both[0][1], both[1][1])
            news[:, columns] = second_decay * column_ref[:, columns] + (1.0 - second_decay) * (
                sums / D + factor_eps
            )
        row_sums = lax.dot_general(
            jnp.ones((8, HALF), jnp.float32),
            squares,
            (((1,), (1,)), ((), ())),
            precision=lax.Precision.HIGHEST,
            preferred_element_type=jnp.float32,
        )
        payload[:, :HALF] = row_sums[:1]
        payload[:, HALF : HALF + 128] = jnp.broadcast_to(total, (1, 128))
        payload[:, HALF + 128 :] = jnp.broadcast_to(weights, (1, 128))

    vmem = pl.BlockSpec(memory_space=pltpu.VMEM)
    columns = jax.ShapeDtypeStruct((1, 2 * HALF), jnp.float32)
    return pl.pallas_call(
        kernel,
        out_shape=(jax.ShapeDtypeStruct((1, HALF + 256), jnp.float32), columns, columns),
        in_specs=[vmem] * 5,
        out_specs=(vmem,) * 3,
        compiler_params=pltpu.CompilerParams(vmem_limit_bytes=32 << 20),
        cost_estimate=CHEAP,
    )(mine, yours, column_factor, kept, got)


def finish(summed, row_total, clips, new_column, row_factor, kept, got):
    step = 128

    def kernel(
        summed_ref, row_total_ref, clip_ref, column_ref, row_ref, kept_ref, got_ref,
        update, new_row_ref,
    ):
        core = coordinates()[3]
        at = pl.ds(pl.multiple_of(pl.program_id(0) * step, step), step)
        clipped_total = summed_ref[:, HALF : HALF + 1]
        weight_total = summed_ref[:, HALF + 128 : HALF + 129]
        row_mean = (
            second_decay * row_total_ref[:, :1]
            + (1.0 - second_decay) * (clipped_total / FF + D * factor_eps)
        ) / D
        weight_rms = jnp.sqrt(weight_total / (D * FF))
        row_sums = summed_ref[:, at]
        new_row = second_decay * row_ref[:, at] + (1.0 - second_decay) * (
            row_sums / FF + factor_eps
        )
        new_row_ref[:, at] = new_row
        down = jnp.broadcast_to(lax.rsqrt(new_row), (step, step)).T[:, :1]
        across = -weight_rms * clip_ref[...] * (jnp.sqrt(row_mean) * lax.rsqrt(column_ref[...]))
        first = jnp.where(core == 0, kept_ref[...], got_ref[...])
        second = jnp.where(core == 0, got_ref[...], kept_ref[...])
        update[:, :HALF] = first * across[:, :HALF] * down
        update[:, HALF:] = second * across[:, HALF:] * down

    whole = lambda *shape: pl.BlockSpec(shape, lambda i: (0, 0))
    rows = lambda width: pl.BlockSpec((step, width), lambda i: (i, 0))
    return pl.pallas_call(
        kernel,
        grid=(HALF // step,),
        out_shape=(
            jax.ShapeDtypeStruct((HALF, 2 * HALF), jnp.float32),
            jax.ShapeDtypeStruct((1, HALF), jnp.float32),
        ),
        in_specs=[
            whole(1, HALF + 256), whole(1, 128), whole(1, 2 * HALF), whole(1, 2 * HALF),
            whole(1, HALF), rows(HALF), rows(HALF),
        ],
        out_specs=(rows(2 * HALF), whole(1, HALF)),
        compiler_params=pltpu.CompilerParams(vmem_limit_bytes=32 << 20),
        cost_estimate=CHEAP,
    )(summed, row_total, clips, new_column, row_factor, kept, got)


def per_device(inputs, preact, upstream, weight, row_factor, column_factor):
    core = coordinates()[3]

    p, q = turn(inputs)
    size = FEAT // 2 // NCH

    p_swap, q_swap = send(p, SWAP), send(q, SWAP)
    ya, xa = send(p, ALONG_Y), send(q, ALONG_X)
    yb, xb = send(p_swap, ALONG_Y), send(q_swap, ALONG_X)
    slope_yours = slope_half(preact, upstream, True, (p_swap, q_swap))
    slope_other = send(slope_yours, SWAP)
    slope_mine = slope_half(preact, upstream, False, (p_swap, q_swap))
    ya, xa, yb, xb = lax.optimization_barrier((ya, xa, yb, xb, slope_yours, slope_mine))[:4]
    y2, x2 = send(ya, ALONG_Y), send(xa, ALONG_X)
    ya_swap, xa_swap = send(ya, SWAP), send(xa, SWAP)
    yb, xb = lax.optimization_barrier((yb, xb, ya_swap, xa_swap))[:2]
    yb_swap, xb_swap = send(yb, SWAP), send(xb, SWAP)
    y2, x2 = lax.optimization_barrier((y2, x2, yb_swap, xb_swap))[:2]
    y2_swap, x2_swap = send(y2, SWAP), send(x2, SWAP)
    p_places = [(p, None), (ya, None), (yb_swap, None), (y2, None)]
    p_places += [(p_swap, None), (yb, None), (ya_swap, None), (y2_swap, None)]
    q_places = [(q, None), (xa, None), (xb_swap, None), (x2, None)]
    q_places += [(q_swap, None), (xb, None), (xa_swap, None), (x2_swap, None)]

    def units(entries, low=0, high=4, waits=()):
        return unit_partials(slope_mine, slope_other, entries, low, high, waits)

    def hop(value):
        return send(value, ALONG_Z)

    def near_entries(x1, x1_swap):
        return [
            [((x1, (0, i)), (x1, (1, i))) for i in range(4)],
            [((x1_swap, (1, FLIP[i])), (x1_swap, (0, FLIP[i]))) for i in range(4)],
        ]

    def far_entries(q_here, y1, y1_swap, x2, x2_swap, y2, y2_swap):
        entries = [[((x2, i), (x2_swap, FLIP[i])) for i in range(4)]]
        for g in range(4):
            entries.append(
                [
                    ((q_here, (0, g)), (q_here, (1, g))),
                    ((y1, (0, g)), (y1, (1, g))),
                    ((y1_swap, (1, FLIP[g])), (y1_swap, (0, FLIP[g]))),
                    ((y2, g), (y2_swap, FLIP[g])),
                ]
            )
        return entries

    p_here = stack_rows(p_places, 0, size)
    q_here = stack_rows(q_places, 0, size)
    x1, y1 = send(p_here, ALONG_X), send(q_here, ALONG_Y)
    own = units([[(p_places[i], p_places[4 + i]) for i in range(4)]], waits=(p_here, q_here))
    own_got = hop(own[0])
    weight = after(weight, own[0])
    weight_local = jnp.sum(weight * weight, axis=0)
    row_local = jnp.broadcast_to(jnp.sum(row_factor)[None], (128,))
    weight_mine = lax.dynamic_slice_in_dim(weight_local, core * HALF, HALF)
    weight_yours = lax.dynamic_slice_in_dim(weight_local, (1 - core) * HALF, HALF)
    early = jnp.concatenate([weight_mine, row_local])
    early = early + send(jnp.concatenate([weight_yours, row_local]), SWAP)
    p_next = stack_rows(p_places, size, size)
    q_next = stack_rows(q_places, size, size)
    own_2 = add_narrow(own[1], own_got)
    own_got = hop(own_2)
    own_3 = add_narrow(own[2], own_got)
    x1, y1 = lax.optimization_barrier((x1, y1, own_3, p_next, q_next, early))[:2]
    x2, y2 = send(x1[0], ALONG_X), send(y1[0], ALONG_Y)
    x1_swap, y1_swap = send(x1, SWAP), send(y1, SWAP)

    p_next, q_next = lax.optimization_barrier((p_next, q_next, x1_swap, y1_swap))[:2]
    x1_next, y1_next = send(p_next, ALONG_X), send(q_next, ALONG_Y)
    near0 = units(near_entries(x1, x1_swap), waits=(y1_swap,))
    near0_got = hop(near0[0])
    x2, y2 = lax.optimization_barrier((x2, y2, near0[0]))[:2]
    x2_swap, y2_swap = send(x2, SWAP), send(y2, SWAP)
    far0_entries = far_entries(q_here, y1, y1_swap, x2, x2_swap, y2, y2_swap)
    near0_2 = add_narrow(near0[1], near0_got)
    near0_got = hop(near0_2)
    far0 = units(far0_entries, 0, 2, waits=(near0_2,))
    far0_got = hop(far0[0])
    near0_3 = add_narrow(near0[2], after(near0_got, far0[0]))
    x1, y1 = lax.optimization_barrier((x1_next, y1_next, far0[0], near0_3))[:2]
    far0_2 = add_narrow(far0[1], far0_got)
    x2, y2 = lax.optimization_barrier((x1[0], y1[0], far0_2))[:2]
    x2, y2 = send(x2, ALONG_X), send(y2, ALONG_Y)
    far0_got = hop(far0_2)
    x1_swap, y1_swap = send(x1, SWAP), send(y1, SWAP)
    near0_got = hop(after(near0_3, x1_swap, y1_swap))
    own_got = hop(after(own_3, x1_swap, y1_swap))
    far0 += units(far0_entries, 2, 4)
    near_pieces = lambda chunk: [(1, chunk * size, 0, size), (2, chunk * size, size, size)]
    far_pieces = lambda chunk: [(3, chunk * size, 0, size)] + [
        (g, FEAT // 2 + chunk * size, (g + 1) * size, size) for g in range(4)
    ]
    near1 = units(near_entries(x1, x1_swap), waits=(far0[2], y1_swap))
    near1_got = hop(near1[0])
    placed = place_rows(own[3], after(own_got, near1[0]), [(0, 0, 0, FEAT // 2)], ())
    placed = place_rows(near0[3], after(near0_got, near1[0]), near_pieces(0), placed)
    x2, y2 = lax.optimization_barrier((x2, y2, near1[0], placed[2]))[:2]
    x2_swap, y2_swap = send(x2, SWAP), send(y2, SWAP)
    far1_entries = far_entries(q_next, y1, y1_swap, x2, x2_swap, y2, y2_swap)
    far0_3 = add_narrow(far0[2], after(far0_got, near1[0]))
    far0_got = hop(far0_3)
    near1_2 = add_narrow(near1[1], near1_got)
    near1_got = hop(near1_2)
    far1 = units(far1_entries[:2], waits=(far0_3, near1_2))
    far1_got = hop(far1[0])
    last1 = units(far1_entries[2:], waits=(far1[0],))
    last1_got = hop(last1[0])
    near1_3 = add_narrow(near1[2], after(near1_got, last1[0]))
    near1_got = hop(near1_3)
    placed = place_rows(far0[3], after(far0_got, near1_3), far_pieces(0), placed)
    far1_2 = add_narrow(far1[1], after(far1_got, near1_3))
    last1_2 = add_narrow(last1[1], after(last1_got, placed[2], far1_2))
    last1_got = hop(last1_2)
    far1_got = hop(far1_2)
    placed = place_rows(near1[3], after(near1_got, last1_2), near_pieces(1), placed)
    far1_got = hop(after(add_narrow(far1[2], far1_got), placed[2]))
    last1_got = hop(add_narrow(last1[2], last1_got))
    placed = place_rows(far1[3], far1_got, far_pieces(1)[:2], placed)
    last_pieces = [(g, low, start - 2 * size, count) for g, low, start, count in far_pieces(1)[2:]]
    placed = place_rows(last1[3], last1_got, last_pieces, placed)
    kept, sent, grad_local = placed
    got = send(sent, SWAP)
    local = jnp.concatenate([grad_local, early[None, :]], axis=1)
    column_stats = local
    for pairs in (ALONG_Z, ALONG_Z2, ALONG_Z3):
        column_stats = column_stats + send(local, pairs)
    yours_stats = send(column_stats, SWAP)
    summed, clips, new_column = clip_rows(
        column_stats, yours_stats, column_factor[None, :], kept, got
    )
    for along in (ROUND_X, ROUND_Y):
        summed = sum((send(summed, pairs) for pairs in along), summed)
    update, new_row = finish(
        summed, column_stats[:, 2 * HALF :], clips, new_column, row_factor[None, :], kept, got
    )
    return (update, new_row[0], new_column[0])


def solution(mesh):
    in_specs = (P("gy", "gx"), P("gy", "gx"), P("gy", "gx"), P("gy", "gx"), P("gy"), P("gx"))
    out_specs = (P("gy", "gx"), P("gy"), P("gx"))
    return jax.shard_map(
        per_device, mesh=mesh, in_specs=in_specs, out_specs=out_specs, check_vma=False
    )
```

```python
import jax
import jax.numpy as jnp
from jax import lax
from jax.experimental import pallas as pl
from jax.experimental.pallas import tpu as pltpu
from jax.sharding import PartitionSpec as P

D = 6144
FF = 24576
TOK = 1024
FEAT = 384
HALF = 768
NCH = 2

second_decay = 0.8
clip_ratio = 1.0
unit_eps = 1e-06
factor_eps = 1e-30

BOTH = ("gx", "gy")
FLIP = (0, 2, 1, 3)


def moves(dx, dy, dz, other_core):
    pairs = []
    for y in range(4):
        for x in range(4):
            for z in range(4):
                for core in range(2):
                    s = 1 - 2 * core
                    tx, ty, tz = (x + s * dx) % 4, (y + s * dy) % 4, (z + s * dz) % 4
                    tc = 1 - core if other_core else core
                    pairs.append(((y * 4 + x) * 8 + z * 2 + core, (ty * 4 + tx) * 8 + tz * 2 + tc))
    return pairs


ALONG_X = moves(1, 0, 0, False)
ALONG_Y = moves(0, 1, 0, False)
ALONG_Z = moves(0, 0, 1, False)
ALONG_Z2 = moves(0, 0, 2, False)
ALONG_Z3 = moves(0, 0, 3, False)
ROUND_X = [moves(k, 0, 0, False) for k in (1, 2, 3)]
ROUND_Y = [moves(0, k, 0, False) for k in (1, 2, 3)]
SWAP = moves(0, 0, 0, True)


STEPS = (0, -1, 1, 2)
CHEAP = pl.CostEstimate(flops=1024, bytes_accessed=1024, transcendentals=0)


def coordinates():
    gx, gy = lax.axis_index("gx"), lax.axis_index("gy")
    return gx >> 2, gx & 3, gy >> 1, gy & 1


def send(value, pairs):
    return lax.ppermute(value, BOTH, pairs)


def slope_half(preact, upstream, other, waits=()):
    count = 4
    rows = TOK // count

    def kernel(pre_ref, up_ref, *refs):
        out, pre, up, sems = refs[len(waits) :]
        core = coordinates()[3]
        half = 1 - core if other else core
        columns = pl.ds(pl.multiple_of(half * HALF, HALF), HALF)
        for k in range(count):
            at = pl.ds(k * rows, rows)
            pltpu.make_async_copy(pre_ref.at[at, columns], pre.at[at], sems.at[0, k]).start()
            pltpu.make_async_copy(up_ref.at[at, columns], up.at[at], sems.at[1, k]).start()
        for k in range(count):
            at = pl.ds(k * rows, rows)
            pltpu.make_async_copy(pre.at[at], pre.at[at], sems.at[0, k]).wait()
            pltpu.make_async_copy(up.at[at], up.at[at], sems.at[1, k]).wait()

            @pl.loop(0, rows // 16)
            def _(j):
                tile = pl.ds(pl.multiple_of(k * rows + j * 16, 16), 16)
                value = pre[tile].astype(jnp.float32)
                normal_cdf = 0.5 * (1.0 + lax.erf(value * 0.7071067811865476))
                density = jnp.exp(-0.5 * value * value) * 0.3989422804014327
                slope = up[tile].astype(jnp.float32) * (normal_cdf + value * density)
                out[tile] = slope.astype(jnp.bfloat16)

    anywhere = pl.BlockSpec(memory_space=pl.ANY)
    half_block = pltpu.VMEM((TOK, HALF), jnp.bfloat16)
    return pl.pallas_call(
        kernel,
        out_shape=jax.ShapeDtypeStruct((TOK, HALF), jnp.bfloat16),
        in_specs=[pl.BlockSpec(memory_space=pltpu.HBM)] * 2 + [anywhere] * len(waits),
        out_specs=pl.BlockSpec(memory_space=pltpu.VMEM),
        scratch_shapes=[half_block, half_block, pltpu.SemaphoreType.DMA((2, count))],
        compiler_params=pltpu.CompilerParams(vmem_limit_bytes=24 << 20),
        cost_estimate=CHEAP,
    )(preact, upstream, *waits)


def unit_partials(slope_own, slope_other, entries, low, high, waits=()):
    arrays = []
    position = {}
    plan = []
    rows = 0
    for places in entries:
        count = places[0][0][0].shape[-2]
        for i, halves in enumerate(places):
            for h, (array, index) in enumerate(halves):
                if id(array) not in position:
                    position[id(array)] = len(arrays)
                    arrays.append(array)
                plan.append((i, h, rows, count, position[id(array)], index))
        rows += count
    many = high - low

    def kernel(own_ref, other_ref, *refs):
        feature_refs = refs[: len(arrays)]
        outs = refs[len(arrays) + len(waits) : len(arrays) + len(waits) + many]
        held, slopes, feature_sem, slope_sem = refs[len(arrays) + len(waits) + many :]
        pltpu.make_async_copy(own_ref, slopes.at[pl.ds(0, TOK)], slope_sem).start()
        pltpu.make_async_copy(other_ref, slopes.at[pl.ds(TOK, TOK)], slope_sem).start()
        y, _, z, core = coordinates()
        for i in range(4):
            place = ((1 - 2 * core) * (z - y) - STEPS[i] + 3) & 3

            @pl.when((place >= low) & (place < high))
            def _():
                base = pl.multiple_of((place - low) * rows, rows)
                for at, h, start, count, which, index in plan:
                    if at == i:
                        source = feature_refs[which]
                        source = source.at[index] if index is not None else source
                        pltpu.make_async_copy(
                            source,
                            held.at[pl.ds(base + start, count), pl.ds(h * TOK, TOK)],
                            feature_sem,
                        ).start()

        pltpu.make_async_copy(slopes, slopes, slope_sem).wait()
        pltpu.make_async_copy(held, held, feature_sem).wait()

        @pl.loop(0, HALF // 256)
        def _(j):
            columns = pl.ds(pl.multiple_of(j * 256, 256), 256)
            total = jnp.dot(held[...], slopes[:, columns], preferred_element_type=jnp.float32)
            for k, out in enumerate(outs):
                out[:, columns] = total[k * rows : (k + 1) * rows].astype(out.dtype)

    vmem = pl.BlockSpec(memory_space=pltpu.VMEM)
    anywhere = pl.BlockSpec(memory_space=pl.ANY)
    return pl.pallas_call(
        kernel,
        out_shape=tuple(
            jax.ShapeDtypeStruct((rows, HALF), jnp.float32 if k == 3 else jnp.bfloat16)
            for k in range(low, high)
        ),
        in_specs=[anywhere] * (2 + len(arrays) + len(waits)),
        out_specs=(vmem,) * many,
        scratch_shapes=[
            pltpu.VMEM((many * rows, 2 * TOK), jnp.bfloat16),
            pltpu.VMEM((2 * TOK, HALF), jnp.bfloat16),
            pltpu.SemaphoreType.DMA,
            pltpu.SemaphoreType.DMA,
        ],
        compiler_params=pltpu.CompilerParams(vmem_limit_bytes=44 << 20),
        cost_estimate=CHEAP,
    )(slope_own, slope_other, *arrays, *waits)


def add_narrow(a, b):
    return (a.astype(jnp.float32) + b.astype(jnp.float32)).astype(jnp.bfloat16)


def after(value, *before):
    return lax.optimization_barrier((value,) + before)[0]


def turn(inputs):
    def kernel(ref, first, second):
        turned = ref[...].T
        first[...] = turned[: FEAT // 2]
        second[...] = turned[FEAT // 2 :]

    vmem = pl.BlockSpec(memory_space=pltpu.VMEM)
    half = jax.ShapeDtypeStruct((FEAT // 2, TOK), jnp.bfloat16)
    return pl.pallas_call(
        kernel, out_shape=(half, half), in_specs=[vmem], out_specs=(vmem, vmem), cost_estimate=CHEAP
    )(inputs)


def stack_rows(sources, start, count):
    arrays = []
    which = []
    for array, index in sources:
        if not any(array is other for other in arrays):
            arrays.append(array)
        which.append(([array is other for other in arrays].index(True), index))

    def kernel(*refs):
        out = refs[-1]
        for k, (at, index) in enumerate(which):
            source = refs[at] if index is None else refs[at].at[index]
            out[k // 4, k % 4] = source[pl.ds(start, count)]

    vmem = pl.BlockSpec(memory_space=pltpu.VMEM)
    return pl.pallas_call(
        kernel,
        out_shape=jax.ShapeDtypeStruct((2, 4, count, TOK), jnp.bfloat16),
        in_specs=[vmem] * len(arrays),
        out_specs=vmem,
        compiler_params=pltpu.CompilerParams(vmem_limit_bytes=24 << 20),
        cost_estimate=CHEAP,
    )(*arrays)


def place_rows(last, got, pieces, before):
    rows = last.shape[0]

    def kernel(last_ref, got_ref, *refs):
        kept, sent, sums, value, sem = refs[len(before) :]
        total = last_ref[...] + got_ref[...].astype(jnp.float32)
        value[...] = total
        _, x, _, core = coordinates()
        for g, low, start, count in pieces:
            column = (x + (1 - 2 * core) * STEPS[g]) & 3
            row = pl.multiple_of((column & 1) * FEAT + low, 32)
            source = value.at[pl.ds(start, count)]

            @pl.when((column >> 1) == core)
            def _():
                pltpu.make_async_copy(source, kept.at[pl.ds(row, count)], sem).start()

            @pl.when((column >> 1) != core)
            def _():
                pltpu.make_async_copy(source, sent.at[pl.ds(row, count)], sem).start()

        squares = jnp.sum(total * total, axis=0, keepdims=True)
        sums[...] = squares + refs[2][...] if before else squares
        pltpu.make_async_copy(value, value, sem).wait()

    anywhere = pl.BlockSpec(memory_space=pl.ANY)
    vmem = pl.BlockSpec(memory_space=pltpu.VMEM)
    block = jax.ShapeDtypeStruct((HALF, HALF), jnp.float32)
    return pl.pallas_call(
        kernel,
        out_shape=(block, block, jax.ShapeDtypeStruct((1, HALF), jnp.float32)),
        in_specs=[vmem, vmem]
        + ([anywhere, anywhere, vmem] if before else []),
        out_specs=(anywhere, anywhere, vmem),
        scratch_shapes=[pltpu.VMEM((rows, HALF), jnp.float32), pltpu.SemaphoreType.DMA],
        input_output_aliases={2: 0, 3: 1} if before else {},
        compiler_params=pltpu.CompilerParams(vmem_limit_bytes=24 << 20),
        cost_estimate=CHEAP,
    )(last, got, *before)


def clip_rows(mine, yours, column_factor, kept, got):
    def kernel(mine_ref, yours_ref, column_ref, kept_ref, got_ref, payload, clips, news):
        core = coordinates()[3]
        total = weights = None
        squares = None
        both = []
        for stats, grad in ((mine_ref, kept_ref), (yours_ref, got_ref)):
            grad_sq, weight_sq = stats[:, :HALF], stats[:, HALF : 2 * HALF]
            clip = jnp.minimum(
                1.0, clip_ratio * jnp.sqrt(weight_sq) / (jnp.sqrt(grad_sq) + unit_eps)
            )
            column = clip * clip * grad_sq
            both.append((clip, column))
            clipped = grad[...] * clip
            squares = clipped * clipped if squares is None else squares + clipped * clipped
            column_total = jnp.sum(column, axis=1, keepdims=True)
            weight_total = jnp.sum(weight_sq, axis=1, keepdims=True)
            total = column_total if total is None else total + column_total
            weights = weight_total if weights is None else weights + weight_total
        for at in range(2):
            columns = pl.ds(at * HALF, HALF)
            here = core == at
            clips[:, columns] = jnp.where(here, both[0][0], both[1][0])
            sums = jnp.where(here, both[0][1], both[1][1])
            news[:, columns] = second_decay * column_ref[:, columns] + (1.0 - second_decay) * (
                sums / D + factor_eps
            )
        row_sums = lax.dot_general(
            jnp.ones((8, HALF), jnp.float32),
            squares,
            (((1,), (1,)), ((), ())),
            precision=lax.Precision.HIGHEST,
            preferred_element_type=jnp.float32,
        )
        payload[:, :HALF] = row_sums[:1]
        payload[:, HALF : HALF + 128] = jnp.broadcast_to(total, (1, 128))
        payload[:, HALF + 128 :] = jnp.broadcast_to(weights, (1, 128))

    vmem = pl.BlockSpec(memory_space=pltpu.VMEM)
    columns = jax.ShapeDtypeStruct((1, 2 * HALF), jnp.float32)
    return pl.pallas_call(
        kernel,
        out_shape=(jax.ShapeDtypeStruct((1, HALF + 256), jnp.float32), columns, columns),
        in_specs=[vmem] * 5,
        out_specs=(vmem,) * 3,
        compiler_params=pltpu.CompilerParams(vmem_limit_bytes=32 << 20),
        cost_estimate=CHEAP,
    )(mine, yours, column_factor, kept, got)


def finish(summed, row_total, clips, new_column, row_factor, kept, got):
    step = 128

    def kernel(
        summed_ref, row_total_ref, clip_ref, column_ref, row_ref, kept_ref, got_ref,
        update, new_row_ref,
    ):
        core = coordinates()[3]
        at = pl.ds(pl.multiple_of(pl.program_id(0) * step, step), step)
        clipped_total = summed_ref[:, HALF : HALF + 1]
        weight_total = summed_ref[:, HALF + 128 : HALF + 129]
        row_mean = (
            second_decay * row_total_ref[:, :1]
            + (1.0 - second_decay) * (clipped_total / FF + D * factor_eps)
        ) / D
        weight_rms = jnp.sqrt(weight_total / (D * FF))
        row_sums = summed_ref[:, at]
        new_row = second_decay * row_ref[:, at] + (1.0 - second_decay) * (
            row_sums / FF + factor_eps
        )
        new_row_ref[:, at] = new_row
        down = jnp.broadcast_to(lax.rsqrt(new_row), (step, step)).T[:, :1]
        across = -weight_rms * clip_ref[...] * (jnp.sqrt(row_mean) * lax.rsqrt(column_ref[...]))
        first = jnp.where(core == 0, kept_ref[...], got_ref[...])
        second = jnp.where(core == 0, got_ref[...], kept_ref[...])
        update[:, :HALF] = first * across[:, :HALF] * down
        update[:, HALF:] = second * across[:, HALF:] * down

    whole = lambda *shape: pl.BlockSpec(shape, lambda i: (0, 0))
    rows = lambda width: pl.BlockSpec((step, width), lambda i: (i, 0))
    return pl.pallas_call(
        kernel,
        grid=(HALF // step,),
        out_shape=(
            jax.ShapeDtypeStruct((HALF, 2 * HALF), jnp.float32),
            jax.ShapeDtypeStruct((1, HALF), jnp.float32),
        ),
        in_specs=[
            whole(1, HALF + 256), whole(1, 128), whole(1, 2 * HALF), whole(1, 2 * HALF),
            whole(1, HALF), rows(HALF), rows(HALF),
        ],
        out_specs=(rows(2 * HALF), whole(1, HALF)),
        compiler_params=pltpu.CompilerParams(vmem_limit_bytes=32 << 20),
        cost_estimate=CHEAP,
    )(summed, row_total, clips, new_column, row_factor, kept, got)


def per_device(inputs, preact, upstream, weight, row_factor, column_factor):
    core = coordinates()[3]

    p, q = turn(inputs)
    size = FEAT // 2 // NCH

    p_swap, q_swap = send(p, SWAP), send(q, SWAP)
    ya, xa = send(p, ALONG_Y), send(q, ALONG_X)
    yb, xb = send(p_swap, ALONG_Y), send(q_swap, ALONG_X)
    slope_yours = slope_half(preact, upstream, True, (p_swap, q_swap))
    slope_other = send(slope_yours, SWAP)
    slope_mine = slope_half(preact, upstream, False, (p_swap, q_swap))
    ya, xa, yb, xb = lax.optimization_barrier((ya, xa, yb, xb, slope_yours, slope_mine))[:4]
    y2, x2 = send(ya, ALONG_Y), send(xa, ALONG_X)
    ya_swap, xa_swap = send(ya, SWAP), send(xa, SWAP)
    yb, xb = lax.optimization_barrier((yb, xb, ya_swap, xa_swap))[:2]
    yb_swap, xb_swap = send(yb, SWAP), send(xb, SWAP)
    y2, x2 = lax.optimization_barrier((y2, x2, yb_swap, xb_swap))[:2]
    y2_swap, x2_swap = send(y2, SWAP), send(x2, SWAP)
    p_places = [(p, None), (ya, None), (yb_swap, None), (y2, None)]
    p_places += [(p_swap, None), (yb, None), (ya_swap, None), (y2_swap, None)]
    q_places = [(q, None), (xa, None), (xb_swap, None), (x2, None)]
    q_places += [(q_swap, None), (xb, None), (xa_swap, None), (x2_swap, None)]

    def units(entries, low=0, high=4, waits=()):
        return unit_partials(slope_mine, slope_other, entries, low, high, waits)

    def hop(value):
        return send(value, ALONG_Z)

    def near_entries(x1, x1_swap):
        return [
            [((x1, (0, i)), (x1, (1, i))) for i in range(4)],
            [((x1_swap, (1, FLIP[i])), (x1_swap, (0, FLIP[i]))) for i in range(4)],
        ]

    def far_entries(q_here, y1, y1_swap, x2, x2_swap, y2, y2_swap):
        entries = [[((x2, i), (x2_swap, FLIP[i])) for i in range(4)]]
        for g in range(4):
            entries.append(
                [
                    ((q_here, (0, g)), (q_here, (1, g))),
                    ((y1, (0, g)), (y1, (1, g))),
                    ((y1_swap, (1, FLIP[g])), (y1_swap, (0, FLIP[g]))),
                    ((y2, g), (y2_swap, FLIP[g])),
                ]
            )
        return entries

    p_here = stack_rows(p_places, 0, size)
    q_here = stack_rows(q_places, 0, size)
    x1, y1 = send(p_here, ALONG_X), send(q_here, ALONG_Y)
    own = units([[(p_places[i], p_places[4 + i]) for i in range(4)]], waits=(p_here, q_here))
    own_got = hop(own[0])
    weight = after(weight, own[0])
    weight_local = jnp.sum(weight * weight, axis=0)
    row_local = jnp.broadcast_to(jnp.sum(row_factor)[None], (128,))
    weight_mine = lax.dynamic_slice_in_dim(weight_local, core * HALF, HALF)
    weight_yours = lax.dynamic_slice_in_dim(weight_local, (1 - core) * HALF, HALF)
    early = jnp.concatenate([weight_mine, row_local])
    early = early + send(jnp.concatenate([weight_yours, row_local]), SWAP)
    p_next = stack_rows(p_places, size, size)
    q_next = stack_rows(q_places, size, size)
    own_2 = add_narrow(own[1], own_got)
    own_got = hop(own_2)
    own_3 = add_narrow(own[2], own_got)
    x1, y1 = lax.optimization_barrier((x1, y1, own_2, p_next, q_next, early))[:2]
    x2, y2 = send(x1[0], ALONG_X), send(y1[0], ALONG_Y)
    x1_swap, y1_swap = send(x1, SWAP), send(y1, SWAP)

    p_next, q_next = lax.optimization_barrier((p_next, q_next, x1_swap, y1_swap))[:2]
    x1_next, y1_next = send(p_next, ALONG_X), send(q_next, ALONG_Y)
    near0 = units(near_entries(x1, x1_swap), waits=(y1_swap, own_3))
    near0_got = hop(near0[0])
    x2, y2 = lax.optimization_barrier((x2, y2, near0[0]))[:2]
    x2_swap, y2_swap = send(x2, SWAP), send(y2, SWAP)
    far0_entries = far_entries(q_here, y1, y1_swap, x2, x2_swap, y2, y2_swap)
    near0_2 = add_narrow(near0[1], near0_got)
    near0_got = hop(near0_2)
    far0 = units(far0_entries, 0, 2, waits=(near0_2,))
    far0_got = hop(far0[0])
    near0_3 = add_narrow(near0[2], after(near0_got, far0[0]))
    x1, y1 = lax.optimization_barrier((x1_next, y1_next, far0[0], near0_3))[:2]
    far0_2 = add_narrow(far0[1], far0_got)
    x2, y2 = lax.optimization_barrier((x1[0], y1[0], far0_2))[:2]
    x2, y2 = send(x2, ALONG_X), send(y2, ALONG_Y)
    far0_got = hop(far0_2)
    x1_swap, y1_swap = send(x1, SWAP), send(y1, SWAP)
    near0_got = hop(after(near0_3, x1_swap, y1_swap))
    own_got = hop(after(own_3, x1_swap, y1_swap))
    far0 += units(far0_entries, 2, 4)
    near_pieces = lambda chunk: [(1, chunk * size, 0, size), (2, chunk * size, size, size)]
    far_pieces = lambda chunk: [(3, chunk * size, 0, size)] + [
        (g, FEAT // 2 + chunk * size, (g + 1) * size, size) for g in range(4)
    ]
    near1 = units(near_entries(x1, x1_swap), waits=(far0[2], y1_swap))
    near1_got = hop(near1[0])
    placed = place_rows(own[3], after(own_got, near1[0]), [(0, 0, 0, FEAT // 2)], ())
    placed = place_rows(near0[3], after(near0_got, near1[0]), near_pieces(0), placed)
    x2, y2 = lax.optimization_barrier((x2, y2, near1[0], placed[2]))[:2]
    x2_swap, y2_swap = send(x2, SWAP), send(y2, SWAP)
    far1_entries = far_entries(q_next, y1, y1_swap, x2, x2_swap, y2, y2_swap)
    far0_3 = add_narrow(far0[2], after(far0_got, near1[0]))
    far0_got = hop(far0_3)
    near1_2 = add_narrow(near1[1], near1_got)
    near1_got = hop(near1_2)
    far1 = units(far1_entries[:2], waits=(far0_3, near1_2))
    far1_got = hop(far1[0])
    last1 = units(far1_entries[2:], waits=(far1[0],))
    last1_got = hop(last1[0])
    near1_3 = add_narrow(near1[2], after(near1_got, last1[0]))
    near1_got = hop(near1_3)
    placed = place_rows(far0[3], after(far0_got, near1_3), far_pieces(0), placed)
    far1_2 = add_narrow(far1[1], after(far1_got, near1_3))
    last1_2 = add_narrow(last1[1], after(last1_got, placed[2], far1_2))
    last1_got = hop(last1_2)
    far1_got = hop(far1_2)
    placed = place_rows(near1[3], after(near1_got, last1_2), near_pieces(1), placed)
    far1_got = hop(after(add_narrow(far1[2], far1_got), placed[2]))
    last1_got = hop(add_narrow(last1[2], last1_got))
    placed = place_rows(far1[3], far1_got, far_pieces(1)[:2], placed)
    last_pieces = [(g, low, start - 2 * size, count) for g, low, start, count in far_pieces(1)[2:]]
    placed = place_rows(last1[3], last1_got, last_pieces, placed)
    kept, sent, grad_local = placed
    got = send(sent, SWAP)
    local = jnp.concatenate([grad_local, early[None, :]], axis=1)
    column_stats = local
    for pairs in (ALONG_Z, ALONG_Z2, ALONG_Z3):
        column_stats = column_stats + send(local, pairs)
    yours_stats = send(column_stats, SWAP)
    summed, clips, new_column = clip_rows(
        column_stats, yours_stats, column_factor[None, :], kept, got
    )
    for along in (ROUND_X, ROUND_Y):
        summed = sum((send(summed, pairs) for pairs in along), summed)
    update, new_row = finish(
        summed, column_stats[:, 2 * HALF :], clips, new_column, row_factor[None, :], kept, got
    )
    return (update, new_row[0], new_column[0])


def solution(mesh):
    in_specs = (P("gy", "gx"), P("gy", "gx"), P("gy", "gx"), P("gy", "gx"), P("gy"), P("gx"))
    out_specs = (P("gy", "gx"), P("gy"), P("gx"))
    return jax.shard_map(
        per_device, mesh=mesh, in_specs=in_specs, out_specs=out_specs, check_vma=False
    )
```
